32 devices in a mesh: gx: 8 (over z, x), gy: 4 (over y, core).
Axes of the slice: x: 2, y: 2, z: 4, core: 2. Of those that a mesh axis runs over, the one named last changes fastest.
Arguments:
- velocity: float32 [3, 128, 64, 128], P(None, 'gx', 'gy'), may hold values from -6 to 6
- velocity_old: float32 [3, 128, 64, 128], P(None, 'gx', 'gy'), may hold values from -6 to 6
- station_cell: int32 [131072], P(('gx', 'gy')), may hold values from 0 to 32767
- station_member: int32 [131072, 1], P(('gx', 'gy')), may hold values from 0 to 511, as said below
- drag_coef: float32 [131072], P(('gx', 'gy')), may hold values from 0.1 to 1
- inertia_coef: float32 [131072], P(('gx', 'gy')), may hold values from 0.3 to 3
- member_velocity: float32 [3, 512], P(None, ('gx', 'gy')), may hold values from -6 to 6
- member_inv_mass: float32 [512], P(('gx', 'gy')), may hold values from 0.002 to 0.02
Outputs:
- velocity_out: float32 [3, 128, 64, 128], P(None, 'gx', 'gy')
- member_out: float32 [3, 512], P(None, ('gx', 'gy'))
The draws below stay inside these ranges and needn't reach their ends.
Inputs may be any that keep to these rules, and one draw needn't show every extreme that they name: `station_member`: members m with m // 16 = d belong to the device d of the joined axis gx+gy, which holds brick d. The stations of a brick name only members of that brick's device or of the devices beside it along gx (same gy index). Among the 4096 stations of one brick no member is named more than 128 times, and some member exactly 128 times; every member has stations in its own brick.
All inputs are finite; a program needn't handle non-finite values.
Results may differ from the reference program's by a relative error of at most 0.00014.
Values sent between devices are 32-bit elements; how exact they have to be, the bound alone decides.
No kernel may reach another device: no remote copies, remote signals or barrier semaphores. Data moves between devices by JAX's collectives and lax.ppermute only.
A program may use at most 64 MiB of HBM per device.

```python
import math
import jax
import jax.numpy as jnp
from jax import lax

CX = 16
CY = 16
CZ = 128
STN_DEV = 4096
MEM_DEV = 16
MOST = 128
STEPS = 2
NX = 128
NY = 64
NZ = 128
STATIONS = 131072
MEMBERS = 512
N_GX = 8
N_GY = 4


def draw_station_member(key, part):
    key = jax.random.fold_in(key, 11)
    bricks = N_GX * N_GY
    per_dir = MEM_DEV * MOST
    width = 3 * per_dir
    raw = jax.random.randint(key, (bricks, width), 0, 65536, dtype=jnp.int32)
    slot_ids = jnp.arange(width, dtype=jnp.int32)[None, :]
    brick_ids = jnp.arange(bricks, dtype=jnp.int32)[:, None]
    brick_x = brick_ids // N_GY
    direction = slot_ids // per_dir
    within = slot_ids % per_dir
    local = within // MOST
    rank = within % MOST
    scores = raw * width + slot_ids
    missing = (direction == 1) & (brick_x == N_GX - 1) | (direction == 2) & (brick_x == 0)
    forced = (direction == 0) & ((local == 0) | (rank == 0))
    scores = jnp.where(forced, slot_ids - width, scores)
    scores = jnp.where(missing, 1073741824 + slot_ids, scores)
    chosen = jnp.argsort(scores, axis=1, stable=True)[:, :STN_DEV].astype(jnp.int32)
    chosen_dir = chosen // per_dir
    chosen_local = chosen % per_dir // MOST
    offset = jnp.where(chosen_dir == 1, 1, jnp.where(chosen_dir == 2, -1, 0)).astype(jnp.int32)
    owner = (brick_x + offset) * N_GY + brick_ids % N_GY
    member = owner * MEM_DEV + chosen_local
    return member.reshape(STATIONS, 1).astype(jnp.int32)


def set_ends(drawn, stream_key, low, top_value):
    place = [jax.random.randint(jax.random.fold_in(stream_key, axis), (), 0, length) for axis, length in enumerate(drawn.shape)]
    main_axis = drawn.shape.index(max(drawn.shape))
    next_to = place[:main_axis] + [(place[main_axis] + 1) % drawn.shape[main_axis]] + place[main_axis + 1:]
    return drawn.at[tuple(place)].set(low).at[tuple(next_to)].set(top_value)


def levels(key, extent, shards, least, high):
    loudness = 1.0
    for position, blocks in shards:
        steps = jax.random.uniform(jax.random.fold_in(jax.random.fold_in(key, 6), position), (blocks,), jnp.float32, least / len(shards), high / len(shards))
        loudness = loudness * jnp.repeat(jnp.exp(steps), extent[position] // blocks).reshape((-1,) + (1,) * (len(extent) - 1 - position))
    return loudness


def scatter_about(rng, dims, spread, bound, pieces=(), held_as=jnp.bfloat16):
    level = levels(rng, dims, pieces, -0.22, 0.18) if pieces else 1.0
    entries = jax.random.normal(rng, dims, jnp.float32) * spread * level
    return jnp.minimum(jnp.maximum(entries, -bound), bound).astype(held_as)


def setup_inputs(seed: int = 0) -> dict:
    key_of = jax.random.split(jax.random.key(seed), 9)
    velocity = scatter_about(key_of[0], (3, NX, NY, NZ), 1.0, 6.0, ((1, 8), (2, 4)), jnp.float32)
    velocity_old = scatter_about(key_of[1], (3, NX, NY, NZ), 1.0, 6.0, ((1, 8), (2, 4)), jnp.float32)
    station_cell = set_ends(jax.random.randint(key_of[2], (STATIONS,), 0, CX * CY * CZ), jax.random.fold_in(key_of[2], 1), 0, (CX * CY * CZ) - 1).astype(jnp.int32)
    station_member = draw_station_member(jax.random.fold_in(key_of[8], 71), 0)
    drag_coef = jnp.clip(jnp.exp(math.log(1.0) - 2.3025851 * jax.random.uniform(key_of[4], (STATIONS,), jnp.float32) ** levels(key_of[4], (STATIONS,), ((0, 32),), -0.2, 0.2)), 0.1, 1.0)
    inertia_coef = jnp.clip(jnp.exp(math.log(3.0) - 2.3025851 * jax.random.uniform(key_of[5], (STATIONS,), jnp.float32) ** levels(key_of[5], (STATIONS,), ((0, 32),), -0.2, 0.2)), 0.3, 3.0)
    member_velocity = scatter_about(key_of[6], (3, MEMBERS), 1.0, 6.0, ((1, 32),), jnp.float32)
    member_inv_mass = jnp.clip(jnp.exp(math.log(0.02) - 2.30258502 * jax.random.uniform(key_of[7], (MEMBERS,), jnp.float32) ** levels(key_of[7], (MEMBERS,), ((0, 32),), -0.2, 0.2)), 0.002, 0.02)
    return {"velocity": velocity, "velocity_old": velocity_old, "station_cell": station_cell, "station_member": station_member, "drag_coef": drag_coef, "inertia_coef": inertia_coef, "member_velocity": member_velocity, "member_inv_mass": member_inv_mass}


viscous = 0.125
softening = 0.01

def smooth_axis(field, axis):
    widths = [(0, 0)] * field.ndim
    widths[axis] = (1, 1)
    padded = jnp.pad(field, widths)
    length = field.shape[axis]
    lower = lax.slice_in_dim(padded, 0, length, axis=axis)
    middle = lax.slice_in_dim(padded, 1, length + 1, axis=axis)
    upper = lax.slice_in_dim(padded, 2, length + 2, axis=axis)
    return 0.25 * lower + 0.5 * middle + 0.25 * upper

def neighbour_sum(field):
    padded = jnp.pad(field, ((0, 0), (1, 1), (1, 1), (1, 1)))
    total = padded[:, 2:, 1:-1, 1:-1] + padded[:, :-2, 1:-1, 1:-1]
    total = total + padded[:, 1:-1, 2:, 1:-1] + padded[:, 1:-1, :-2, 1:-1]
    total = total + padded[:, 1:-1, 1:-1, 2:] + padded[:, 1:-1, 1:-1, :-2]
    return total

def reference(velocity, velocity_old, station_cell, station_member, drag_coef, inertia_coef, member_velocity, member_inv_mass):
    indices = jnp.arange(STATIONS, dtype=jnp.int32)
    bricks = indices // STN_DEV
    brick_x = bricks // N_GY
    brick_y = bricks % N_GY
    coord_x = brick_x * CX + station_cell // (CY * CZ)
    coord_y = brick_y * CY + station_cell // CZ % CY
    coord_z = station_cell % CZ
    members = station_member[:, 0]
    for step_index in range(STEPS):
        samples = velocity[:, coord_x, coord_y, coord_z]
        old_samples = velocity_old[:, coord_x, coord_y, coord_z]
        relative = samples - member_velocity[:, members]
        speeds = jnp.sqrt(lax.optimization_barrier(jnp.sum(relative * relative, axis=0)) + softening)
        forces = drag_coef * speeds * relative + inertia_coef * (samples - old_samples)
        totals = jnp.zeros((3, MEMBERS), jnp.float32).at[:, members].add(forces)
        member_velocity = member_velocity + member_inv_mass * totals
        point_force = jnp.zeros_like(velocity).at[:, coord_x, coord_y, coord_z].add(-forces)
        source = smooth_axis(smooth_axis(smooth_axis(point_force, 1), 2), 3)
        updated = velocity + viscous * (neighbour_sum(velocity) - 6.0 * velocity) + source
        velocity_old = velocity
        velocity = updated
    return (velocity, member_velocity)
```

```python
import functools

import jax
import jax.numpy as jnp
from jax import lax
from jax.experimental import pallas as pl
from jax.experimental.pallas import tpu as pltpu
from jax.sharding import PartitionSpec as P

STEPS = 2
LANES = 128
WIDE = 256

viscous = 0.125
softening = 0.01

f32 = jnp.float32
bf16 = jnp.bfloat16
VMEM = pltpu.VMEM


def call(body, outs, scratch=(), flops=0, size=0, limit=24):
    return pl.pallas_call(
        body,
        out_shape=[jax.ShapeDtypeStruct(s, f32) for s in outs],
        scratch_shapes=list(scratch),
        compiler_params=pltpu.CompilerParams(vmem_limit_bytes=limit << 20),
        cost_estimate=pl.CostEstimate(flops=flops, bytes_accessed=size, transcendentals=0),
    )


def split(x):
    top = x.astype(bf16)
    return top, (x - top.astype(f32)).astype(bf16)


def one_hot_t(index_row, count):
    ids = lax.broadcasted_iota(jnp.int32, (count, index_row.shape[1]), 0)
    return jnp.where(ids == index_row, 1.0, 0.0).astype(bf16)


def wide_row(ref, first):
    return jnp.concatenate([ref[pl.ds(first, 1), :], ref[pl.ds(first + 1, 1), :]], axis=1)


def pick_depth(product, depth_row, shape_z):
    ids = lax.broadcasted_iota(jnp.int32, (shape_z, depth_row.shape[1]), 0)
    hit = ids == depth_row
    count = product.shape[0] // shape_z
    return [
        jnp.sum(jnp.where(hit, product[k * shape_z : (k + 1) * shape_z], 0.0), axis=0, keepdims=True)
        for k in range(count)
    ]


def gather_columns(tables, table_ref, cell_ref, write, onehot_ref=None):
    rows, shape_z = tables[0].shape
    count = len(tables)
    for k, table in enumerate(tables):
        top, low = split(table.T)
        table_ref[0, k * shape_z : (k + 1) * shape_z, :] = top
        table_ref[1, k * shape_z : (k + 1) * shape_z, :] = low
    chunks = cell_ref.shape[0] // 2

    def step(j, carry):
        cell = wide_row(cell_ref, 2 * j)
        hot = one_hot_t(cell // shape_z, rows)
        product = jnp.dot(table_ref[0, : count * shape_z], hot, preferred_element_type=f32)
        product = product + jnp.dot(table_ref[1, : count * shape_z], hot, preferred_element_type=f32)
        for k, picked in enumerate(pick_depth(product, cell % shape_z, shape_z)):
            write(k, j, picked)
        return carry

    lax.fori_loop(0, chunks, step, 0, unroll=2)


def sample_kernel(v_ref, old_ref, cell_ref, inertia_ref, s_ref, acc_ref, table_ref):
    shape = v_ref.shape
    rows = shape[1] * shape[2]
    tables = [r[k].reshape(rows, shape[3]) for r in (v_ref, old_ref) for k in range(3)]

    def write(k, j, picked):
        ref = s_ref if k < 3 else acc_ref
        ref[k % 3, pl.ds(2 * j, 1), :] = picked[:, :LANES]
        ref[k % 3, pl.ds(2 * j + 1, 1), :] = picked[:, LANES:]

    gather_columns(tables, table_ref, cell_ref, write)
    for k in range(3):
        acc_ref[k] = inertia_ref[...] * (s_ref[k] - acc_ref[k])


def member_lookup(table, slot):
    wide = jnp.broadcast_to(table, slot.shape)
    return jnp.take_along_axis(wide, slot, axis=1)


def forces_deposit(samples, acc, slot, drag, table, cell_ref, force_ref, column_ref, field_ref, slot_ref):
    relative = [samples[k] - member_lookup(table[k : k + 1], slot) for k in range(3)]
    square = relative[0] * relative[0] + relative[1] * relative[1] + relative[2] * relative[2]
    speed = drag * jnp.sqrt(square + softening)
    for k in range(3):
        force = speed * relative[k] + acc[k]
        top = force.astype(bf16).astype(f32)
        force_ref[k] = top
        force_ref[3 + k] = force - top
    slot_ref[...] = slot
    rows, width = field_ref.shape
    shape_z = width // 6
    chunks = cell_ref.shape[0] // 2
    total0 = jnp.zeros((8, LANES), f32)
    field_ref[...] = jnp.zeros_like(field_ref)

    def step(j, total):
        cell = wide_row(cell_ref, 2 * j)
        hot = one_hot_t(cell // shape_z, rows)
        depth = one_hot_t(cell % shape_z, shape_z) > 0
        pieces = [wide_row(force_ref.at[k], 2 * j) for k in range(6)]
        for k in range(6):
            wide = jnp.broadcast_to(pieces[k].astype(bf16), depth.shape)
            column_ref[k * shape_z : (k + 1) * shape_z] = jnp.where(depth, wide, jnp.zeros_like(wide))
        field_ref[...] += lax.dot_general(
            hot, column_ref[...], (((1,), (1,)), ((), ())), preferred_element_type=f32
        )
        members = one_hot_t(wide_row(slot_ref, 2 * j), LANES)
        stack = jnp.concatenate(pieces + [jnp.zeros((2, WIDE), f32)], axis=0).astype(bf16)
        return total + lax.dot_general(
            stack, members, (((1,), (1,)), ((), ())), preferred_element_type=f32
        )

    total = lax.fori_loop(0, chunks, step, total0, unroll=2)
    total = total + pltpu.roll(total, 5, axis=0)
    half = width // 2
    return total, -(field_ref[:, :half] + field_ref[:, half:])


def shift(x, axis, by):
    n = x.shape[axis]
    if axis == x.ndim - 1 or axis == x.ndim - 2:
        moved = pltpu.roll(x, by % n, axis=axis)
        ids = lax.broadcasted_iota(jnp.int32, x.shape, axis)
        return jnp.where(ids == (0 if by > 0 else n - 1), 0.0, moved)
    zero = jnp.zeros_like(lax.slice_in_dim(x, 0, 1, axis=axis))
    if by > 0:
        return jnp.concatenate([zero, lax.slice_in_dim(x, 0, n - 1, axis=axis)], axis=axis)
    return jnp.concatenate([lax.slice_in_dim(x, 1, n, axis=axis), zero], axis=axis)


def both(x, axis):
    return shift(x, axis, 1) + shift(x, axis, -1)


def local_update(v_ref, field, l_ref, spill_ref, y_refs, own_y):
    comps, nx, ny, nz = v_ref.shape
    for c in range(comps):
        v = v_ref[c]
        w = field[:, c * nz : (c + 1) * nz].reshape(nx, ny, nz)
        w = 0.5 * w + 0.25 * both(w, 2)
        w_y = 0.5 * w + 0.25 * both(w, 1)
        w_x = 0.5 * w_y + 0.25 * both(w_y, 0)
        beside = both(v, 0) + both(v, 1) + both(v, 2)
        l_ref[c] = v + viscous * (beside - 6.0 * v) + w_x
        spill_ref[0, c] = 0.25 * w_y[0] + viscous * v[0]
        spill_ref[1, c] = 0.25 * w_y[nx - 1] + viscous * v[nx - 1]
        ends = []
        for y in (0, ny - 1):
            edge = 0.25 * w[:, y, :]
            end = 0.5 * edge + 0.25 * both(edge, 0) + viscous * v[:, y, :]
            ends.append((end, 0.25 * edge[0:1], 0.25 * edge[nx - 1 : nx]))
        even = own_y % 2 == 0
        for ref, flip in zip(y_refs, (even, jnp.logical_not(even))):
            for part, (low, high) in enumerate(zip(*ends)):
                chosen = jnp.where(flip, high, low)
                if part == 0:
                    ref[c] = chosen
                else:
                    ref[comps, 3 * (part - 1) + c : 3 * (part - 1) + c + 1, :] = chosen


def beside(even_msg, odd_msg, own, count):
    even = own % 2 == 0
    low = jnp.where(own > 0, jnp.where(even, odd_msg, even_msg), 0.0)
    high = jnp.where(own < count - 1, jnp.where(even, even_msg, odd_msg), 0.0)
    return low, high


def member_table(own, low, high, held):
    return low + pltpu.roll(own, held, axis=1) + pltpu.roll(high, 2 * held, axis=1)


def first_kernel(held, count_x, v_ref, s_ref, acc_ref, slot_ref, drag_ref, cell_ref, own_ref, even_ref, odd_ref,
                 l_ref, spill_ref, ye_ref, yo_ref, total_ref, table_ref,
                 force_ref, column_ref, field_ref, slot_copy):
    own_x = lax.axis_index("gx")
    low, high = beside(even_ref[...], odd_ref[...], own_x, count_x)
    table = member_table(own_ref[...], low, high, held)
    table_ref[...] = table
    samples = [s_ref[k] for k in range(3)]
    acc = [acc_ref[k] for k in range(3)]
    total, field = forces_deposit(samples, acc, slot_ref[...], drag_ref[...], table, cell_ref,
                                  force_ref, column_ref, field_ref, slot_copy)
    total_ref[...] = total
    local_update(v_ref, field, l_ref, spill_ref, (ye_ref, yo_ref), lax.axis_index("gy"))


def y_kernel(count_y, l_ref, spill_ref, even_ref, odd_ref, total_ref, l_out, xe_ref, xo_ref):
    comps, nx, ny, nz = l_ref.shape
    own_y = lax.axis_index("gy")
    low, high = beside(even_ref[...], odd_ref[...], own_y, count_y)
    l_out[...] = l_ref[...]
    even = lax.axis_index("gx") % 2 == 0
    ids = lax.broadcasted_iota(jnp.int32, (ny, nz), 0)
    for c in range(comps):
        l_out[c, :, 0, :] += low[c]
        l_out[c, :, ny - 1, :] += high[c]
        sides = []
        for side in range(2):
            row = 3 * side + c
            face = spill_ref[side, c]
            face = face + jnp.where(ids == 0, low[comps, row : row + 1], 0.0)
            face = face + jnp.where(ids == ny - 1, high[comps, row : row + 1], 0.0)
            sides.append(face)
        xe_ref[c] = jnp.where(even, sides[1], sides[0])
        xo_ref[c] = jnp.where(even, sides[0], sides[1])
    for ref in (xe_ref, xo_ref):
        ref[comps, 0:8, :] = total_ref[...]
        ref[comps, 8:16, :] = jnp.zeros_like(total_ref)


def second_kernel(held, count_x, s_ref, slot_ref, drag_ref, inertia_ref, cell_ref, mtable_ref, total_ref,
                  l_ref, xe_ref, xo_ref, te_ref, to_ref,
                  l_out, spill_ref, ye_ref, yo_ref, total_out, mtable_out,
                  v_ref, table_ref, sample_ref, force_ref, column_ref, field_ref, slot_copy):
    comps, nx, ny, nz = l_ref.shape
    own_x = lax.axis_index("gx")
    low, high = beside(xe_ref[...], xo_ref[...], own_x, count_x)
    v_ref[...] = l_ref[...]
    for c in range(comps):
        v_ref[c, 0] += low[c]
        v_ref[c, nx - 1] += high[c]
    second_even = own_x // 2 % 2 == 0
    low2 = jnp.where(own_x > 1, jnp.where(second_even, to_ref[...], te_ref[...]), 0.0)
    high2 = jnp.where(own_x < count_x - 2, jnp.where(second_even, te_ref[...], to_ref[...]), 0.0)
    low1, high1 = low[comps, 0:8], high[comps, 0:8]
    lane = lax.broadcasted_iota(jnp.int32, (8, LANES), 1)
    total = total_ref[...]
    total = total + pltpu.roll(low1, LANES - held, axis=1) + pltpu.roll(high1, held, axis=1)
    total = total + jnp.where(lane < held, pltpu.roll(low2, LANES - 2 * held, axis=1), 0.0)
    total = total + jnp.where(lane // held == 2, pltpu.roll(high2, 2 * held, axis=1), 0.0)
    old = mtable_ref[...]
    row = lax.broadcasted_iota(jnp.int32, (8, LANES), 0)
    table = jnp.where((row < 3) & (lane < 3 * held), old + old[3:4] * total, old)
    mtable_out[...] = table
    tables = [v_ref[k].reshape(nx * ny, nz) for k in range(comps)]

    def write(k, j, picked):
        sample_ref[k, pl.ds(2 * j, 1), :] = picked[:, :LANES]
        sample_ref[k, pl.ds(2 * j + 1, 1), :] = picked[:, LANES:]

    gather_columns(tables, table_ref, cell_ref, write)
    samples = [sample_ref[k] for k in range(3)]
    acc = [inertia_ref[...] * (samples[k] - s_ref[k]) for k in range(3)]
    total, field = forces_deposit(samples, acc, slot_ref[...], drag_ref[...], table, cell_ref,
                                  force_ref, column_ref, field_ref, slot_copy)
    total_out[...] = total
    local_update(v_ref, field, l_out, spill_ref, (ye_ref, yo_ref), lax.axis_index("gy"))


def last_kernel(held, count_x, l_ref, xe_ref, xo_ref, mtable_ref, total_ref, v_out, m_out):
    comps, nx, ny, nz = l_ref.shape
    low, high = beside(xe_ref[...], xo_ref[...], lax.axis_index("gx"), count_x)
    v_out[...] = l_ref[...]
    for c in range(comps):
        v_out[c, 0] += low[c]
        v_out[c, nx - 1] += high[c]
    total = total_ref[...] + pltpu.roll(low[comps, 0:8], LANES - held, axis=1)
    total = total + pltpu.roll(high[comps, 0:8], held, axis=1)
    table = mtable_ref[...]
    table = table + table[3:4] * total
    m_out[...] = pltpu.roll(table, LANES - held, axis=1)[0:3, :held]


def swaps(count, stride):
    even = [(i, i ^ stride) for i in range(count)]
    odd = [(i, (((i + stride) ^ stride) - stride) % count) for i in range(count)]
    return even, odd


def exchange(even_msg, odd_msg, axis, stride=1):
    even, odd = swaps(lax.axis_size(axis), stride)
    return lax.ppermute(even_msg, axis, even), lax.ppermute(odd_msg, axis, odd)


def per_device(velocity, velocity_old, station_cell, station_member, drag_coef, inertia_coef, member_velocity,
               member_inv_mass):
    count_x, count_y = lax.axis_size("gx"), lax.axis_size("gy")
    held = member_velocity.shape[1]
    comps, nx, ny, nz = velocity.shape
    rows = nx * ny
    stations = station_cell.shape[0]
    lines = (stations // LANES, LANES)
    cell = station_cell.reshape(lines)
    drag = drag_coef.reshape(lines)
    inertia = inertia_coef.reshape(lines)
    member = station_member.reshape(lines)
    offset = member // held // count_y - lax.axis_index("gx") + 1
    slot = offset * held + member % held
    own = jnp.concatenate([member_velocity, member_inv_mass[None]], axis=0)
    own = jnp.pad(own, ((0, 4), (0, LANES - held)))
    own_even, own_odd = exchange(own, own, "gx")

    def gather_flops(c):
        return 4 * c * nz * rows * stations

    table = lambda c: pltpu.VMEM((2, c * nz, rows), bf16)
    work = [
        pltpu.VMEM((6,) + lines, f32),
        pltpu.VMEM((6 * nz, WIDE), bf16),
        pltpu.VMEM((rows, 6 * nz), f32),
        pltpu.VMEM(lines, jnp.int32),
    ]
    face = (comps + 1, nx, nz)
    grid = velocity.shape
    samples, acc = call(
        sample_kernel, [(3,) + lines] * 2, [table(6)], gather_flops(6), 1 << 21
    )(velocity, velocity_old, cell, inertia)
    parts = [grid, (2, comps, ny, nz), face, face, (8, LANES), (8, LANES)]
    local, spill, y_even, y_odd, total, mtable = call(
        functools.partial(first_kernel, held, count_x), parts, work, gather_flops(3), 1 << 21
    )(velocity, samples, acc, slot, drag, cell, own, own_even, own_odd)

    def y_stage(local, spill, y_even, y_odd, total):
        y_even, y_odd = exchange(y_even, y_odd, "gy")
        return call(functools.partial(y_kernel, count_y), [grid, face, face], (), 1 << 20, 1 << 19)(
            local, spill, y_even, y_odd, total
        )

    second_even, second_odd = exchange(total, total, "gx", 2)
    local, x_even, x_odd = y_stage(local, spill, y_even, y_odd, total)
    x_even, x_odd = exchange(x_even, x_odd, "gx")
    local, spill, y_even, y_odd, total, mtable = call(
        functools.partial(second_kernel, held, count_x),
        parts,
        [pltpu.VMEM(grid, f32), table(3), pltpu.VMEM((3,) + lines, f32)] + work,
        gather_flops(6),
        1 << 21,
    )(samples, slot, drag, inertia, cell, mtable, total, local, x_even, x_odd, second_even, second_odd)
    local, x_even, x_odd = y_stage(local, spill, y_even, y_odd, total)
    x_even, x_odd = exchange(x_even, x_odd, "gx")
    velocity, members = call(functools.partial(last_kernel, held, count_x), [grid, (3, held)], (), 1 << 20, 1 << 20)(
        local, x_even, x_odd, mtable, total
    )
    return velocity, members


def solution(mesh):
    return jax.shard_map(
        per_device,
        mesh=mesh,
        in_specs=(
            P(None, "gx", "gy", None),
            P(None, "gx", "gy", None),
            P(("gx", "gy")),
            P(("gx", "gy"), None),
            P(("gx", "gy")),
            P(("gx", "gy")),
            P(None, ("gx", "gy")),
            P(("gx", "gy")),
        ),
        out_specs=(P(None, "gx", "gy", None), P(None, ("gx", "gy"))),
        check_vma=False,
    )
```

```python
import functools

import jax
import jax.numpy as jnp
from jax import lax
from jax.experimental import pallas as pl
from jax.experimental.pallas import tpu as pltpu
from jax.sharding import PartitionSpec as P

STEPS = 2
LANES = 128
WIDE = 256

viscous = 0.125
softening = 0.01

f32 = jnp.float32
i32 = jnp.int32
bf16 = jnp.bfloat16
HBM = pl.BlockSpec(memory_space=pltpu.HBM)
NT = (((1,), (1,)), ((), ()))


def call(name, body, ins, outs, scratch=(), in_hbm=(), out_hbm=(), flops=0, size=1 << 18, aliases=None):
    whole = pl.BlockSpec(memory_space=pltpu.VMEM)
    ins = [pltpu.with_memory_space_constraint(x, pltpu.HBM) if k in in_hbm else x for k, x in enumerate(ins)]
    outs = [pltpu.HBM(x.shape, x.dtype) if k in out_hbm else x for k, x in enumerate(outs)]
    return pl.pallas_call(
        body,
        name=name,
        out_shape=outs,
        in_specs=[HBM if k in in_hbm else whole for k in range(len(ins))],
        out_specs=[HBM if k in out_hbm else whole for k in range(len(outs))],
        scratch_shapes=list(scratch),
        input_output_aliases=aliases or {},
        compiler_params=pltpu.CompilerParams(vmem_limit_bytes=24 << 20),
        cost_estimate=pl.CostEstimate(flops=flops, bytes_accessed=size, transcendentals=0),
    )(*ins)


def real(*shape):
    return jax.ShapeDtypeStruct(shape, f32)


def split(x):
    top = x.astype(bf16)
    return top, (x - top.astype(f32)).astype(bf16)


def hot_rows(index, count):
    ids = lax.broadcasted_iota(i32, (count, index.shape[1]), 0).astype(f32).astype(bf16)
    wide = jnp.broadcast_to(index.astype(f32).astype(bf16), ids.shape)
    return jnp.where(ids == wide, jnp.ones_like(wide), jnp.zeros_like(wide))


def wide_row(ref, j):
    return jnp.concatenate([ref[2 * j : 2 * j + 1, :], ref[2 * j + 1 : 2 * j + 2, :]], axis=1)


def store_row(ref, k, j, row):
    ref[k, 2 * j : 2 * j + 1, :] = row[:, :LANES]
    ref[k, 2 * j + 1 : 2 * j + 2, :] = row[:, LANES:]


def pick(product, depth_row, count):
    z = product.shape[0] // count
    hit = lax.broadcasted_iota(i32, (z, depth_row.shape[1]), 0) == depth_row
    return [
        jnp.sum(jnp.where(hit, product[k * z : (k + 1) * z], 0.0), axis=0, keepdims=True) for k in range(count)
    ]


def gather(fields, table_ref, row_ref, depth_ref, out_ref):
    rows, z = fields[0].shape
    count = len(fields)
    for k, field in enumerate(fields):
        table_ref[0, k * z : (k + 1) * z, :], table_ref[1, k * z : (k + 1) * z, :] = split(field.T)
    for j in range(row_ref.shape[0] // 2):
        hot = hot_rows(wide_row(row_ref, j), rows)
        product = jnp.dot(table_ref[0], hot, preferred_element_type=f32)
        product = product + jnp.dot(table_ref[1], hot, preferred_element_type=f32)
        for k, row in enumerate(pick(product, wide_row(depth_ref, j), count)):
            store_row(out_ref, k, j, row)


def columns(ref, force_ref, depth_row, z, j, groups):
    hit = hot_rows(depth_row, z) > 0
    for c in range(3):
        for p, piece in enumerate(split(wide_row(force_ref.at[c], j))):
            wide = jnp.broadcast_to(piece, hit.shape)
            at = (p * groups + c) * z
            ref[at : at + z, :] = jnp.where(hit, wide, jnp.zeros_like(wide))


def moved(x, axis, by):
    n = x.shape[axis]
    if axis >= x.ndim - 2:
        ids = lax.broadcasted_iota(i32, x.shape, axis)
        return jnp.where(ids == (0 if by > 0 else n - 1), 0.0, pltpu.roll(x, by % n, axis=axis))
    zero = jnp.zeros_like(lax.slice_in_dim(x, 0, 1, axis=axis))
    if by > 0:
        return jnp.concatenate([zero, lax.slice_in_dim(x, 0, n - 1, axis=axis)], axis=axis)
    return jnp.concatenate([lax.slice_in_dim(x, 1, n, axis=axis), zero], axis=axis)


def both(x, axis):
    return moved(x, axis, 1) + moved(x, axis, -1)


def smooth(x, axis):
    return 0.5 * x + 0.25 * both(x, axis)


def beside(even_msg, odd_msg, own, count):
    even = own % 2 == 0
    low = jnp.where(own > 0, jnp.where(even, odd_msg, even_msg), 0.0)
    high = jnp.where(own < count - 1, jnp.where(even, even_msg, odd_msg), 0.0)
    return low, high


def add_y(c, face_low, face_high, ref):
    ny = ref.shape[2]
    ref[c, :, 0, :] += face_low[c]
    ref[c, :, ny - 1, :] += face_high[c]


def edges(v_ref, force_ref, key_ref, low_ref, col_ref, acc_ref, spill_ref, y_refs):
    comps, nx, ny, nz = v_ref.shape
    ring = 2 * (nx + ny)
    parts = WIDE // ring
    z = nz // parts
    col_ref[...] = jnp.zeros_like(col_ref)
    for j in range(key_ref.shape[0] // 2):
        hot = hot_rows(wide_row(key_ref, j), WIDE)
        columns(col_ref, force_ref, wide_row(low_ref, j), z, j, 4)
        part = lax.dot_general(hot, col_ref[...], NT, preferred_element_type=f32)
        acc_ref[...] = part if j == 0 else acc_ref[...] + part
    found = -(acc_ref[:, :LANES] + acc_ref[:, LANES:])
    lane = lax.broadcasted_iota(i32, (ring, LANES), 1) // z
    yid = lax.broadcasted_iota(i32, (ny, nz), 0)
    even = lax.axis_index("gy") % 2 == 0
    for c in range(comps):
        w = jnp.zeros((ring, nz), f32)
        for h in range(parts):
            block = found[h * ring : (h + 1) * ring]
            by = (h - c) * z % LANES
            block = pltpu.roll(block, by, axis=1) if by else block
            w = jnp.where(lane == h, block, w)
        w = smooth(w, 1)
        y_ends = (w[:nx], w[nx : 2 * nx])
        for side, x in ((0, 0), (1, nx - 1)):
            face = w[2 * nx + side * ny : 2 * nx + (side + 1) * ny]
            face = jnp.where(yid == 0, y_ends[0][x : x + 1], face)
            face = jnp.where(yid == ny - 1, y_ends[1][x : x + 1], face)
            spill_ref[side, c] = 0.25 * smooth(face, 0) + viscous * v_ref[c, x]
        low, high = [
            (smooth(0.25 * w_y, 0) + viscous * v_ref[c, :, y, :], 0.0625 * w_y[0:1], 0.0625 * w_y[nx - 1 : nx])
            for y, w_y in zip((0, ny - 1), y_ends)
        ]
        for ref, flip in zip(y_refs, (even, jnp.logical_not(even))):
            ref[c] = jnp.where(flip, high[0], low[0])
            for side in range(2):
                at = 3 * side + c
                ref[comps, at : at + 1, :] = jnp.where(flip, high[1 + side], low[1 + side])


def forces(samples, acc, slot, drag, table, force_ref):
    relative = [
        samples[c] - jnp.take_along_axis(jnp.broadcast_to(table[c : c + 1], slot.shape), slot, axis=1)
        for c in range(3)
    ]
    square = relative[0] * relative[0] + relative[1] * relative[1] + relative[2] * relative[2]
    speed = drag * jnp.sqrt(square + softening)
    for c in range(3):
        force_ref[c] = speed * relative[c] + acc[c]


def totals_kernel(force_ref, slot_ref, after_ref, total_ref):
    total = jnp.zeros((8, LANES), f32)
    for j in range(slot_ref.shape[0] // 2):
        rows = [wide_row(force_ref.at[c], j) for c in range(3)]
        tops = [r.astype(bf16).astype(f32) for r in rows]
        rest = [r - t for r, t in zip(rows, tops)]
        stack = jnp.concatenate(tops + rest + [jnp.zeros((2, WIDE), f32)], axis=0).astype(bf16)
        total = total + lax.dot_general(
            stack, hot_rows(wide_row(slot_ref, j), LANES), NT, preferred_element_type=f32
        )
    total_ref[...] = total + pltpu.roll(total, 5, axis=0)


def start_kernel(held, count_y, v_any, old_any, cell_any, member_any, drag_any, inertia_any, mv_any, mass_any,
                 v_ref, old_ref, drag_ref, inertia_ref, slot_ref, row_ref, depth_ref, key_ref, low_ref, xkey_ref,
                 xlow_ref, own_ref, s_ref, cell_ref, member_ref, mv_ref, mass_ref, table_ref, sem):
    pairs = [(cell_any, cell_ref), (v_any, v_ref), (member_any, member_ref), (mv_any, mv_ref), (mass_any, mass_ref),
             (drag_any, drag_ref), (inertia_any, inertia_ref), (old_any, old_ref)]
    copies = [pltpu.make_async_copy(a, b, sem.at[k]) for k, (a, b) in enumerate(pairs)]
    for copy in copies:
        copy.start()
    comps, nx, ny, nz = v_ref.shape
    copies[0].wait()
    cell = cell_ref[...]
    row, depth = lax.div(cell, nz), lax.rem(cell, nz)
    row_ref[...] = row
    depth_ref[...] = depth
    x, y = lax.div(row, ny), lax.rem(row, ny)
    ring = 2 * (nx + ny)
    edge = jnp.where(x == 0, 2 * nx + y, jnp.where(x == nx - 1, 2 * nx + ny + y, -1))
    edge = jnp.where(y == 0, x, jnp.where(y == ny - 1, nx + x, edge))
    z = nz * ring // WIDE
    key_ref[...] = jnp.where(edge < 0, -1, lax.div(depth, z) * ring + edge)
    low_ref[...] = lax.rem(depth, z)
    face = jnp.where(x == 0, y, jnp.where(x == nx - 1, ny + y, -1))
    z = nz * 2 * ny // WIDE
    xkey_ref[...] = jnp.where(face < 0, -1, lax.div(depth, z) * (2 * ny) + face)
    xlow_ref[...] = lax.rem(depth, z)
    copies[1].wait()
    gather([v_ref[k].reshape(nx * ny, nz) for k in range(comps)], table_ref, row_ref, depth_ref, s_ref)
    for copy in copies[2:]:
        copy.wait()
    member = member_ref[...]
    owner = lax.div(lax.div(member, held), count_y)
    slot_ref[...] = (owner - lax.axis_index("gx") + 1) * held + lax.rem(member, held)
    own_ref[...] = jnp.zeros_like(own_ref)
    own_ref[0:3, 0:held] = mv_ref[...]
    own_ref[3:4, 0:held] = mass_ref[...]


def old_kernel(old_ref, row_ref, depth_ref, inertia_ref, s_ref, acc_ref, table_ref):
    comps, nx, ny, nz = old_ref.shape
    gather([old_ref[k].reshape(nx * ny, nz) for k in range(comps)], table_ref, row_ref, depth_ref, acc_ref)
    for c in range(comps):
        acc_ref[c] = inertia_ref[...] * (s_ref[c] - acc_ref[c])


def first_kernel(held, count_x, v_ref, s_ref, acc_ref, slot_ref, drag_ref, key_ref, low_ref, own_ref, even_ref,
                 odd_ref, force_ref, mtable_ref, spill_ref, ye_ref, yo_ref, col_ref, field_ref):
    low, high = beside(even_ref[...], odd_ref[...], lax.axis_index("gx"), count_x)
    table = low + pltpu.roll(own_ref[...], held, axis=1) + pltpu.roll(high, 2 * held, axis=1)
    mtable_ref[...] = table
    forces([s_ref[c] for c in range(3)], [acc_ref[c] for c in range(3)], slot_ref[...], drag_ref[...], table,
           force_ref)
    edges(v_ref, force_ref, key_ref, low_ref, col_ref, field_ref, spill_ref, (ye_ref, yo_ref))


def deposit_kernel(force_ref, row_ref, depth_ref, after_ref, out_ref, col_ref, acc_ref):
    comps, rows, nz = out_ref.shape
    for j in range(row_ref.shape[0] // 2):
        hot = hot_rows(wide_row(row_ref, j), rows)
        columns(col_ref, force_ref, wide_row(depth_ref, j), nz, j, 3)
        part = lax.dot_general(hot, col_ref[...], NT, preferred_element_type=f32)
        acc_ref[...] = part if j == 0 else acc_ref[...] + part
    for c in range(comps):
        out_ref[c] = -(acc_ref[:, c * nz : (c + 1) * nz] + acc_ref[:, (3 + c) * nz : (4 + c) * nz])


def turn_kernel(count_y, spill_ref, even_ref, odd_ref, total_ref, after_ref, xe_ref, xo_ref):
    comps, ny, nz = spill_ref.shape[1:]
    low, high = beside(even_ref[comps], odd_ref[comps], lax.axis_index("gy"), count_y)
    even = lax.axis_index("gx") % 2 == 0
    ids = lax.broadcasted_iota(i32, (ny, nz), 0)
    for c in range(comps):
        sides = []
        for side in range(2):
            at = 3 * side + c
            face = spill_ref[side, c]
            face = face + jnp.where(ids == 0, low[at : at + 1], 0.0)
            face = face + jnp.where(ids == ny - 1, high[at : at + 1], 0.0)
            sides.append(face)
        xe_ref[c] = jnp.where(even, sides[1], sides[0])
        xo_ref[c] = jnp.where(even, sides[0], sides[1])
    for ref in (xe_ref, xo_ref):
        ref[comps, 0:8, :] = total_ref[...]
        ref[comps, 8:16, :] = jnp.zeros_like(total_ref)


def own_update(c, v_ref, load_ref, l_ref, low, high):
    nx, ny, nz = v_ref.shape[1:]
    v = v_ref[c]
    w = smooth(smooth(smooth(load_ref[c].reshape(nx, ny, nz), 2), 1), 0)
    beside_all = both(v, 0) + both(v, 1) + both(v, 2)
    l_ref[c] = v + viscous * (beside_all - 6.0 * v) + w
    add_y(c, low, high, l_ref)


def middle_kernel(count_y, v_ref, load_ref, even_ref, odd_ref, row_ref, depth_ref, after_ref, l_ref, s_ref,
                  table_ref):
    comps, nx, ny, nz = v_ref.shape
    low, high = beside(even_ref[...], odd_ref[...], lax.axis_index("gy"), count_y)
    for c in range(comps):
        own_update(c, v_ref, load_ref, l_ref, low, high)
    gather([l_ref[k].reshape(nx * ny, nz) for k in range(comps)], table_ref, row_ref, depth_ref, s_ref)


def sum_totals(held, count_x, total, low1, high1, even2, odd2):
    own_x = lax.axis_index("gx")
    even = own_x // 2 % 2 == 0
    low2 = jnp.where(own_x > 1, jnp.where(even, odd2, even2), 0.0)
    high2 = jnp.where(own_x < count_x - 2, jnp.where(even, even2, odd2), 0.0)
    lane = lax.broadcasted_iota(i32, (8, LANES), 1)
    total = total + pltpu.roll(low1, LANES - held, axis=1) + pltpu.roll(high1, held, axis=1)
    total = total + jnp.where(lane < held, pltpu.roll(low2, LANES - 2 * held, axis=1), 0.0)
    return total + jnp.where(lane // held == 2, pltpu.roll(high2, 2 * held, axis=1), 0.0)


def second_kernel(held, count_x, l_ref, sp_ref, xe_ref, xo_ref, s_ref, inertia_ref, slot_ref, drag_ref, key_ref,
                  low_ref, xkey_ref, xlow_ref, old_table_ref, old_total_ref, te_ref, to_ref,
                  v_ref, force_ref, mtable_ref, spill_ref, ye_ref, yo_ref,
                  col_ref, field_ref, face_ref, sample_ref):
    comps, nx, ny, nz = l_ref.shape
    low, high = beside(xe_ref[...], xo_ref[...], lax.axis_index("gx"), count_x)
    total = sum_totals(held, count_x, old_total_ref[...], low[comps, 0:8], high[comps, 0:8], te_ref[...], to_ref[...])
    old = old_table_ref[...]
    row = lax.broadcasted_iota(i32, (8, LANES), 0)
    lane = lax.broadcasted_iota(i32, (8, LANES), 1)
    table = jnp.where((row < 3) & (lane < 3 * held), old + old[3:4] * total, old)
    mtable_ref[...] = table
    z = nz * 2 * ny // WIDE
    for c in range(comps):
        turned = jnp.concatenate([low[c], high[c]], axis=0).T
        wide = jnp.concatenate([turned[h * z : (h + 1) * z] for h in range(nz // z)], axis=1)
        face_ref[0, c * z : (c + 1) * z, :], face_ref[1, c * z : (c + 1) * z, :] = split(wide)
    for j in range(xkey_ref.shape[0] // 2):
        hot = hot_rows(wide_row(xkey_ref, j), WIDE)
        product = jnp.dot(face_ref[0], hot, preferred_element_type=f32)
        product = product + jnp.dot(face_ref[1], hot, preferred_element_type=f32)
        for k, found in enumerate(pick(product, wide_row(xlow_ref, j), comps)):
            store_row(sample_ref, k, j, found)
    v_ref[...] = l_ref[...]
    for c in range(comps):
        v_ref[c, 0] += low[c]
        v_ref[c, nx - 1] += high[c]
    samples = [sp_ref[c] + sample_ref[c] for c in range(comps)]
    acc = [inertia_ref[...] * (samples[c] - s_ref[c]) for c in range(comps)]
    forces(samples, acc, slot_ref[...], drag_ref[...], table, force_ref)
    edges(v_ref, force_ref, key_ref, low_ref, col_ref, field_ref, spill_ref, (ye_ref, yo_ref))


def finish_kernel(count_y, v_ref, load_ref, even_ref, odd_ref, after_ref, out_hbm, face_ref, l_ref, sem):
    comps, nx = v_ref.shape[:2]
    low, high = beside(even_ref[...], odd_ref[...], lax.axis_index("gy"), count_y)
    for c in range(comps):
        own_update(c, v_ref, load_ref, l_ref, low, high)
        pltpu.make_async_copy(l_ref.at[c], out_hbm.at[c], sem.at[c]).start()
        face_ref[c, 0] = l_ref[c, 0]
        face_ref[c, 1] = l_ref[c, nx - 1]
    for c in range(comps):
        pltpu.make_async_copy(l_ref.at[c], out_hbm.at[c], sem.at[c]).wait()


def last_kernel(held, count_x, face_ref, xe_ref, xo_ref, mtable_ref, total_ref, old_hbm, m_hbm, v_hbm, new_ref, m_ref, sem):
    comps, nx = v_hbm.shape[:2]
    low, high = beside(xe_ref[...], xo_ref[...], lax.axis_index("gx"), count_x)
    copies = []
    for side, part in enumerate((low, high)):
        for c in range(comps):
            new_ref[side, c] = face_ref[c, side] + part[c]
        copies.append(pltpu.make_async_copy(new_ref.at[side], v_hbm.at[:, side * (nx - 1)], sem.at[side]))
        copies[-1].start()
    total = total_ref[...] + pltpu.roll(low[comps, 0:8], LANES - held, axis=1)
    total = total + pltpu.roll(high[comps, 0:8], held, axis=1)
    table = mtable_ref[...]
    table = table + table[3:4] * total
    m_ref[...] = pltpu.roll(table, LANES - held, axis=1)[0:3, :held]
    copies.append(pltpu.make_async_copy(m_ref, m_hbm, sem.at[2]))
    copies[-1].start()
    for copy in copies:
        copy.wait()


def pairs(axis, stride, odd):
    count_x, count_y = lax.axis_size("gx"), lax.axis_size("gy")
    found = []
    for x in range(count_x):
        for y in range(count_y):
            at, count = (x, count_x) if axis == "gx" else (y, count_y)
            to = ((at + stride) ^ stride) - stride if odd else at ^ stride
            if axis == "gy":
                target = (x, to % count)
            else:
                target = (to, y) if 0 <= to < count else (x, y ^ 1)
            found.append((x * count_y + y, target[0] * count_y + target[1]))
    return found


def exchange(even_msg, odd_msg, axis, stride=1):
    both_axes = ("gx", "gy")
    return (
        lax.ppermute(even_msg, both_axes, pairs(axis, stride, False)),
        lax.ppermute(odd_msg, both_axes, pairs(axis, stride, True)),
    )


def per_device(velocity, velocity_old, station_cell, station_member, drag_coef, inertia_coef, member_velocity,
               member_inv_mass):
    count_x, count_y = lax.axis_size("gx"), lax.axis_size("gy")
    held = member_velocity.shape[1]
    grid = velocity.shape
    comps, nx, ny, nz = grid
    rows = nx * ny
    lines = (station_cell.shape[0] // LANES, LANES)
    ints = jax.ShapeDtypeStruct(lines, i32)
    one = real(*lines)
    three = real(3, *lines)
    tile = real(8, LANES)
    face = real(comps + 1, max(nx, ny), nz)
    spill = real(2, comps, ny, nz)
    product = 12 * nz * rows * lines[0] * LANES
    table = pltpu.VMEM((2, comps * nz, rows), bf16)

    (v, old, drag, inertia, slot, row, depth, key, low, xkey, xlow, own, s) = call(
        "start", functools.partial(start_kernel, held, count_y),
        (velocity, velocity_old, station_cell.reshape(lines), station_member.reshape(lines),
         drag_coef.reshape(lines), inertia_coef.reshape(lines), member_velocity, member_inv_mass.reshape(1, held)),
        [real(*grid)] * 2 + [one] * 2 + [ints] * 7 + [tile, three],
        [pltpu.VMEM(lines, i32), pltpu.VMEM(lines, i32), pltpu.VMEM((3, held), f32), pltpu.VMEM((1, held), f32),
         table, pltpu.SemaphoreType.DMA((8,))],
        in_hbm=range(8), flops=product,
    )
    own_even, own_odd = exchange(own, own, "gx")
    (acc,) = call("old_samples", old_kernel, (old, row, depth, inertia, s), [three], [table], flops=product)
    work = [pltpu.VMEM((WIDE, WIDE), bf16), pltpu.VMEM((WIDE, WIDE), f32)]
    edge_parts = [three, tile, spill, face, face]
    force, mtable, spills, y_even, y_odd = call(
        "first_forces", functools.partial(first_kernel, held, count_x),
        (v, s, acc, slot, drag, key, low, own, own_even, own_odd), edge_parts, work, flops=product // 2,
    )

    def turn(force, spills, y_even, y_odd):
        (total,) = call("totals", totals_kernel, (force, slot, y_even), [tile])
        y_even, y_odd = exchange(y_even, y_odd, "gy")
        (load,) = call(
            "deposit", deposit_kernel, (force, row, depth, total), [real(comps, rows, nz)],
            [pltpu.VMEM((6 * nz, WIDE), bf16), pltpu.VMEM((rows, 6 * nz), f32)], flops=product,
        )
        x_even, x_odd = call(
            "turn", functools.partial(turn_kernel, count_y), (spills, y_even, y_odd, total, load), [face, face]
        )
        return total, load, y_even, y_odd, x_even, x_odd

    total, load, y_even, y_odd, x_even, x_odd = turn(force, spills, y_even, y_odd)
    second_even, second_odd = exchange(total, total, "gx", 2)
    local, samples = call(
        "middle", functools.partial(middle_kernel, count_y), (v, load, y_even, y_odd, row, depth, x_even),
        [real(*grid), three], [table], flops=product,
    )
    x_even, x_odd = exchange(x_even, x_odd, "gx")
    z = nz * 2 * ny // WIDE
    v, force, mtable, spills, y_even, y_odd = call(
        "second_forces", functools.partial(second_kernel, held, count_x),
        (local, samples, x_even, x_odd, s, inertia, slot, drag, key, low, xkey, xlow, mtable, total,
         second_even, second_odd),
        [real(*grid)] + edge_parts, work + [pltpu.VMEM((2, comps * z, WIDE), bf16), pltpu.VMEM((3,) + lines, f32)],
        flops=product // 2,
    )
    total, load, y_even, y_odd, x_even, x_odd = turn(force, spills, y_even, y_odd)
    out, faces = call(
        "finish", functools.partial(finish_kernel, count_y), (v, load, y_even, y_odd, x_even),
        [real(*grid), real(comps, 2, ny, nz)], [pltpu.VMEM(grid, f32), pltpu.SemaphoreType.DMA((comps,))],
        out_hbm=(0,),
    )
    x_even, x_odd = exchange(x_even, x_odd, "gx")
    members, out = call(
        "last", functools.partial(last_kernel, held, count_x), (faces, x_even, x_odd, mtable, total, out),
        [real(3, held), real(*grid)], [pltpu.VMEM((2, comps, ny, nz), f32), pltpu.VMEM((3, held), f32), pltpu.SemaphoreType.DMA((3,))],
        in_hbm=(5,), out_hbm=(0, 1), aliases={5: 1},
    )
    return out, members


def solution(mesh):
    return jax.shard_map(
        per_device,
        mesh=mesh,
        in_specs=(
            P(None, "gx", "gy", None),
            P(None, "gx", "gy", None),
            P(("gx", "gy")),
            P(("gx", "gy"), None),
            P(("gx", "gy")),
            P(("gx", "gy")),
            P(None, ("gx", "gy")),
            P(("gx", "gy")),
        ),
        out_specs=(P(None, "gx", "gy", None), P(None, ("gx", "gy"))),
        check_vma=False,
    )
```

```python
import functools

import jax
import jax.numpy as jnp
from jax import lax
from jax.experimental import pallas as pl
from jax.experimental.pallas import tpu as pltpu
from jax.sharding import PartitionSpec as P

STEPS = 2
LANES = 128
WIDE = 256

viscous = 0.125
softening = 0.01

f32 = jnp.float32
i32 = jnp.int32
bf16 = jnp.bfloat16
HBM = pl.BlockSpec(memory_space=pltpu.HBM)
NT = (((1,), (1,)), ((), ()))


def call(name, body, ins, outs, scratch=(), in_hbm=(), out_hbm=(), flops=0, size=1 << 18, aliases=None):
    whole = pl.BlockSpec(memory_space=pltpu.VMEM)
    ins = [pltpu.with_memory_space_constraint(x, pltpu.HBM) if k in in_hbm else x for k, x in enumerate(ins)]
    outs = [pltpu.HBM(x.shape, x.dtype) if k in out_hbm else x for k, x in enumerate(outs)]
    return pl.pallas_call(
        body,
        name=name,
        out_shape=outs,
        in_specs=[HBM if k in in_hbm else whole for k in range(len(ins))],
        out_specs=[HBM if k in out_hbm else whole for k in range(len(outs))],
        scratch_shapes=list(scratch),
        input_output_aliases=aliases or {},
        compiler_params=pltpu.CompilerParams(vmem_limit_bytes=24 << 20),
        cost_estimate=pl.CostEstimate(flops=flops, bytes_accessed=size, transcendentals=0),
    )(*ins)


def real(*shape):
    return jax.ShapeDtypeStruct(shape, f32)


def split(x):
    top = x.astype(bf16)
    return top, (x - top.astype(f32)).astype(bf16)


def hot_rows(index, count):
    ids = lax.broadcasted_iota(i32, (count, index.shape[1]), 0).astype(f32).astype(bf16)
    wide = jnp.broadcast_to(index.astype(f32).astype(bf16), ids.shape)
    return jnp.where(ids == wide, jnp.ones_like(wide), jnp.zeros_like(wide))


def wide_row(ref, j):
    return jnp.concatenate([ref[2 * j : 2 * j + 1, :], ref[2 * j + 1 : 2 * j + 2, :]], axis=1)


def store_row(ref, k, j, row):
    ref[k, 2 * j : 2 * j + 1, :] = row[:, :LANES]
    ref[k, 2 * j + 1 : 2 * j + 2, :] = row[:, LANES:]


def pick(product, depth_row, count):
    z = product.shape[0] // count
    hit = lax.broadcasted_iota(i32, (z, depth_row.shape[1]), 0) == depth_row
    return [
        jnp.sum(jnp.where(hit, product[k * z : (k + 1) * z], 0.0), axis=0, keepdims=True) for k in range(count)
    ]


def gather(fields, table_ref, row_ref, depth_ref, out_ref):
    rows, z = fields[0].shape
    count = len(fields)
    for k, field in enumerate(fields):
        table_ref[0, k * z : (k + 1) * z, :], table_ref[1, k * z : (k + 1) * z, :] = split(field.T)
    for j in range(row_ref.shape[0] // 2):
        hot = hot_rows(wide_row(row_ref, j), rows)
        product = jnp.dot(table_ref[0], hot, preferred_element_type=f32)
        product = product + jnp.dot(table_ref[1], hot, preferred_element_type=f32)
        for k, row in enumerate(pick(product, wide_row(depth_ref, j), count)):
            store_row(out_ref, k, j, row)


def columns(ref, force_ref, depth_row, z, j, groups):
    hit = hot_rows(depth_row, z) > 0
    for c in range(3):
        for p, piece in enumerate(split(wide_row(force_ref.at[c], j))):
            wide = jnp.broadcast_to(piece, hit.shape)
            at = (p * groups + c) * z
            ref[at : at + z, :] = jnp.where(hit, wide, jnp.zeros_like(wide))


def moved(x, axis, by):
    n = x.shape[axis]
    if axis >= x.ndim - 2:
        ids = lax.broadcasted_iota(i32, x.shape, axis)
        return jnp.where(ids == (0 if by > 0 else n - 1), 0.0, pltpu.roll(x, by % n, axis=axis))
    zero = jnp.zeros_like(lax.slice_in_dim(x, 0, 1, axis=axis))
    if by > 0:
        return jnp.concatenate([zero, lax.slice_in_dim(x, 0, n - 1, axis=axis)], axis=axis)
    return jnp.concatenate([lax.slice_in_dim(x, 1, n, axis=axis), zero], axis=axis)


def both(x, axis):
    return moved(x, axis, 1) + moved(x, axis, -1)


def smooth(x, axis):
    return 0.5 * x + 0.25 * both(x, axis)


def beside(even_msg, odd_msg, own, count):
    even = own % 2 == 0
    low = jnp.where(own > 0, jnp.where(even, odd_msg, even_msg), 0.0)
    high = jnp.where(own < count - 1, jnp.where(even, even_msg, odd_msg), 0.0)
    return low, high


def add_y(c, face_low, face_high, ref):
    ny = ref.shape[2]
    ref[c, :, 0, :] += face_low[c]
    ref[c, :, ny - 1, :] += face_high[c]


def edges(v_ref, force_ref, key_ref, low_ref, slot_ref, col_ref, acc_ref, spill_ref, y_refs, total_ref):
    comps, nx, ny, nz = v_ref.shape
    ring = 2 * (nx + ny)
    parts = WIDE // ring
    z = nz // parts
    slots = acc_ref.shape[0] - WIDE
    free = 3 * z
    for p in range(2):
        col_ref[p * LANES + free : (p + 1) * LANES, :] = jnp.zeros((LANES - free, WIDE), bf16)
    for j in range(key_ref.shape[0] // 2):
        hot = jnp.concatenate([hot_rows(wide_row(key_ref, j), WIDE), hot_rows(wide_row(slot_ref, j), slots)], axis=0)
        columns(col_ref, force_ref, wide_row(low_ref, j), z, j, LANES // z)
        pieces = [split(wide_row(force_ref.at[c], j)) for c in range(3)]
        for p in range(2):
            rows = [piece[p].astype(f32) for piece in pieces] + [jnp.zeros((13, WIDE), f32)]
            col_ref[p * LANES + free : p * LANES + free + 16, :] = jnp.concatenate(rows, axis=0).astype(bf16)
        part = lax.dot_general(hot, col_ref[...], NT, preferred_element_type=f32)
        acc_ref[...] = part if j == 0 else acc_ref[...] + part
    found = acc_ref[:, :LANES] + acc_ref[:, LANES:]
    sums = jnp.concatenate([found[WIDE:], jnp.zeros((LANES - slots, LANES), f32)], axis=0)
    total_ref[...] = sums.T[free : free + 8]
    found = -found[:WIDE]
    lane = lax.broadcasted_iota(i32, (ring, LANES), 1) // z
    yid = lax.broadcasted_iota(i32, (ny, nz), 0)
    even = lax.axis_index("gy") % 2 == 0
    for c in range(comps):
        w = jnp.zeros((ring, nz), f32)
        for h in range(parts):
            block = found[h * ring : (h + 1) * ring]
            by = (h - c) * z % LANES
            block = pltpu.roll(block, by, axis=1) if by else block
            w = jnp.where(lane == h, block, w)
        w = smooth(w, 1)
        y_ends = (w[:nx], w[nx : 2 * nx])
        for side, x in ((0, 0), (1, nx - 1)):
            face = w[2 * nx + side * ny : 2 * nx + (side + 1) * ny]
            face = jnp.where(yid == 0, y_ends[0][x : x + 1], face)
            face = jnp.where(yid == ny - 1, y_ends[1][x : x + 1], face)
            spill_ref[side, c] = 0.25 * smooth(face, 0) + viscous * v_ref[c, x]
        low, high = [
            (smooth(0.25 * w_y, 0) + viscous * v_ref[c, :, y, :], 0.0625 * w_y[0:1], 0.0625 * w_y[nx - 1 : nx])
            for y, w_y in zip((0, ny - 1), y_ends)
        ]
        for ref, flip in zip(y_refs, (even, jnp.logical_not(even))):
            ref[c] = jnp.where(flip, high[0], low[0])
            for side in range(2):
                at = 3 * side + c
                ref[comps, at : at + 1, :] = jnp.where(flip, high[1 + side], low[1 + side])


def forces(samples, acc, slot, drag, table, force_ref):
    relative = [
        samples[c] - jnp.take_along_axis(jnp.broadcast_to(table[c : c + 1], slot.shape), slot, axis=1)
        for c in range(3)
    ]
    square = relative[0] * relative[0] + relative[1] * relative[1] + relative[2] * relative[2]
    speed = drag * jnp.sqrt(square + softening)
    for c in range(3):
        force_ref[c] = speed * relative[c] + acc[c]


def load_kernel(held, count_y, v_any, old_any, cell_any, member_any, drag_any, inertia_any, mv_any, mass_any,
                v_ref, old_ref, drag_ref, inertia_ref, slot_ref, row_ref, depth_ref, key_ref, low_ref, xkey_ref,
                xlow_ref, own_ref, cell_ref, member_ref, mv_ref, mass_ref, sem):
    pairs = [(cell_any, cell_ref), (member_any, member_ref), (mv_any, mv_ref), (mass_any, mass_ref),
             (drag_any, drag_ref), (inertia_any, inertia_ref), (v_any, v_ref), (old_any, old_ref)]
    copies = [pltpu.make_async_copy(a, b, sem.at[k]) for k, (a, b) in enumerate(pairs)]
    for copy in copies:
        copy.start()
    comps, nx, ny, nz = v_ref.shape
    copies[0].wait()
    cell = cell_ref[...]
    row, depth = lax.div(cell, nz), lax.rem(cell, nz)
    row_ref[...] = row
    depth_ref[...] = depth
    x, y = lax.div(row, ny), lax.rem(row, ny)
    ring = 2 * (nx + ny)
    edge = jnp.where(x == 0, 2 * nx + y, jnp.where(x == nx - 1, 2 * nx + ny + y, -1))
    edge = jnp.where(y == 0, x, jnp.where(y == ny - 1, nx + x, edge))
    z = nz * ring // WIDE
    key_ref[...] = jnp.where(edge < 0, -1, lax.div(depth, z) * ring + edge)
    low_ref[...] = lax.rem(depth, z)
    face = jnp.where(x == 0, y, jnp.where(x == nx - 1, ny + y, -1))
    z = nz * 2 * ny // WIDE
    xkey_ref[...] = jnp.where(face < 0, -1, lax.div(depth, z) * (2 * ny) + face)
    xlow_ref[...] = lax.rem(depth, z)
    copies[1].wait()
    member = member_ref[...]
    owner = lax.div(lax.div(member, held), count_y)
    slot_ref[...] = (owner - lax.axis_index("gx") + 1) * held + lax.rem(member, held)
    for copy in copies[2:]:
        copy.wait()
    own_ref[...] = jnp.zeros_like(own_ref)
    own_ref[0:3, 0:held] = mv_ref[...]
    own_ref[3:4, 0:held] = mass_ref[...]


def sample_kernel(v_ref, old_ref, row_ref, depth_ref, inertia_ref, s_ref, acc_ref, table_ref, six_ref):
    comps, nx, ny, nz = v_ref.shape
    fields = [ref[k].reshape(nx * ny, nz) for ref in (v_ref, old_ref) for k in range(comps)]
    gather(fields, table_ref, row_ref, depth_ref, six_ref)
    for c in range(comps):
        s_ref[c] = six_ref[c]
        acc_ref[c] = inertia_ref[...] * (six_ref[c] - six_ref[comps + c])


def first_kernel(held, count_x, v_ref, s_ref, acc_ref, slot_ref, drag_ref, key_ref, low_ref, own_ref, odd_ref,
                 even_ref, force_ref, mtable_ref, spill_ref, ye_ref, yo_ref, total_ref, col_ref, field_ref):
    low, high = beside(even_ref[...], odd_ref[...], lax.axis_index("gx"), count_x)
    table = low + pltpu.roll(own_ref[...], held, axis=1) + pltpu.roll(high, 2 * held, axis=1)
    mtable_ref[...] = table
    forces([s_ref[c] for c in range(3)], [acc_ref[c] for c in range(3)], slot_ref[...], drag_ref[...], table,
           force_ref)
    edges(v_ref, force_ref, key_ref, low_ref, slot_ref, col_ref, field_ref, spill_ref, (ye_ref, yo_ref), total_ref)


def deposit(comps, force_ref, row_ref, depth_ref, col_ref, acc_ref, out_ref):
    rows, nz = out_ref.shape[1:]
    count = len(comps)
    for j in range(row_ref.shape[0] // 2):
        hot = hot_rows(wide_row(row_ref, j), rows)
        hit = hot_rows(wide_row(depth_ref, j), nz) > 0
        for k, c in enumerate(comps):
            for p, piece in enumerate(split(wide_row(force_ref.at[c], j))):
                wide = jnp.broadcast_to(piece, hit.shape)
                at = (p * count + k) * nz
                col_ref[at : at + nz, :] = jnp.where(hit, wide, jnp.zeros_like(wide))
        part = lax.dot_general(hot, col_ref[...], NT, preferred_element_type=f32)
        acc_ref[...] = part if j == 0 else acc_ref[...] + part
    for k in range(count):
        out_ref[k] = -(acc_ref[:, k * nz : (k + 1) * nz] + acc_ref[:, (count + k) * nz : (count + k + 1) * nz])


def deposit_kernel(comps, force_ref, row_ref, depth_ref, total_ref, out_ref, same_ref, col_ref, acc_ref):
    same_ref[...] = total_ref[...]
    deposit(comps, force_ref, row_ref, depth_ref, col_ref, acc_ref, out_ref)


def turn_kernel(count_y, spill_ref, odd_ref, even_ref, total_ref, after_ref, xe_ref, xo_ref):
    comps, ny, nz = spill_ref.shape[1:]
    low, high = beside(even_ref[comps], odd_ref[comps], lax.axis_index("gy"), count_y)
    even = lax.axis_index("gx") % 2 == 0
    ids = lax.broadcasted_iota(i32, (ny, nz), 0)
    for c in range(comps):
        sides = []
        for side in range(2):
            at = 3 * side + c
            face = spill_ref[side, c]
            face = face + jnp.where(ids == 0, low[at : at + 1], 0.0)
            face = face + jnp.where(ids == ny - 1, high[at : at + 1], 0.0)
            sides.append(face)
        xe_ref[c] = jnp.where(even, sides[1], sides[0])
        xo_ref[c] = jnp.where(even, sides[0], sides[1])
    for ref in (xe_ref, xo_ref):
        ref[comps, 0:8, :] = total_ref[...]
        ref[comps, 8:16, :] = jnp.zeros_like(total_ref)


def own_update(c, v_ref, load, l_ref, low, high):
    nx, ny, nz = v_ref.shape[1:]
    v = v_ref[c]
    w = smooth(smooth(smooth(load.reshape(nx, ny, nz), 2), 1), 0)
    beside_all = both(v, 0) + both(v, 1) + both(v, 2)
    l_ref[c] = v + viscous * (beside_all - 6.0 * v) + w
    add_y(c, low, high, l_ref)


def middle_kernel(count_y, v_ref, load_ref, odd_ref, even_ref, row_ref, depth_ref, after_ref, l_ref, s_ref,
                  table_ref):
    comps, nx, ny, nz = v_ref.shape
    low, high = beside(even_ref[...], odd_ref[...], lax.axis_index("gy"), count_y)
    for c in range(comps):
        own_update(c, v_ref, load_ref[c], l_ref, low, high)
    gather([l_ref[k].reshape(nx * ny, nz) for k in range(comps)], table_ref, row_ref, depth_ref, s_ref)


def sum_totals(held, count_x, total, low1, high1, even2, odd2):
    own_x = lax.axis_index("gx")
    even = own_x // 2 % 2 == 0
    low2 = jnp.where(own_x > 1, jnp.where(even, odd2, even2), 0.0)
    high2 = jnp.where(own_x < count_x - 2, jnp.where(even, even2, odd2), 0.0)
    lane = lax.broadcasted_iota(i32, (8, LANES), 1)
    total = total + pltpu.roll(low1, LANES - held, axis=1) + pltpu.roll(high1, held, axis=1)
    total = total + jnp.where(lane < held, pltpu.roll(low2, LANES - 2 * held, axis=1), 0.0)
    return total + jnp.where(lane // held == 2, pltpu.roll(high2, 2 * held, axis=1), 0.0)


def second_kernel(held, count_x, l_ref, sp_ref, xo_ref, xe_ref, s_ref, inertia_ref, slot_ref, drag_ref, key_ref,
                  low_ref, xkey_ref, xlow_ref, old_table_ref, old_total_ref, te_ref, to_ref,
                  v_ref, force_ref, mtable_ref, spill_ref, ye_ref, yo_ref, total_ref,
                  col_ref, field_ref, face_ref, sample_ref):
    comps, nx, ny, nz = l_ref.shape
    low, high = beside(xe_ref[...], xo_ref[...], lax.axis_index("gx"), count_x)
    total = sum_totals(held, count_x, old_total_ref[...], low[comps, 0:8], high[comps, 0:8], te_ref[...], to_ref[...])
    old = old_table_ref[...]
    row = lax.broadcasted_iota(i32, (8, LANES), 0)
    lane = lax.broadcasted_iota(i32, (8, LANES), 1)
    table = jnp.where((row < 3) & (lane < 3 * held), old + old[3:4] * total, old)
    mtable_ref[...] = table
    z = nz * 2 * ny // WIDE
    for c in range(comps):
        turned = jnp.concatenate([low[c], high[c]], axis=0).T
        wide = jnp.concatenate([turned[h * z : (h + 1) * z] for h in range(nz // z)], axis=1)
        face_ref[0, c * z : (c + 1) * z, :], face_ref[1, c * z : (c + 1) * z, :] = split(wide)
    for j in range(xkey_ref.shape[0] // 2):
        hot = hot_rows(wide_row(xkey_ref, j), WIDE)
        product = jnp.dot(face_ref[0], hot, preferred_element_type=f32)
        product = product + jnp.dot(face_ref[1], hot, preferred_element_type=f32)
        for k, found in enumerate(pick(product, wide_row(xlow_ref, j), comps)):
            store_row(sample_ref, k, j, found)
    v_ref[...] = l_ref[...]
    for c in range(comps):
        v_ref[c, 0] += low[c]
        v_ref[c, nx - 1] += high[c]
    samples = [sp_ref[c] + sample_ref[c] for c in range(comps)]
    acc = [inertia_ref[...] * (samples[c] - s_ref[c]) for c in range(comps)]
    forces(samples, acc, slot_ref[...], drag_ref[...], table, force_ref)
    edges(v_ref, force_ref, key_ref, low_ref, slot_ref, col_ref, field_ref, spill_ref, (ye_ref, yo_ref), total_ref)


def finish_kernel(count_y, early, v_ref, load_ref, odd_ref, even_ref, force_ref, row_ref, depth_ref, after_ref,
                  out_hbm, face_ref, l_ref, rest_ref, col_ref, acc_ref, sem):
    comps, nx = v_ref.shape[:2]
    low, high = beside(even_ref[...], odd_ref[...], lax.axis_index("gy"), count_y)
    if early < comps:
        deposit(range(early, comps), force_ref, row_ref, depth_ref, col_ref, acc_ref, rest_ref)
    for c in range(comps):
        load = load_ref[c] if c < early else rest_ref[c - early]
        own_update(c, v_ref, load, l_ref, low, high)
        pltpu.make_async_copy(l_ref.at[c], out_hbm.at[c], sem.at[c]).start()
        face_ref[c, 0] = l_ref[c, 0]
        face_ref[c, 1] = l_ref[c, nx - 1]
    for c in range(comps):
        pltpu.make_async_copy(l_ref.at[c], out_hbm.at[c], sem.at[c]).wait()


def last_kernel(held, count_x, face_ref, xo_ref, xe_ref, mtable_ref, total_ref, old_hbm, m_hbm, v_hbm, new_ref, m_ref, sem):
    comps, nx = v_hbm.shape[:2]
    low, high = beside(xe_ref[...], xo_ref[...], lax.axis_index("gx"), count_x)
    copies = []
    for side, part in enumerate((low, high)):
        for c in range(comps):
            new_ref[side, c] = face_ref[c, side] + part[c]
        copies.append(pltpu.make_async_copy(new_ref.at[side], v_hbm.at[:, side * (nx - 1)], sem.at[side]))
        copies[-1].start()
    total = total_ref[...] + pltpu.roll(low[comps, 0:8], LANES - held, axis=1)
    total = total + pltpu.roll(high[comps, 0:8], held, axis=1)
    table = mtable_ref[...]
    table = table + table[3:4] * total
    m_ref[...] = pltpu.roll(table, LANES - held, axis=1)[0:3, :held]
    copies.append(pltpu.make_async_copy(m_ref, m_hbm, sem.at[2]))
    copies[-1].start()
    for copy in copies:
        copy.wait()


def pairs(axis, stride, odd):
    count_x, count_y = lax.axis_size("gx"), lax.axis_size("gy")
    found = []
    for x in range(count_x):
        for y in range(count_y):
            at, count = (x, count_x) if axis == "gx" else (y, count_y)
            to = ((at + stride) ^ stride) - stride if odd else at ^ stride
            if axis == "gy":
                target = (x, to % count)
            else:
                target = (to, y) if 0 <= to < count else (x, y ^ 1)
            found.append((x * count_y + y, target[0] * count_y + target[1]))
    return found


def exchange(even_msg, odd_msg, axis, stride=1):
    both_axes = ("gx", "gy")
    came_odd = lax.ppermute(odd_msg, both_axes, pairs(axis, stride, True))
    came_even = lax.ppermute(even_msg, both_axes, pairs(axis, stride, False))
    return came_even, came_odd


def per_device(velocity, velocity_old, station_cell, station_member, drag_coef, inertia_coef, member_velocity,
               member_inv_mass):
    count_x, count_y = lax.axis_size("gx"), lax.axis_size("gy")
    held = member_velocity.shape[1]
    grid = velocity.shape
    comps, nx, ny, nz = grid
    rows = nx * ny
    lines = (station_cell.shape[0] // LANES, LANES)
    ints = jax.ShapeDtypeStruct(lines, i32)
    one = real(*lines)
    three = real(3, *lines)
    tile = real(8, LANES)
    face = real(comps + 1, max(nx, ny), nz)
    spill = real(2, comps, ny, nz)
    product = 12 * nz * rows * lines[0] * LANES
    table = pltpu.VMEM((2, comps * nz, rows), bf16)

    (v, old, drag, inertia, slot, row, depth, key, low, xkey, xlow, own) = call(
        "load", functools.partial(load_kernel, held, count_y),
        (velocity, velocity_old, station_cell.reshape(lines), station_member.reshape(lines),
         drag_coef.reshape(lines), inertia_coef.reshape(lines), member_velocity, member_inv_mass.reshape(1, held)),
        [real(*grid)] * 2 + [one] * 2 + [ints] * 7 + [tile],
        [pltpu.VMEM(lines, i32), pltpu.VMEM(lines, i32), pltpu.VMEM((3, held), f32), pltpu.VMEM((1, held), f32),
         pltpu.SemaphoreType.DMA((8,))],
        in_hbm=range(8),
    )
    own_even, own_odd = exchange(own, own, "gx")
    s, acc = call(
        "samples", sample_kernel, (v, old, row, depth, inertia), [three, three],
        [pltpu.VMEM((2, 2 * comps * nz, rows), bf16), pltpu.VMEM((6,) + lines, f32)], flops=2 * product,
    )
    slots = -(-3 * held // 16) * 16
    work = [pltpu.VMEM((WIDE, WIDE), bf16), pltpu.VMEM((WIDE + slots, WIDE), f32)]
    edge_parts = [three, tile, spill, face, face, tile]
    force, mtable, spills, y_even, y_odd, total = call(
        "first_forces", functools.partial(first_kernel, held, count_x),
        (v, s, acc, slot, drag, key, low, own, own_odd, own_even), edge_parts, work, flops=product // 2,
    )

    def dep_scratch(count):
        return [pltpu.VMEM((2 * count * nz, WIDE), bf16), pltpu.VMEM((rows, 2 * count * nz), f32)]

    def spread(force, count, after):
        return call(
            "deposit", functools.partial(deposit_kernel, range(count)), (force, row, depth, after),
            [real(count, rows, nz), tile], dep_scratch(count), flops=product * count // comps,
        )

    def turn(spills, y_even, y_odd, total, after):
        return call(
            "turn", functools.partial(turn_kernel, count_y), (spills, y_odd, y_even, total, after), [face, face]
        )

    y_even, y_odd = exchange(y_even, y_odd, "gy")
    load, total = spread(force, comps, total)
    second_even, second_odd = exchange(total, total, "gx", 2)
    x_even, x_odd = turn(spills, y_even, y_odd, total, load)
    local, samples = call(
        "middle", functools.partial(middle_kernel, count_y), (v, load, y_odd, y_even, row, depth, x_even),
        [real(*grid), three], [table], flops=product,
    )
    x_even, x_odd = exchange(x_even, x_odd, "gx")
    z = nz * 2 * ny // WIDE
    v, force, mtable, spills, y_even, y_odd, total = call(
        "second_forces", functools.partial(second_kernel, held, count_x),
        (local, samples, x_odd, x_even, s, inertia, slot, drag, key, low, xkey, xlow, mtable, total,
         second_even, second_odd),
        [real(*grid)] + edge_parts, work + [pltpu.VMEM((2, comps * z, WIDE), bf16), pltpu.VMEM((3,) + lines, f32)],
        flops=product // 2,
    )
    y_even, y_odd = exchange(y_even, y_odd, "gy")
    load, total = spread(force, 2, total)
    x_even, x_odd = turn(spills, y_even, y_odd, total, load)
    late = max(comps - 2, 1)
    out, faces = call(
        "finish", functools.partial(finish_kernel, count_y, 2),
        (v, load, y_odd, y_even, force, row, depth, x_even),
        [real(*grid), real(comps, 2, ny, nz)],
        [pltpu.VMEM(grid, f32), pltpu.VMEM((late, rows, nz), f32)] + dep_scratch(late)
        + [pltpu.SemaphoreType.DMA((comps,))],
        out_hbm=(0,), flops=product // 3,
    )
    x_even, x_odd = exchange(x_even, x_odd, "gx")
    members, out = call(
        "last", functools.partial(last_kernel, held, count_x), (faces, x_odd, x_even, mtable, total, out),
        [real(3, held), real(*grid)],
        [pltpu.VMEM((2, comps, ny, nz), f32), pltpu.VMEM((3, held), f32), pltpu.SemaphoreType.DMA((3,))],
        in_hbm=(5,), out_hbm=(0, 1), aliases={5: 1},
    )
    return out, members


def solution(mesh):
    return jax.shard_map(
        per_device,
        mesh=mesh,
        in_specs=(
            P(None, "gx", "gy", None),
            P(None, "gx", "gy", None),
            P(("gx", "gy")),
            P(("gx", "gy"), None),
            P(("gx", "gy")),
            P(("gx", "gy")),
            P(None, ("gx", "gy")),
            P(("gx", "gy")),
        ),
        out_specs=(P(None, "gx", "gy", None), P(None, ("gx", "gy"))),
        check_vma=False,
    )
```

```python
import functools

import jax
import jax.numpy as jnp
from jax import lax
from jax.experimental import pallas as pl
from jax.experimental.pallas import tpu as pltpu
from jax.sharding import PartitionSpec as P

LANES = 128
WIDE = 256

viscous = 0.125
softening = 0.01

f32 = jnp.float32
i32 = jnp.int32
bf16 = jnp.bfloat16
HBM = pl.BlockSpec(memory_space=pltpu.HBM)
NT = (((1,), (1,)), ((), ()))


def call(name, body, ins, outs, scratch=(), in_hbm=(), out_hbm=(), flops=0, size=1 << 18, aliases=None):
    whole = pl.BlockSpec(memory_space=pltpu.VMEM)
    ins = [pltpu.with_memory_space_constraint(x, pltpu.HBM) if k in in_hbm else x for k, x in enumerate(ins)]
    outs = [pltpu.HBM(x.shape, x.dtype) if k in out_hbm else x for k, x in enumerate(outs)]
    return pl.pallas_call(
        body,
        name=name,
        out_shape=outs,
        in_specs=[HBM if k in in_hbm else whole for k in range(len(ins))],
        out_specs=[HBM if k in out_hbm else whole for k in range(len(outs))],
        scratch_shapes=list(scratch),
        input_output_aliases=aliases or {},
        compiler_params=pltpu.CompilerParams(vmem_limit_bytes=24 << 20),
        cost_estimate=pl.CostEstimate(flops=flops, bytes_accessed=size, transcendentals=0),
    )(*ins)


def real(*shape):
    return jax.ShapeDtypeStruct(shape, f32)


def split(x):
    top = x.astype(bf16)
    return top, (x - top.astype(f32)).astype(bf16)


def hot_rows(index, count):
    ids = lax.broadcasted_iota(i32, (count, index.shape[1]), 0).astype(f32).astype(bf16)
    wide = jnp.broadcast_to(index.astype(f32).astype(bf16), ids.shape)
    return jnp.where(ids == wide, jnp.ones_like(wide), jnp.zeros_like(wide))


def wide_row(ref, j):
    return jnp.concatenate([ref[2 * j : 2 * j + 1, :], ref[2 * j + 1 : 2 * j + 2, :]], axis=1)


def store_row(ref, k, j, row):
    ref[k, 2 * j : 2 * j + 1, :] = row[:, :LANES]
    ref[k, 2 * j + 1 : 2 * j + 2, :] = row[:, LANES:]


def pick(product, depth_row, count):
    z = product.shape[0] // count
    hit = lax.broadcasted_iota(i32, (z, depth_row.shape[1]), 0) == depth_row
    return [
        jnp.sum(jnp.where(hit, product[k * z : (k + 1) * z], 0.0), axis=0, keepdims=True) for k in range(count)
    ]


def gather(fields, table_ref, row_ref, depth_ref, out_ref):
    rows, z = fields[0].shape
    count = len(fields)
    for k, field in enumerate(fields):
        table_ref[0, k * z : (k + 1) * z, :], table_ref[1, k * z : (k + 1) * z, :] = split(field.T)
    for j in range(row_ref.shape[0] // 2):
        hot = hot_rows(wide_row(row_ref, j), rows)
        product = jnp.dot(table_ref[0], hot, preferred_element_type=f32)
        product = product + jnp.dot(table_ref[1], hot, preferred_element_type=f32)
        for k, row in enumerate(pick(product, wide_row(depth_ref, j), count)):
            store_row(out_ref, k, j, row)


def columns(ref, force_ref, depth_row, z, j, groups):
    hit = hot_rows(depth_row, z) > 0
    for c in range(3):
        for p, piece in enumerate(split(wide_row(force_ref.at[c], j))):
            wide = jnp.broadcast_to(piece, hit.shape)
            at = (p * groups + c) * z
            ref[at : at + z, :] = jnp.where(hit, wide, jnp.zeros_like(wide))


def moved(x, axis, by):
    n = x.shape[axis]
    if axis >= x.ndim - 2:
        ids = lax.broadcasted_iota(i32, x.shape, axis)
        return jnp.where(ids == (0 if by > 0 else n - 1), 0.0, pltpu.roll(x, by % n, axis=axis))
    zero = jnp.zeros_like(lax.slice_in_dim(x, 0, 1, axis=axis))
    if by > 0:
        return jnp.concatenate([zero, lax.slice_in_dim(x, 0, n - 1, axis=axis)], axis=axis)
    return jnp.concatenate([lax.slice_in_dim(x, 1, n, axis=axis), zero], axis=axis)


def both(x, axis):
    return moved(x, axis, 1) + moved(x, axis, -1)


def smooth(x, axis):
    return 0.5 * x + 0.25 * both(x, axis)


def beside(even_msg, odd_msg, own, count):
    even = own % 2 == 0
    low = jnp.where(own > 0, jnp.where(even, odd_msg, even_msg), 0.0)
    high = jnp.where(own < count - 1, jnp.where(even, even_msg, odd_msg), 0.0)
    return low, high


def add_y(c, face_low, face_high, ref):
    ny = ref.shape[2]
    ref[c, :, 0, :] += face_low[c]
    ref[c, :, ny - 1, :] += face_high[c]


def edges(v_ref, force_ref, key_ref, low_ref, slot_ref, col_ref, acc_ref, spill_ref, y_refs, total_ref):
    comps, nx, ny, nz = v_ref.shape
    ring = 2 * (nx + ny)
    parts = WIDE // ring
    z = nz // parts
    slots = acc_ref.shape[0] - WIDE
    free = 3 * z
    for p in range(2):
        col_ref[p * LANES + free : (p + 1) * LANES, :] = jnp.zeros((LANES - free, WIDE), bf16)
    for j in range(key_ref.shape[0] // 2):
        hot = jnp.concatenate([hot_rows(wide_row(key_ref, j), WIDE), hot_rows(wide_row(slot_ref, j), slots)], axis=0)
        columns(col_ref, force_ref, wide_row(low_ref, j), z, j, LANES // z)
        pieces = [split(wide_row(force_ref.at[c], j)) for c in range(3)]
        for p in range(2):
            rows = [piece[p].astype(f32) for piece in pieces] + [jnp.zeros((13, WIDE), f32)]
            col_ref[p * LANES + free : p * LANES + free + 16, :] = jnp.concatenate(rows, axis=0).astype(bf16)
        part = lax.dot_general(hot, col_ref[...], NT, preferred_element_type=f32)
        acc_ref[...] = part if j == 0 else acc_ref[...] + part
    found = acc_ref[:, :LANES] + acc_ref[:, LANES:]
    sums = jnp.concatenate([found[WIDE:], jnp.zeros((LANES - slots, LANES), f32)], axis=0)
    total_ref[...] = sums.T[free : free + 8]
    found = -found[:WIDE]
    lane = lax.broadcasted_iota(i32, (ring, LANES), 1) // z
    yid = lax.broadcasted_iota(i32, (ny, nz), 0)
    even = lax.axis_index("gy") % 2 == 0
    for c in range(comps):
        w = jnp.zeros((ring, nz), f32)
        for h in range(parts):
            block = found[h * ring : (h + 1) * ring]
            by = (h - c) * z % LANES
            block = pltpu.roll(block, by, axis=1) if by else block
            w = jnp.where(lane == h, block, w)
        w = smooth(w, 1)
        y_ends = (w[:nx], w[nx : 2 * nx])
        for side, x in ((0, 0), (1, nx - 1)):
            face = w[2 * nx + side * ny : 2 * nx + (side + 1) * ny]
            face = jnp.where(yid == 0, y_ends[0][x : x + 1], face)
            face = jnp.where(yid == ny - 1, y_ends[1][x : x + 1], face)
            spill_ref[side, c] = 0.25 * smooth(face, 0) + viscous * v_ref[c, x]
        low, high = [
            (smooth(0.25 * w_y, 0) + viscous * v_ref[c, :, y, :], 0.0625 * w_y[0:1], 0.0625 * w_y[nx - 1 : nx])
            for y, w_y in zip((0, ny - 1), y_ends)
        ]
        for ref, flip in zip(y_refs, (even, jnp.logical_not(even))):
            ref[c] = jnp.where(flip, high[0], low[0])
            for side in range(2):
                at = 3 * side + c
                ref[comps, at : at + 1, :] = jnp.where(flip, high[1 + side], low[1 + side])


def forces(samples, acc, slot, drag, table, force_ref):
    relative = [
        samples[c] - jnp.take_along_axis(jnp.broadcast_to(table[c : c + 1], slot.shape), slot, axis=1)
        for c in range(3)
    ]
    square = relative[0] * relative[0] + relative[1] * relative[1] + relative[2] * relative[2]
    speed = drag * jnp.sqrt(square + softening)
    for c in range(3):
        force_ref[c] = speed * relative[c] + acc[c]


def load_kernel(held, count_y, v_any, old_any, cell_any, member_any, drag_any, inertia_any, mv_any, mass_any,
                v_ref, old_ref, drag_ref, inertia_ref, slot_ref, row_ref, depth_ref, key_ref, low_ref, xkey_ref,
                xlow_ref, own_ref, cell_ref, member_ref, mv_ref, mass_ref, sem):
    pairs = [(cell_any, cell_ref), (member_any, member_ref), (mv_any, mv_ref), (mass_any, mass_ref),
             (drag_any, drag_ref), (inertia_any, inertia_ref)]
    for a, b in ((v_any, v_ref), (old_any, old_ref)):
        pairs += [(a.at[c], b.at[c]) for c in range(b.shape[0])]
    copies = [pltpu.make_async_copy(a, b, sem.at[k]) for k, (a, b) in enumerate(pairs)]
    for copy in copies:
        copy.start()
    comps, nx, ny, nz = v_ref.shape
    copies[0].wait()
    cell = cell_ref[...]
    row, depth = lax.div(cell, nz), lax.rem(cell, nz)
    row_ref[...] = row
    depth_ref[...] = depth
    x, y = lax.div(row, ny), lax.rem(row, ny)
    ring = 2 * (nx + ny)
    edge = jnp.where(x == 0, 2 * nx + y, jnp.where(x == nx - 1, 2 * nx + ny + y, -1))
    edge = jnp.where(y == 0, x, jnp.where(y == ny - 1, nx + x, edge))
    z = nz * ring // WIDE
    key_ref[...] = jnp.where(edge < 0, -1, lax.div(depth, z) * ring + edge)
    low_ref[...] = lax.rem(depth, z)
    face = jnp.where(x == 0, y, jnp.where(x == nx - 1, ny + y, -1))
    z = nz * 2 * ny // WIDE
    xkey_ref[...] = jnp.where(face < 0, -1, lax.div(depth, z) * (2 * ny) + face)
    xlow_ref[...] = lax.rem(depth, z)
    copies[1].wait()
    member = member_ref[...]
    owner = lax.div(lax.div(member, held), count_y)
    slot_ref[...] = (owner - lax.axis_index("gx") + 1) * held + lax.rem(member, held)
    for copy in copies[2:]:
        copy.wait()
    own_ref[...] = jnp.zeros_like(own_ref)
    own_ref[0:3, 0:held] = mv_ref[...]
    own_ref[3:4, 0:held] = mass_ref[...]


def sample_kernel(v_ref, old_ref, row_ref, depth_ref, inertia_ref, s_ref, acc_ref, table_ref, six_ref):
    comps, nx, ny, nz = v_ref.shape
    fields = [ref[k].reshape(nx * ny, nz) for ref in (v_ref, old_ref) for k in range(comps)]
    gather(fields, table_ref, row_ref, depth_ref, six_ref)
    for c in range(comps):
        s_ref[c] = six_ref[c]
        acc_ref[c] = inertia_ref[...] * (six_ref[c] - six_ref[comps + c])


def first_kernel(held, count_x, v_ref, s_ref, acc_ref, slot_ref, drag_ref, key_ref, low_ref, own_ref, even_ref,
                 odd_ref, force_ref, mtable_ref, spill_ref, ye_ref, yo_ref, total_ref, col_ref, field_ref):
    low, high = beside(even_ref[...], odd_ref[...], lax.axis_index("gx"), count_x)
    table = low + pltpu.roll(own_ref[...], held, axis=1) + pltpu.roll(high, 2 * held, axis=1)
    mtable_ref[...] = table
    forces([s_ref[c] for c in range(3)], [acc_ref[c] for c in range(3)], slot_ref[...], drag_ref[...], table,
           force_ref)
    edges(v_ref, force_ref, key_ref, low_ref, slot_ref, col_ref, field_ref, spill_ref, (ye_ref, yo_ref), total_ref)
    comps = v_ref.shape[0]
    for ref in (ye_ref, yo_ref):
        ref[comps, 8:16, :] = total_ref[...]


def pair_kernel(total_ref, came_ref, after_ref, out_ref):
    comps = came_ref.shape[0] - 1
    even = lax.axis_index("gy") % 2 == 0
    own, other = total_ref[...], came_ref[comps, 8:16, :]
    out_ref[0:8, :] = jnp.where(even, own, other)
    out_ref[8:16, :] = jnp.where(even, other, own)


def share_kernel(came_ref, after_ref, keep_ref, give_ref):
    even = lax.axis_index("gy") % 2 == 0
    first, second = came_ref[0:8, :], came_ref[8:16, :]
    keep_ref[...] = jnp.where(even, first, second)
    give_ref[...] = jnp.where(even, second, first)


def deposit(comps, force_ref, row_ref, depth_ref, col_ref, acc_ref, out_ref):
    rows, nz = out_ref.shape[1:]
    count = len(comps)
    for j in range(row_ref.shape[0] // 2):
        hot = hot_rows(wide_row(row_ref, j), rows)
        hit = hot_rows(wide_row(depth_ref, j), nz) > 0
        for k, c in enumerate(comps):
            for p, piece in enumerate(split(wide_row(force_ref.at[c], j))):
                wide = jnp.broadcast_to(piece, hit.shape)
                at = (p * count + k) * nz
                col_ref[at : at + nz, :] = jnp.where(hit, wide, jnp.zeros_like(wide))
        part = lax.dot_general(hot, col_ref[...], NT, preferred_element_type=f32)
        acc_ref[...] = part if j == 0 else acc_ref[...] + part
    for k in range(count):
        out_ref[k] = -(acc_ref[:, k * nz : (k + 1) * nz] + acc_ref[:, (count + k) * nz : (count + k + 1) * nz])


def deposit_kernel(comps, force_ref, row_ref, depth_ref, total_ref, out_ref, same_ref, col_ref, acc_ref):
    same_ref[...] = total_ref[...]
    deposit(comps, force_ref, row_ref, depth_ref, col_ref, acc_ref, out_ref)


def turn_kernel(count_y, spill_ref, odd_ref, even_ref, total_ref, after_ref, xe_ref, xo_ref):
    comps, ny, nz = spill_ref.shape[1:]
    low, high = beside(even_ref[comps], odd_ref[comps], lax.axis_index("gy"), count_y)
    even = lax.axis_index("gx") % 2 == 0
    ids = lax.broadcasted_iota(i32, (ny, nz), 0)
    for c in range(comps):
        sides = []
        for side in range(2):
            at = 3 * side + c
            face = spill_ref[side, c]
            face = face + jnp.where(ids == 0, low[at : at + 1], 0.0)
            face = face + jnp.where(ids == ny - 1, high[at : at + 1], 0.0)
            sides.append(face)
        xe_ref[c] = jnp.where(even, sides[1], sides[0])
        xo_ref[c] = jnp.where(even, sides[0], sides[1])
    for ref in (xe_ref, xo_ref):
        ref[comps, 0:8, :] = total_ref[...]
        ref[comps, 8:16, :] = jnp.zeros_like(total_ref)


def own_update(c, v_ref, load, l_ref, low, high):
    nx, ny, nz = v_ref.shape[1:]
    v = v_ref[c]
    w = smooth(smooth(smooth(load.reshape(nx, ny, nz), 2), 1), 0)
    beside_all = both(v, 0) + both(v, 1) + both(v, 2)
    l_ref[c] = v + viscous * (beside_all - 6.0 * v) + w
    add_y(c, low, high, l_ref)


def middle_kernel(count_y, v_ref, load_ref, odd_ref, even_ref, row_ref, depth_ref, after_ref, l_ref, s_ref,
                  table_ref):
    comps, nx, ny, nz = v_ref.shape
    low, high = beside(even_ref[...], odd_ref[...], lax.axis_index("gy"), count_y)
    for c in range(comps):
        own_update(c, v_ref, load_ref[c], l_ref, low, high)
    gather([l_ref[k].reshape(nx * ny, nz) for k in range(comps)], table_ref, row_ref, depth_ref, s_ref)


def sum_totals(held, count_x, total, low1, high1, kept, shared):
    own_x = lax.axis_index("gx")
    even = lax.axis_index("gy") % 2 == 0
    low2 = jnp.where(own_x > 1, jnp.where(even, kept, shared), 0.0)
    high2 = jnp.where(own_x < count_x - 2, jnp.where(even, shared, kept), 0.0)
    lane = lax.broadcasted_iota(i32, (8, LANES), 1)
    total = total + pltpu.roll(low1, LANES - held, axis=1) + pltpu.roll(high1, held, axis=1)
    total = total + jnp.where(lane < held, pltpu.roll(low2, LANES - 2 * held, axis=1), 0.0)
    return total + jnp.where(lane // held == 2, pltpu.roll(high2, 2 * held, axis=1), 0.0)


def second_kernel(held, count_x, l_ref, sp_ref, xo_ref, xe_ref, s_ref, inertia_ref, slot_ref, drag_ref, key_ref,
                  low_ref, xkey_ref, xlow_ref, old_table_ref, old_total_ref, te_ref, to_ref,
                  v_ref, force_ref, mtable_ref, spill_ref, ye_ref, yo_ref, total_ref,
                  col_ref, field_ref, face_ref, sample_ref):
    comps, nx, ny, nz = l_ref.shape
    low, high = beside(xe_ref[...], xo_ref[...], lax.axis_index("gx"), count_x)
    total = sum_totals(held, count_x, old_total_ref[...], low[comps, 0:8], high[comps, 0:8], te_ref[...], to_ref[...])
    old = old_table_ref[...]
    row = lax.broadcasted_iota(i32, (8, LANES), 0)
    lane = lax.broadcasted_iota(i32, (8, LANES), 1)
    table = jnp.where((row < 3) & (lane < 3 * held), old + old[3:4] * total, old)
    mtable_ref[...] = table
    z = nz * 2 * ny // WIDE
    for c in range(comps):
        turned = jnp.concatenate([low[c], high[c]], axis=0).T
        wide = jnp.concatenate([turned[h * z : (h + 1) * z] for h in range(nz // z)], axis=1)
        at = comps * z + c * z
        face_ref[c * z : (c + 1) * z, :], face_ref[at : at + z, :] = split(wide)
    for j in range(xkey_ref.shape[0] // 2):
        hot = hot_rows(wide_row(xkey_ref, j), WIDE)
        product = jnp.dot(face_ref[...], hot, preferred_element_type=f32)
        product = product[: comps * z] + product[comps * z :]
        for k, found in enumerate(pick(product, wide_row(xlow_ref, j), comps)):
            store_row(sample_ref, k, j, found)
    for c in range(comps):
        v_ref[c, 0] = l_ref[c, 0] + low[c]
        v_ref[c, nx - 1] = l_ref[c, nx - 1] + high[c]
    samples = [sp_ref[c] + sample_ref[c] for c in range(comps)]
    acc = [inertia_ref[...] * (samples[c] - s_ref[c]) for c in range(comps)]
    forces(samples, acc, slot_ref[...], drag_ref[...], table, force_ref)
    edges(v_ref, force_ref, key_ref, low_ref, slot_ref, col_ref, field_ref, spill_ref, (ye_ref, yo_ref), total_ref)


def finish_kernel(count_y, early, v_ref, load_ref, odd_ref, even_ref, force_ref, row_ref, depth_ref, after_ref,
                  out_hbm, face_ref, l_ref, rest_ref, col_ref, acc_ref, sem):
    comps, nx = v_ref.shape[:2]
    low, high = beside(even_ref[...], odd_ref[...], lax.axis_index("gy"), count_y)
    if early < comps:
        deposit(range(early, comps), force_ref, row_ref, depth_ref, col_ref, acc_ref, rest_ref)
    for c in range(comps):
        load = load_ref[c] if c < early else rest_ref[c - early]
        own_update(c, v_ref, load, l_ref, low, high)
        pltpu.make_async_copy(l_ref.at[c], out_hbm.at[c], sem.at[c]).start()
        face_ref[c, 0] = l_ref[c, 0]
        face_ref[c, 1] = l_ref[c, nx - 1]
    for c in range(comps):
        pltpu.make_async_copy(l_ref.at[c], out_hbm.at[c], sem.at[c]).wait()


def last_kernel(held, count_x, face_ref, xo_ref, xe_ref, mtable_ref, total_ref, old_hbm, m_hbm, v_hbm, new_ref, m_ref, sem):
    comps, nx = v_hbm.shape[:2]
    low, high = beside(xe_ref[...], xo_ref[...], lax.axis_index("gx"), count_x)
    copies = []
    for side, part in enumerate((low, high)):
        for c in range(comps):
            new_ref[side, c] = face_ref[c, side] + part[c]
        copies.append(pltpu.make_async_copy(new_ref.at[side], v_hbm.at[:, side * (nx - 1)], sem.at[side]))
        copies[-1].start()
    total = total_ref[...] + pltpu.roll(low[comps, 0:8], LANES - held, axis=1)
    total = total + pltpu.roll(high[comps, 0:8], held, axis=1)
    table = mtable_ref[...]
    table = table + table[3:4] * total
    m_ref[...] = pltpu.roll(table, LANES - held, axis=1)[0:3, :held]
    copies.append(pltpu.make_async_copy(m_ref, m_hbm, sem.at[2]))
    copies[-1].start()
    for copy in copies:
        copy.wait()


def near_pairs(axis, odd):
    count_x, count_y = lax.axis_size("gx"), lax.axis_size("gy")
    found = []
    for x in range(count_x):
        for y in range(count_y):
            at, count = (x, count_x) if axis == "gx" else (y, count_y)
            to = ((at + 1) ^ 1) - 1 if odd else at ^ 1
            if axis == "gy":
                target = (x, to % count)
            else:
                target = (to, y) if 0 <= to < count else (x, y ^ 1)
            found.append((x * count_y + y, target[0] * count_y + target[1]))
    return found


def cross_pairs():
    count_x, count_y = lax.axis_size("gx"), lax.axis_size("gy")
    found = []
    for x in range(count_x):
        for y in range(count_y):
            to = x - 2 if y % 2 == 0 else x + 2
            target = (to, y ^ 1) if 0 <= to < count_x else (x ^ 1, y)
            found.append((x * count_y + y, target[0] * count_y + target[1]))
    return found


def exchange(even_msg, odd_msg, axis):
    both_axes = ("gx", "gy")
    came_odd = lax.ppermute(odd_msg, both_axes, near_pairs(axis, True))
    came_even = lax.ppermute(even_msg, both_axes, near_pairs(axis, False))
    return came_even, came_odd


def per_device(velocity, velocity_old, station_cell, station_member, drag_coef, inertia_coef, member_velocity,
               member_inv_mass):
    count_x, count_y = lax.axis_size("gx"), lax.axis_size("gy")
    held = member_velocity.shape[1]
    grid = velocity.shape
    comps, nx, ny, nz = grid
    rows = nx * ny
    lines = (station_cell.shape[0] // LANES, LANES)
    ints = jax.ShapeDtypeStruct(lines, i32)
    one = real(*lines)
    three = real(3, *lines)
    tile = real(8, LANES)
    face = real(comps + 1, max(nx, ny), nz)
    spill = real(2, comps, ny, nz)
    product = 12 * nz * rows * lines[0] * LANES
    table = pltpu.VMEM((2, comps * nz, rows), bf16)

    (v, old, drag, inertia, slot, row, depth, key, low, xkey, xlow, own) = call(
        "load", functools.partial(load_kernel, held, count_y),
        (velocity, velocity_old, station_cell.reshape(lines), station_member.reshape(lines),
         drag_coef.reshape(lines), inertia_coef.reshape(lines), member_velocity, member_inv_mass.reshape(1, held)),
        [real(*grid)] * 2 + [one] * 2 + [ints] * 7 + [tile],
        [pltpu.VMEM(lines, i32), pltpu.VMEM(lines, i32), pltpu.VMEM((3, held), f32), pltpu.VMEM((1, held), f32),
         pltpu.SemaphoreType.DMA((6 + 2 * comps,))],
        in_hbm=range(8),
    )
    own_even, own_odd = exchange(own, own, "gx")
    s, acc = call(
        "samples", sample_kernel, (v, old, row, depth, inertia), [three, three],
        [pltpu.VMEM((2, 2 * comps * nz, rows), bf16), pltpu.VMEM((6,) + lines, f32)], flops=2 * product,
    )
    slots = -(-3 * held // 16) * 16
    work = [pltpu.VMEM((WIDE, WIDE), bf16), pltpu.VMEM((WIDE + slots, WIDE), f32)]
    edge_parts = [three, tile, spill, face, face, tile]
    force, mtable, spills, y_even, y_odd, total = call(
        "first_forces", functools.partial(first_kernel, held, count_x),
        (v, s, acc, slot, drag, key, low, own, own_even, own_odd), edge_parts, work, flops=product // 2,
    )

    def dep_scratch(count):
        return [pltpu.VMEM((2 * count * nz, WIDE), bf16), pltpu.VMEM((rows, 2 * count * nz), f32)]

    def spread(force, count, after):
        return call(
            "deposit", functools.partial(deposit_kernel, range(count)), (force, row, depth, after),
            [real(count, rows, nz), tile], dep_scratch(count), flops=product * count // comps,
        )

    def turn(spills, y_even, y_odd, total, after):
        return call(
            "turn", functools.partial(turn_kernel, count_y), (spills, y_odd, y_even, total, after), [face, face]
        )

    y_even, y_odd = exchange(y_even, y_odd, "gy")
    load, total = spread(force, comps, total)
    (sums,) = call("pair", pair_kernel, (total, y_even, load), [real(16, LANES)])
    sums = lax.ppermute(sums, ("gx", "gy"), cross_pairs())
    x_even, x_odd = turn(spills, y_even, y_odd, total, load)
    kept, given = call("share", share_kernel, (sums, x_even), [tile, tile])
    shared = lax.ppermute(given, ("gx", "gy"), near_pairs("gy", False))
    local, samples = call(
        "middle", functools.partial(middle_kernel, count_y), (v, load, y_odd, y_even, row, depth, kept),
        [real(*grid), three], [table], flops=product,
    )
    x_even, x_odd = exchange(x_even, x_odd, "gx")
    z = nz * 2 * ny // WIDE
    v, force, mtable, spills, y_even, y_odd, total = call(
        "second_forces", functools.partial(second_kernel, held, count_x),
        (local, samples, x_odd, x_even, s, inertia, slot, drag, key, low, xkey, xlow, mtable, total,
         kept, shared),
        [real(*grid)] + edge_parts, work + [pltpu.VMEM((2 * comps * z, WIDE), bf16), pltpu.VMEM((3,) + lines, f32)],
        flops=product // 2, aliases={0: 0},
    )
    y_even, y_odd = exchange(y_even, y_odd, "gy")
    load, total = spread(force, 2, total)
    x_even, x_odd = turn(spills, y_even, y_odd, total, load)
    late = max(comps - 2, 1)
    out, faces = call(
        "finish", functools.partial(finish_kernel, count_y, 2),
        (v, load, y_odd, y_even, force, row, depth, x_even),
        [real(*grid), real(comps, 2, ny, nz)],
        [pltpu.VMEM(grid, f32), pltpu.VMEM((late, rows, nz), f32)] + dep_scratch(late)
        + [pltpu.SemaphoreType.DMA((comps,))],
        out_hbm=(0,), flops=product // 3,
    )
    x_even, x_odd = exchange(x_even, x_odd, "gx")
    members, out = call(
        "last", functools.partial(last_kernel, held, count_x), (faces, x_odd, x_even, mtable, total, out),
        [real(3, held), real(*grid)],
        [pltpu.VMEM((2, comps, ny, nz), f32), pltpu.VMEM((3, held), f32), pltpu.SemaphoreType.DMA((3,))],
        in_hbm=(5,), out_hbm=(0, 1), aliases={5: 1},
    )
    return out, members


def solution(mesh):
    return jax.shard_map(
        per_device,
        mesh=mesh,
        in_specs=(
            P(None, "gx", "gy", None),
            P(None, "gx", "gy", None),
            P(("gx", "gy")),
            P(("gx", "gy"), None),
            P(("gx", "gy")),
            P(("gx", "gy")),
            P(None, ("gx", "gy")),
            P(("gx", "gy")),
        ),
        out_specs=(P(None, "gx", "gy", None), P(None, ("gx", "gy"))),
        check_vma=False,
    )
```

```python
import functools

import jax
import jax.numpy as jnp
from jax import lax
from jax.experimental import pallas as pl
from jax.experimental.pallas import tpu as pltpu
from jax.sharding import PartitionSpec as P

LANES = 128
WIDE = 256
FACE_ROWS = 32

viscous = 0.125
softening = 0.01

f32 = jnp.float32
i32 = jnp.int32
bf16 = jnp.bfloat16
HBM = pl.BlockSpec(memory_space=pltpu.HBM)
NT = (((1,), (1,)), ((), ()))


def call(name, body, ins, outs, scratch=(), in_hbm=(), out_hbm=(), flops=0, size=1 << 18, aliases=None):
    whole = pl.BlockSpec(memory_space=pltpu.VMEM)
    ins = [pltpu.with_memory_space_constraint(x, pltpu.HBM) if k in in_hbm else x for k, x in enumerate(ins)]
    outs = [pltpu.HBM(x.shape, x.dtype) if k in out_hbm else x for k, x in enumerate(outs)]
    return pl.pallas_call(
        body,
        name=name,
        out_shape=outs,
        in_specs=[HBM if k in in_hbm else whole for k in range(len(ins))],
        out_specs=[HBM if k in out_hbm else whole for k in range(len(outs))],
        scratch_shapes=list(scratch),
        input_output_aliases=aliases or {},
        compiler_params=pltpu.CompilerParams(vmem_limit_bytes=24 << 20),
        cost_estimate=pl.CostEstimate(flops=flops, bytes_accessed=size, transcendentals=0),
    )(*ins)


def real(*shape):
    return jax.ShapeDtypeStruct(shape, f32)


def split(x):
    top = x.astype(bf16)
    return top, (x - top.astype(f32)).astype(bf16)


def hot_rows(index, count):
    ids = lax.broadcasted_iota(i32, (count, index.shape[1]), 0).astype(f32).astype(bf16)
    wide = jnp.broadcast_to(index.astype(f32).astype(bf16), ids.shape)
    return jnp.where(ids == wide, jnp.ones_like(wide), jnp.zeros_like(wide))


def wide_row(ref, j):
    return jnp.concatenate([ref[2 * j : 2 * j + 1, :], ref[2 * j + 1 : 2 * j + 2, :]], axis=1)


def store_row(ref, k, j, row):
    ref[k, 2 * j : 2 * j + 1, :] = row[:, :LANES]
    ref[k, 2 * j + 1 : 2 * j + 2, :] = row[:, LANES:]


def pick(product, depth_row, count):
    z = product.shape[0] // count
    hit = lax.broadcasted_iota(i32, (z, depth_row.shape[1]), 0) == depth_row
    return [
        jnp.sum(jnp.where(hit, product[k * z : (k + 1) * z], 0.0), axis=0, keepdims=True) for k in range(count)
    ]


def gather(fields, table_ref, row_ref, depth_ref, out_ref):
    rows, z = fields[0].shape
    count = len(fields)
    for k, field in enumerate(fields):
        table_ref[0, k * z : (k + 1) * z, :], table_ref[1, k * z : (k + 1) * z, :] = split(field.T)
    for j in range(row_ref.shape[0] // 2):
        hot = hot_rows(wide_row(row_ref, j), rows)
        hit = lax.broadcasted_iota(i32, (z, WIDE), 0) == wide_row(depth_ref, j)
        for k in range(count):
            part = slice(k * z, (k + 1) * z)
            product = jnp.dot(table_ref[0, part], hot, preferred_element_type=f32)
            product = product + jnp.dot(table_ref[1, part], hot, preferred_element_type=f32)
            store_row(out_ref, k, j, jnp.sum(jnp.where(hit, product, 0.0), axis=0, keepdims=True))


def columns(ref, force_ref, depth_row, z, j, groups):
    hit = hot_rows(depth_row, z) > 0
    for c in range(3):
        for p, piece in enumerate(split(wide_row(force_ref.at[c], j))):
            wide = jnp.broadcast_to(piece, hit.shape)
            at = (p * groups + c) * z
            ref[at : at + z, :] = jnp.where(hit, wide, jnp.zeros_like(wide))


def moved(x, axis, by):
    n = x.shape[axis]
    if axis >= x.ndim - 2:
        ids = lax.broadcasted_iota(i32, x.shape, axis)
        return jnp.where(ids == (0 if by > 0 else n - 1), 0.0, pltpu.roll(x, by % n, axis=axis))
    zero = jnp.zeros_like(lax.slice_in_dim(x, 0, 1, axis=axis))
    if by > 0:
        return jnp.concatenate([zero, lax.slice_in_dim(x, 0, n - 1, axis=axis)], axis=axis)
    return jnp.concatenate([lax.slice_in_dim(x, 1, n, axis=axis), zero], axis=axis)


def both(x, axis):
    return moved(x, axis, 1) + moved(x, axis, -1)


def smooth(x, axis):
    return 0.5 * x + 0.25 * both(x, axis)


def beside(even_msg, odd_msg, own, count):
    even = own % 2 == 0
    low = jnp.where(own > 0, jnp.where(even, odd_msg, even_msg), 0.0)
    high = jnp.where(own < count - 1, jnp.where(even, even_msg, odd_msg), 0.0)
    return low, high


def add_y(c, face_low, face_high, ref):
    ny = ref.shape[2]
    ref[c, :, 0, :] += face_low[c]
    ref[c, :, ny - 1, :] += face_high[c]


def edges(v_ref, force_ref, key_ref, low_ref, slot_ref, col_ref, acc_ref, spill_ref, y_refs, total_ref):
    comps, nx, ny, nz = v_ref.shape
    ring = 2 * (nx + ny)
    parts = WIDE // ring
    z = nz // parts
    slots = acc_ref.shape[0] - WIDE
    free = 3 * z
    for p in range(2):
        col_ref[p * LANES + free : (p + 1) * LANES, :] = jnp.zeros((LANES - free, WIDE), bf16)
    for j in range(key_ref.shape[0] // 2):
        hot = jnp.concatenate([hot_rows(wide_row(key_ref, j), WIDE), hot_rows(wide_row(slot_ref, j), slots)], axis=0)
        columns(col_ref, force_ref, wide_row(low_ref, j), z, j, LANES // z)
        pieces = [split(wide_row(force_ref.at[c], j)) for c in range(3)]
        for p in range(2):
            rows = [piece[p].astype(f32) for piece in pieces] + [jnp.zeros((13, WIDE), f32)]
            col_ref[p * LANES + free : p * LANES + free + 16, :] = jnp.concatenate(rows, axis=0).astype(bf16)
        part = lax.dot_general(hot, col_ref[...], NT, preferred_element_type=f32)
        acc_ref[...] = part if j == 0 else acc_ref[...] + part
    found = acc_ref[:, :LANES] + acc_ref[:, LANES:]
    sums = jnp.concatenate([found[WIDE:], jnp.zeros((LANES - slots, LANES), f32)], axis=0)
    total_ref[...] = sums.T[free : free + 8]
    found = -found[:WIDE]
    lane = lax.broadcasted_iota(i32, (ring, LANES), 1) // z
    yid = lax.broadcasted_iota(i32, (ny, nz), 0)
    for c in range(comps):
        w = jnp.zeros((ring, nz), f32)
        for h in range(parts):
            block = found[h * ring : (h + 1) * ring]
            by = (h - c) * z % LANES
            block = pltpu.roll(block, by, axis=1) if by else block
            w = jnp.where(lane == h, block, w)
        w = smooth(w, 1)
        y_ends = (w[:nx], w[nx : 2 * nx])
        for side, x in ((0, 0), (1, nx - 1)):
            face = w[2 * nx + side * ny : 2 * nx + (side + 1) * ny]
            face = jnp.where(yid == 0, y_ends[0][x : x + 1], face)
            face = jnp.where(yid == ny - 1, y_ends[1][x : x + 1], face)
            spill_ref[side, c] = 0.25 * smooth(face, 0) + viscous * v_ref[c, x]
        y_messages(v_ref, c, y_ends, y_refs)


def faces_of(key_ref, low_ref, slot_ref, force_ref, col_ref, acc_ref, nz):
    parts = LANES // FACE_ROWS
    z = nz // parts
    free = 3 * z
    slots = acc_ref.shape[0] - LANES
    for p in range(2):
        col_ref[p * LANES + free : (p + 1) * LANES, :] = jnp.zeros((LANES - free, WIDE), bf16)
    for j in range(key_ref.shape[0] // 2):
        hot = hot_rows(wide_row(key_ref, j), LANES)
        columns(col_ref, force_ref, wide_row(low_ref, j), z, j, LANES // z)
        if slot_ref is not None:
            hot = jnp.concatenate([hot, hot_rows(wide_row(slot_ref, j), slots)], axis=0)
            pieces = [split(wide_row(force_ref.at[c], j)) for c in range(3)]
            for p in range(2):
                rows = [piece[p].astype(f32) for piece in pieces] + [jnp.zeros((13, WIDE), f32)]
                col_ref[p * LANES + free : p * LANES + free + 16, :] = jnp.concatenate(rows, axis=0).astype(bf16)
        part = lax.dot_general(hot, col_ref[...], NT, preferred_element_type=f32)
        acc_ref[...] = part if j == 0 else acc_ref[...] + part
    found = acc_ref[:, :LANES] + acc_ref[:, LANES:]
    total = None
    if slot_ref is not None:
        sums = jnp.concatenate([found[LANES:], jnp.zeros((LANES - slots, LANES), f32)], axis=0)
        total = sums.T[free : free + 8]
    lane = lax.broadcasted_iota(i32, (FACE_ROWS, LANES), 1) // z
    fields = []
    for c in range(3):
        w = jnp.zeros((FACE_ROWS, nz), f32)
        for h in range(parts):
            block = -found[h * FACE_ROWS : (h + 1) * FACE_ROWS]
            by = (h - c) * z % LANES
            block = pltpu.roll(block, by, axis=1) if by else block
            w = jnp.where(lane == h, block, w)
        fields.append(smooth(w, 1))
    return fields, total


def y_messages(v_ref, c, y_ends, y_refs):
    comps, nx, ny, nz = v_ref.shape
    even = lax.axis_index("gy") % 2 == 0
    low, high = [
        (smooth(0.25 * w_y, 0) + viscous * v_ref[c, :, y, :], 0.0625 * w_y[0:1], 0.0625 * w_y[nx - 1 : nx])
        for y, w_y in zip((0, ny - 1), y_ends)
    ]
    for ref, flip in zip(y_refs, (even, jnp.logical_not(even))):
        ref[c] = jnp.where(flip, high[0], low[0])
        for side in range(2):
            at = 3 * side + c
            ref[comps, at : at + 1, :] = jnp.where(flip, high[1 + side], low[1 + side])


def spill_kernel(v_ref, force_ref, key_ref, low_ref, slot_ref, spill_ref, total_ref, col_ref, acc_ref):
    comps, nx, ny, nz = v_ref.shape
    fields, total = faces_of(key_ref, low_ref, slot_ref, force_ref, col_ref, acc_ref, nz)
    total_ref[...] = total
    for c in range(comps):
        for side, x in ((0, 0), (1, nx - 1)):
            face = fields[c][side * ny : (side + 1) * ny]
            spill_ref[side, c] = 0.25 * smooth(face, 0) + viscous * v_ref[c, x]


def forces(samples, acc, slot, drag, table, force_ref):
    relative = [
        samples[c] - jnp.take_along_axis(jnp.broadcast_to(table[c : c + 1], slot.shape), slot, axis=1)
        for c in range(3)
    ]
    square = relative[0] * relative[0] + relative[1] * relative[1] + relative[2] * relative[2]
    speed = drag * jnp.sqrt(square + softening)
    for c in range(3):
        force_ref[c] = speed * relative[c] + acc[c]


def load_kernel(held, count_y, v_any, old_any, cell_any, member_any, drag_any, inertia_any, mv_any, mass_any,
                v_ref, old_ref, drag_ref, inertia_ref, slot_ref, row_ref, depth_ref, key_ref, low_ref, xkey_ref,
                xface_ref, yface_ref, xlow_ref, own_ref, cell_ref, member_ref, mv_ref, mass_ref, sem):
    pairs = [(cell_any, cell_ref), (member_any, member_ref), (mv_any, mv_ref), (mass_any, mass_ref),
             (drag_any, drag_ref), (inertia_any, inertia_ref), (v_any, v_ref), (old_any, old_ref)]
    copies = [pltpu.make_async_copy(a, b, sem.at[k]) for k, (a, b) in enumerate(pairs)]
    for copy in copies:
        copy.start()
    comps, nx, ny, nz = v_ref.shape
    copies[0].wait()
    cell = cell_ref[...]
    row, depth = lax.div(cell, nz), lax.rem(cell, nz)
    row_ref[...] = row
    depth_ref[...] = depth
    x, y = lax.div(row, ny), lax.rem(row, ny)
    ring = 2 * (nx + ny)
    edge = jnp.where(x == 0, 2 * nx + y, jnp.where(x == nx - 1, 2 * nx + ny + y, -1))
    edge = jnp.where(y == 0, x, jnp.where(y == ny - 1, nx + x, edge))
    z = nz * ring // WIDE
    key_ref[...] = jnp.where(edge < 0, -1, lax.div(depth, z) * ring + edge)
    low_ref[...] = lax.rem(depth, z)
    part = lax.div(depth, nz // (LANES // FACE_ROWS)) * FACE_ROWS
    face = jnp.where(y == 0, x, jnp.where(y == ny - 1, nx + x, -1))
    yface_ref[...] = jnp.where(face < 0, -1, part + face)
    face = jnp.where(x == 0, y, jnp.where(x == nx - 1, ny + y, -1))
    xface_ref[...] = jnp.where(face < 0, -1, part + face)
    z = nz * 2 * ny // WIDE
    xkey_ref[...] = jnp.where(face < 0, -1, lax.div(depth, z) * (2 * ny) + face)
    xlow_ref[...] = lax.rem(depth, z)
    copies[1].wait()
    member = member_ref[...]
    owner = lax.div(lax.div(member, held), count_y)
    slot_ref[...] = (owner - lax.axis_index("gx") + 1) * held + lax.rem(member, held)
    for copy in copies[2:]:
        copy.wait()
    own_ref[...] = jnp.zeros_like(own_ref)
    own_ref[0:3, 0:held] = mv_ref[...]
    own_ref[3:4, 0:held] = mass_ref[...]


def sample_kernel(v_ref, old_ref, row_ref, depth_ref, inertia_ref, s_ref, acc_ref, table_ref, six_ref):
    comps, nx, ny, nz = v_ref.shape
    fields = [ref[k].reshape(nx * ny, nz) for ref in (v_ref, old_ref) for k in range(comps)]
    gather(fields, table_ref, row_ref, depth_ref, six_ref)
    for c in range(comps):
        s_ref[c] = six_ref[c]
        acc_ref[c] = inertia_ref[...] * (six_ref[c] - six_ref[comps + c])


def first_kernel(held, count_x, v_ref, s_ref, acc_ref, slot_ref, drag_ref, key_ref, low_ref, own_ref, even_ref,
                 odd_ref, force_ref, mtable_ref, spill_ref, ye_ref, yo_ref, total_ref, col_ref, field_ref):
    low, high = beside(even_ref[...], odd_ref[...], lax.axis_index("gx"), count_x)
    table = low + pltpu.roll(own_ref[...], held, axis=1) + pltpu.roll(high, 2 * held, axis=1)
    mtable_ref[...] = table
    forces([s_ref[c] for c in range(3)], [acc_ref[c] for c in range(3)], slot_ref[...], drag_ref[...], table,
           force_ref)
    edges(v_ref, force_ref, key_ref, low_ref, slot_ref, col_ref, field_ref, spill_ref, (ye_ref, yo_ref), total_ref)
    comps = v_ref.shape[0]
    for ref in (ye_ref, yo_ref):
        ref[comps, 8:16, :] = total_ref[...]


def pair_kernel(total_ref, came_ref, after_ref, out_ref):
    comps = came_ref.shape[0] - 1
    even = lax.axis_index("gy") % 2 == 0
    own, other = total_ref[...], came_ref[comps, 8:16, :]
    out_ref[0:8, :] = jnp.where(even, own, other)
    out_ref[8:16, :] = jnp.where(even, other, own)


def share_kernel(came_ref, after_ref, keep_ref, give_ref):
    even = lax.axis_index("gy") % 2 == 0
    first, second = came_ref[0:8, :], came_ref[8:16, :]
    keep_ref[...] = jnp.where(even, first, second)
    give_ref[...] = jnp.where(even, second, first)


def deposit(comps, force_ref, row_ref, depth_ref, col_ref, acc_ref, out_ref):
    rows, nz = out_ref.shape[1:]
    count = len(comps)
    for j in range(row_ref.shape[0] // 2):
        hot = hot_rows(wide_row(row_ref, j), rows)
        hit = hot_rows(wide_row(depth_ref, j), nz) > 0
        for k, c in enumerate(comps):
            for p, piece in enumerate(split(wide_row(force_ref.at[c], j))):
                wide = jnp.broadcast_to(piece, hit.shape)
                at = (p * count + k) * nz
                col_ref[at : at + nz, :] = jnp.where(hit, wide, jnp.zeros_like(wide))
        part = lax.dot_general(hot, col_ref[...], NT, preferred_element_type=f32)
        acc_ref[...] = part if j == 0 else acc_ref[...] + part
    for k in range(count):
        out_ref[k] = -(acc_ref[:, k * nz : (k + 1) * nz] + acc_ref[:, (count + k) * nz : (count + k + 1) * nz])


def deposit_kernel(comps, force_ref, row_ref, depth_ref, total_ref, out_ref, same_ref, col_ref, acc_ref):
    same_ref[...] = total_ref[...]
    deposit(comps, force_ref, row_ref, depth_ref, col_ref, acc_ref, out_ref)


def turn_kernel(count_y, spill_ref, odd_ref, even_ref, total_ref, after_ref, xe_ref, xo_ref):
    comps, ny, nz = spill_ref.shape[1:]
    low, high = beside(even_ref[comps], odd_ref[comps], lax.axis_index("gy"), count_y)
    even = lax.axis_index("gx") % 2 == 0
    ids = lax.broadcasted_iota(i32, (ny, nz), 0)
    for c in range(comps):
        sides = []
        for side in range(2):
            at = 3 * side + c
            face = spill_ref[side, c]
            face = face + jnp.where(ids == 0, low[at : at + 1], 0.0)
            face = face + jnp.where(ids == ny - 1, high[at : at + 1], 0.0)
            sides.append(face)
        xe_ref[c] = jnp.where(even, sides[1], sides[0])
        xo_ref[c] = jnp.where(even, sides[0], sides[1])
    for ref in (xe_ref, xo_ref):
        ref[comps, 0:8, :] = total_ref[...]
        ref[comps, 8:16, :] = jnp.zeros_like(total_ref)


def own_update(c, v_ref, load, l_ref, low, high):
    nx, ny, nz = v_ref.shape[1:]
    v = v_ref[c]
    w = smooth(smooth(smooth(load.reshape(nx, ny, nz), 2), 1), 0)
    beside_all = both(v, 0) + both(v, 1) + both(v, 2)
    l_ref[c] = v + viscous * (beside_all - 6.0 * v) + w
    add_y(c, low, high, l_ref)


def middle_kernel(count_y, v_ref, load_ref, odd_ref, even_ref, row_ref, depth_ref, after_ref, l_ref, s_ref,
                  table_ref):
    comps, nx, ny, nz = v_ref.shape
    low, high = beside(even_ref[...], odd_ref[...], lax.axis_index("gy"), count_y)
    for c in range(comps):
        own_update(c, v_ref, load_ref[c], l_ref, low, high)
    gather([l_ref[k].reshape(nx * ny, nz) for k in range(comps)], table_ref, row_ref, depth_ref, s_ref)


def sum_totals(held, count_x, total, low1, high1, kept, shared):
    own_x = lax.axis_index("gx")
    even = lax.axis_index("gy") % 2 == 0
    low2 = jnp.where(own_x > 1, jnp.where(even, kept, shared), 0.0)
    high2 = jnp.where(own_x < count_x - 2, jnp.where(even, shared, kept), 0.0)
    lane = lax.broadcasted_iota(i32, (8, LANES), 1)
    total = total + pltpu.roll(low1, LANES - held, axis=1) + pltpu.roll(high1, held, axis=1)
    total = total + jnp.where(lane < held, pltpu.roll(low2, LANES - 2 * held, axis=1), 0.0)
    return total + jnp.where(lane // held == 2, pltpu.roll(high2, 2 * held, axis=1), 0.0)


def second_kernel(held, count_x, l_ref, sp_ref, xo_ref, xe_ref, s_ref, inertia_ref, slot_ref, drag_ref, xkey_ref,
                  xlow_ref, yface_ref, low_ref, old_table_ref, old_total_ref, kept_ref, shared_ref,
                  v_ref, force_ref, mtable_ref, ye_ref, yo_ref, col_ref, acc_ref, face_ref, sample_ref):
    comps, nx, ny, nz = l_ref.shape
    low, high = beside(xe_ref[...], xo_ref[...], lax.axis_index("gx"), count_x)
    total = sum_totals(held, count_x, old_total_ref[...], low[comps, 0:8], high[comps, 0:8], kept_ref[...], shared_ref[...])
    old = old_table_ref[...]
    row = lax.broadcasted_iota(i32, (8, LANES), 0)
    lane = lax.broadcasted_iota(i32, (8, LANES), 1)
    table = jnp.where((row < 3) & (lane < 3 * held), old + old[3:4] * total, old)
    mtable_ref[...] = table
    z = nz * 2 * ny // WIDE
    for c in range(comps):
        turned = jnp.concatenate([low[c], high[c]], axis=0).T
        wide = jnp.concatenate([turned[h * z : (h + 1) * z] for h in range(nz // z)], axis=1)
        at = comps * z + c * z
        face_ref[c * z : (c + 1) * z, :], face_ref[at : at + z, :] = split(wide)
    for j in range(xkey_ref.shape[0] // 2):
        hot = hot_rows(wide_row(xkey_ref, j), WIDE)
        product = jnp.dot(face_ref[...], hot, preferred_element_type=f32)
        product = product[: comps * z] + product[comps * z :]
        for k, found in enumerate(pick(product, wide_row(xlow_ref, j), comps)):
            store_row(sample_ref, k, j, found)
    for c in range(comps):
        v_ref[c, 0] = l_ref[c, 0] + low[c]
        v_ref[c, nx - 1] = l_ref[c, nx - 1] + high[c]
    samples = [sp_ref[c] + sample_ref[c] for c in range(comps)]
    acc = [inertia_ref[...] * (samples[c] - s_ref[c]) for c in range(comps)]
    forces(samples, acc, slot_ref[...], drag_ref[...], table, force_ref)
    fields, _ = faces_of(yface_ref, low_ref, None, force_ref, col_ref, acc_ref, nz)
    for c in range(comps):
        y_messages(v_ref, c, (fields[c][:nx], fields[c][nx:]), (ye_ref, yo_ref))


def finish_kernel(count_y, early, v_ref, load_ref, odd_ref, even_ref, force_ref, row_ref, depth_ref, after_ref,
                  out_hbm, face_ref, l_ref, rest_ref, col_ref, acc_ref, sem):
    comps, nx = v_ref.shape[:2]
    low, high = beside(even_ref[...], odd_ref[...], lax.axis_index("gy"), count_y)
    if early < comps:
        deposit(range(early, comps), force_ref, row_ref, depth_ref, col_ref, acc_ref, rest_ref)
    for c in range(comps):
        load = load_ref[c] if c < early else rest_ref[c - early]
        own_update(c, v_ref, load, l_ref, low, high)
        pltpu.make_async_copy(l_ref.at[c], out_hbm.at[c], sem.at[c]).start()
        face_ref[c, 0] = l_ref[c, 0]
        face_ref[c, 1] = l_ref[c, nx - 1]
    for c in range(comps):
        pltpu.make_async_copy(l_ref.at[c], out_hbm.at[c], sem.at[c]).wait()


def last_kernel(held, count_x, face_ref, xo_ref, xe_ref, mtable_ref, total_ref, old_hbm, m_hbm, v_hbm, new_ref, m_ref, sem):
    comps, nx = v_hbm.shape[:2]
    low, high = beside(xe_ref[...], xo_ref[...], lax.axis_index("gx"), count_x)
    copies = []
    for side, part in enumerate((low, high)):
        for c in range(comps):
            new_ref[side, c] = face_ref[c, side] + part[c]
        copies.append(pltpu.make_async_copy(new_ref.at[side], v_hbm.at[:, side * (nx - 1)], sem.at[side]))
        copies[-1].start()
    total = total_ref[...] + pltpu.roll(low[comps, 0:8], LANES - held, axis=1)
    total = total + pltpu.roll(high[comps, 0:8], held, axis=1)
    table = mtable_ref[...]
    table = table + table[3:4] * total
    m_ref[...] = pltpu.roll(table, LANES - held, axis=1)[0:3, :held]
    copies.append(pltpu.make_async_copy(m_ref, m_hbm, sem.at[2]))
    copies[-1].start()
    for copy in copies:
        copy.wait()


def near_pairs(axis, odd):
    count_x, count_y = lax.axis_size("gx"), lax.axis_size("gy")
    found = []
    for x in range(count_x):
        for y in range(count_y):
            at, count = (x, count_x) if axis == "gx" else (y, count_y)
            to = ((at + 1) ^ 1) - 1 if odd else at ^ 1
            if axis == "gy":
                target = (x, to % count)
            else:
                target = (to, y) if 0 <= to < count else (x, y ^ 1)
            found.append((x * count_y + y, target[0] * count_y + target[1]))
    return found


def cross_pairs():
    count_x, count_y = lax.axis_size("gx"), lax.axis_size("gy")
    found = []
    for x in range(count_x):
        for y in range(count_y):
            to = x - 2 if y % 2 == 0 else x + 2
            target = (to, y ^ 1) if 0 <= to < count_x else (x ^ 1, y)
            found.append((x * count_y + y, target[0] * count_y + target[1]))
    return found


def exchange(even_msg, odd_msg, axis):
    both_axes = ("gx", "gy")
    came_odd = lax.ppermute(odd_msg, both_axes, near_pairs(axis, True))
    came_even = lax.ppermute(even_msg, both_axes, near_pairs(axis, False))
    return came_even, came_odd


def per_device(velocity, velocity_old, station_cell, station_member, drag_coef, inertia_coef, member_velocity,
               member_inv_mass):
    count_x, count_y = lax.axis_size("gx"), lax.axis_size("gy")
    held = member_velocity.shape[1]
    grid = velocity.shape
    comps, nx, ny, nz = grid
    rows = nx * ny
    lines = (station_cell.shape[0] // LANES, LANES)
    ints = jax.ShapeDtypeStruct(lines, i32)
    one = real(*lines)
    three = real(3, *lines)
    tile = real(8, LANES)
    face = real(comps + 1, max(nx, ny), nz)
    spill = real(2, comps, ny, nz)
    product = 12 * nz * rows * lines[0] * LANES
    table = pltpu.VMEM((2, comps * nz, rows), bf16)

    (v, old, drag, inertia, slot, row, depth, key, low, xkey, xface, yface, xlow, own) = call(
        "load", functools.partial(load_kernel, held, count_y),
        (velocity, velocity_old, station_cell.reshape(lines), station_member.reshape(lines),
         drag_coef.reshape(lines), inertia_coef.reshape(lines), member_velocity, member_inv_mass.reshape(1, held)),
        [real(*grid)] * 2 + [one] * 2 + [ints] * 9 + [tile],
        [pltpu.VMEM(lines, i32), pltpu.VMEM(lines, i32), pltpu.VMEM((3, held), f32), pltpu.VMEM((1, held), f32),
         pltpu.SemaphoreType.DMA((8,))],
        in_hbm=range(8),
    )
    own_even, own_odd = exchange(own, own, "gx")
    s, acc = call(
        "samples", sample_kernel, (v, old, row, depth, inertia), [three, three],
        [pltpu.VMEM((2, 2 * comps * nz, rows), bf16), pltpu.VMEM((6,) + lines, f32)], flops=2 * product,
    )
    slots = -(-3 * held // 16) * 16
    work = [pltpu.VMEM((WIDE, WIDE), bf16), pltpu.VMEM((WIDE + slots, WIDE), f32)]
    edge_parts = [three, tile, spill, face, face, tile]
    force, mtable, spills, y_even, y_odd, total = call(
        "first_forces", functools.partial(first_kernel, held, count_x),
        (v, s, acc, slot, drag, key, low, own, own_even, own_odd), edge_parts, work, flops=product // 2,
    )

    def dep_scratch(count):
        return [pltpu.VMEM((2 * count * nz, WIDE), bf16), pltpu.VMEM((rows, 2 * count * nz), f32)]

    def spread(force, count, after):
        return call(
            "deposit", functools.partial(deposit_kernel, range(count)), (force, row, depth, after),
            [real(count, rows, nz), tile], dep_scratch(count), flops=product * count // comps,
        )

    def turn(spills, y_even, y_odd, total, after):
        return call(
            "turn", functools.partial(turn_kernel, count_y), (spills, y_odd, y_even, total, after), [face, face]
        )

    y_even, y_odd = exchange(y_even, y_odd, "gy")
    load, total = spread(force, comps, total)
    (sums,) = call("pair", pair_kernel, (total, y_even, load), [real(16, LANES)])
    sums = lax.ppermute(sums, ("gx", "gy"), cross_pairs())
    x_even, x_odd = turn(spills, y_even, y_odd, total, load)
    kept, given = call("share", share_kernel, (sums, x_even), [tile, tile])
    shared = lax.ppermute(given, ("gx", "gy"), near_pairs("gy", False))
    local, samples = call(
        "middle", functools.partial(middle_kernel, count_y), (v, load, y_odd, y_even, row, depth, kept),
        [real(*grid), three], [table], flops=product,
    )
    x_even, x_odd = exchange(x_even, x_odd, "gx")
    z = nz * 2 * ny // WIDE
    v, force, mtable, y_even, y_odd = call(
        "second_forces", functools.partial(second_kernel, held, count_x),
        (local, samples, x_odd, x_even, s, inertia, slot, drag, xkey, xlow, yface, low, mtable, total,
         kept, shared),
        [real(*grid), three, tile, face, face],
        [pltpu.VMEM((WIDE, WIDE), bf16), pltpu.VMEM((LANES, WIDE), f32),
         pltpu.VMEM((2 * comps * z, WIDE), bf16), pltpu.VMEM((3,) + lines, f32)],
        flops=product // 2, aliases={0: 0},
    )
    y_even, y_odd = exchange(y_even, y_odd, "gy")
    spills, total = call(
        "spills", spill_kernel, (v, force, xface, low, slot), [spill, tile],
        [pltpu.VMEM((WIDE, WIDE), bf16), pltpu.VMEM((LANES + slots, WIDE), f32)], flops=product // 4,
    )
    load, total = spread(force, 2, total)
    x_even, x_odd = turn(spills, y_even, y_odd, total, load)
    late = max(comps - 2, 1)
    out, faces = call(
        "finish", functools.partial(finish_kernel, count_y, 2),
        (v, load, y_odd, y_even, force, row, depth, x_even),
        [real(*grid), real(comps, 2, ny, nz)],
        [pltpu.VMEM(grid, f32), pltpu.VMEM((late, rows, nz), f32)] + dep_scratch(late)
        + [pltpu.SemaphoreType.DMA((comps,))],
        out_hbm=(0,), flops=product // 3,
    )
    x_even, x_odd = exchange(x_even, x_odd, "gx")
    members, out = call(
        "last", functools.partial(last_kernel, held, count_x), (faces, x_odd, x_even, mtable, total, out),
        [real(3, held), real(*grid)],
        [pltpu.VMEM((2, comps, ny, nz), f32), pltpu.VMEM((3, held), f32), pltpu.SemaphoreType.DMA((3,))],
        in_hbm=(5,), out_hbm=(0, 1), aliases={5: 1},
    )
    return out, members


def solution(mesh):
    return jax.shard_map(
        per_device,
        mesh=mesh,
        in_specs=(
            P(None, "gx", "gy", None),
            P(None, "gx", "gy", None),
            P(("gx", "gy")),
            P(("gx", "gy"), None),
            P(("gx", "gy")),
            P(("gx", "gy")),
            P(None, ("gx", "gy")),
            P(("gx", "gy")),
        ),
        out_specs=(P(None, "gx", "gy", None), P(None, ("gx", "gy"))),
        check_vma=False,
    )
```

```python
import functools

import jax
import jax.numpy as jnp
from jax import lax
from jax.experimental import pallas as pl
from jax.experimental.pallas import tpu as pltpu
from jax.sharding import PartitionSpec as P

LANES = 128
WIDE = 256
FACE_ROWS = 32

viscous = 0.125
softening = 0.01

f32 = jnp.float32
i32 = jnp.int32
bf16 = jnp.bfloat16
HBM = pl.BlockSpec(memory_space=pltpu.HBM)
NT = (((1,), (1,)), ((), ()))


def call(name, body, ins, outs, scratch=(), in_hbm=(), out_hbm=(), flops=0, size=1 << 18, aliases=None):
    whole = pl.BlockSpec(memory_space=pltpu.VMEM)
    ins = [pltpu.with_memory_space_constraint(x, pltpu.HBM) if k in in_hbm else x for k, x in enumerate(ins)]
    outs = [pltpu.HBM(x.shape, x.dtype) if k in out_hbm else x for k, x in enumerate(outs)]
    return pl.pallas_call(
        body,
        name=name,
        out_shape=outs,
        in_specs=[HBM if k in in_hbm else whole for k in range(len(ins))],
        out_specs=[HBM if k in out_hbm else whole for k in range(len(outs))],
        scratch_shapes=list(scratch),
        input_output_aliases=aliases or {},
        compiler_params=pltpu.CompilerParams(vmem_limit_bytes=24 << 20),
        cost_estimate=pl.CostEstimate(flops=flops, bytes_accessed=size, transcendentals=0),
    )(*ins)


def real(*shape):
    return jax.ShapeDtypeStruct(shape, f32)


def split(x):
    top = x.astype(bf16)
    return top, (x - top.astype(f32)).astype(bf16)


def hot_rows(index, count):
    ids = lax.broadcasted_iota(i32, (count, index.shape[1]), 0).astype(f32).astype(bf16)
    wide = jnp.broadcast_to(index.astype(f32).astype(bf16), ids.shape)
    return jnp.where(ids == wide, jnp.ones_like(wide), jnp.zeros_like(wide))


def wide_row(ref, j):
    return jnp.concatenate([ref[2 * j : 2 * j + 1, :], ref[2 * j + 1 : 2 * j + 2, :]], axis=1)


def store_row(ref, k, j, row):
    ref[k, 2 * j : 2 * j + 1, :] = row[:, :LANES]
    ref[k, 2 * j + 1 : 2 * j + 2, :] = row[:, LANES:]


def pick(product, depth_row, count):
    z = product.shape[0] // count
    hit = lax.broadcasted_iota(i32, (z, depth_row.shape[1]), 0) == depth_row
    return [
        jnp.sum(jnp.where(hit, product[k * z : (k + 1) * z], 0.0), axis=0, keepdims=True) for k in range(count)
    ]


def gather(fields, table_ref, row_ref, depth_ref, out_ref):
    rows, z = fields[0].shape
    count = len(fields)
    for k, field in enumerate(fields):
        table_ref[0, k * z : (k + 1) * z, :], table_ref[1, k * z : (k + 1) * z, :] = split(field.T)
    for j in range(row_ref.shape[0] // 2):
        hot = hot_rows(wide_row(row_ref, j), rows)
        hit = lax.broadcasted_iota(i32, (z, WIDE), 0) == wide_row(depth_ref, j)
        for k in range(count):
            part = slice(k * z, (k + 1) * z)
            product = jnp.dot(table_ref[0, part], hot, preferred_element_type=f32)
            product = product + jnp.dot(table_ref[1, part], hot, preferred_element_type=f32)
            store_row(out_ref, k, j, jnp.sum(jnp.where(hit, product, 0.0), axis=0, keepdims=True))


def columns(ref, force_ref, depth_row, z, j, groups):
    hit = hot_rows(depth_row, z) > 0
    for c in range(3):
        for p, piece in enumerate(split(wide_row(force_ref.at[c], j))):
            wide = jnp.broadcast_to(piece, hit.shape)
            at = (p * groups + c) * z
            ref[at : at + z, :] = jnp.where(hit, wide, jnp.zeros_like(wide))


def moved(x, axis, by):
    n = x.shape[axis]
    if axis >= x.ndim - 2:
        ids = lax.broadcasted_iota(i32, x.shape, axis)
        return jnp.where(ids == (0 if by > 0 else n - 1), 0.0, pltpu.roll(x, by % n, axis=axis))
    zero = jnp.zeros_like(lax.slice_in_dim(x, 0, 1, axis=axis))
    if by > 0:
        return jnp.concatenate([zero, lax.slice_in_dim(x, 0, n - 1, axis=axis)], axis=axis)
    return jnp.concatenate([lax.slice_in_dim(x, 1, n, axis=axis), zero], axis=axis)


def both(x, axis):
    return moved(x, axis, 1) + moved(x, axis, -1)


def smooth(x, axis):
    return 0.5 * x + 0.25 * both(x, axis)


def beside(even_msg, odd_msg, own, count):
    even = own % 2 == 0
    low = jnp.where(own > 0, jnp.where(even, odd_msg, even_msg), 0.0)
    high = jnp.where(own < count - 1, jnp.where(even, even_msg, odd_msg), 0.0)
    return low, high


def add_y(c, face_low, face_high, ref):
    ny = ref.shape[2]
    ref[c, :, 0, :] += face_low[c]
    ref[c, :, ny - 1, :] += face_high[c]


def edges(v_ref, force_ref, key_ref, low_ref, slot_ref, col_ref, acc_ref, spill_ref, y_refs, total_ref):
    comps, nx, ny, nz = v_ref.shape
    ring = 2 * (nx + ny)
    parts = WIDE // ring
    z = nz // parts
    slots = acc_ref.shape[0] - WIDE
    free = 3 * z
    for p in range(2):
        col_ref[p * LANES + free : (p + 1) * LANES, :] = jnp.zeros((LANES - free, WIDE), bf16)
    for j in range(key_ref.shape[0] // 2):
        hot = jnp.concatenate([hot_rows(wide_row(key_ref, j), WIDE), hot_rows(wide_row(slot_ref, j), slots)], axis=0)
        columns(col_ref, force_ref, wide_row(low_ref, j), z, j, LANES // z)
        pieces = [split(wide_row(force_ref.at[c], j)) for c in range(3)]
        for p in range(2):
            rows = [piece[p].astype(f32) for piece in pieces] + [jnp.zeros((13, WIDE), f32)]
            col_ref[p * LANES + free : p * LANES + free + 16, :] = jnp.concatenate(rows, axis=0).astype(bf16)
        part = lax.dot_general(hot, col_ref[...], NT, preferred_element_type=f32)
        acc_ref[...] = part if j == 0 else acc_ref[...] + part
    found = acc_ref[:, :LANES] + acc_ref[:, LANES:]
    sums = jnp.concatenate([found[WIDE:], jnp.zeros((LANES - slots, LANES), f32)], axis=0)
    total_ref[...] = sums.T[free : free + 8]
    found = -found[:WIDE]
    lane = lax.broadcasted_iota(i32, (ring, LANES), 1) // z
    yid = lax.broadcasted_iota(i32, (ny, nz), 0)
    for c in range(comps):
        w = jnp.zeros((ring, nz), f32)
        for h in range(parts):
            block = found[h * ring : (h + 1) * ring]
            by = (h - c) * z % LANES
            block = pltpu.roll(block, by, axis=1) if by else block
            w = jnp.where(lane == h, block, w)
        w = smooth(w, 1)
        y_ends = (w[:nx], w[nx : 2 * nx])
        for side, x in ((0, 0), (1, nx - 1)):
            face = w[2 * nx + side * ny : 2 * nx + (side + 1) * ny]
            face = jnp.where(yid == 0, y_ends[0][x : x + 1], face)
            face = jnp.where(yid == ny - 1, y_ends[1][x : x + 1], face)
            spill_ref[side, c] = 0.25 * smooth(face, 0) + viscous * v_ref[c, x]
        y_messages(v_ref, c, y_ends, y_refs)


def faces_of(key_ref, low_ref, slot_ref, force_ref, col_ref, acc_ref, nz):
    parts = LANES // FACE_ROWS
    z = nz // parts
    free = 3 * z
    slots = acc_ref.shape[0] - LANES
    for p in range(2):
        col_ref[p * LANES + free : (p + 1) * LANES, :] = jnp.zeros((LANES - free, WIDE), bf16)
    for j in range(key_ref.shape[0] // 2):
        hot = hot_rows(wide_row(key_ref, j), LANES)
        columns(col_ref, force_ref, wide_row(low_ref, j), z, j, LANES // z)
        if slot_ref is not None:
            hot = jnp.concatenate([hot, hot_rows(wide_row(slot_ref, j), slots)], axis=0)
            pieces = [split(wide_row(force_ref.at[c], j)) for c in range(3)]
            for p in range(2):
                rows = [piece[p].astype(f32) for piece in pieces] + [jnp.zeros((13, WIDE), f32)]
                col_ref[p * LANES + free : p * LANES + free + 16, :] = jnp.concatenate(rows, axis=0).astype(bf16)
        part = lax.dot_general(hot, col_ref[...], NT, preferred_element_type=f32)
        acc_ref[...] = part if j == 0 else acc_ref[...] + part
    found = acc_ref[:, :LANES] + acc_ref[:, LANES:]
    total = None
    if slot_ref is not None:
        sums = jnp.concatenate([found[LANES:], jnp.zeros((LANES - slots, LANES), f32)], axis=0)
        total = sums.T[free : free + 8]
    lane = lax.broadcasted_iota(i32, (FACE_ROWS, LANES), 1) // z
    fields = []
    for c in range(3):
        w = jnp.zeros((FACE_ROWS, nz), f32)
        for h in range(parts):
            block = -found[h * FACE_ROWS : (h + 1) * FACE_ROWS]
            by = (h - c) * z % LANES
            block = pltpu.roll(block, by, axis=1) if by else block
            w = jnp.where(lane == h, block, w)
        fields.append(smooth(w, 1))
    return fields, total


def y_messages(v_ref, c, y_ends, y_refs):
    comps, nx, ny, nz = v_ref.shape
    even = lax.axis_index("gy") % 2 == 0
    low, high = [
        (smooth(0.25 * w_y, 0) + viscous * v_ref[c, :, y, :], 0.0625 * w_y[0:1], 0.0625 * w_y[nx - 1 : nx])
        for y, w_y in zip((0, ny - 1), y_ends)
    ]
    for ref, flip in zip(y_refs, (even, jnp.logical_not(even))):
        ref[c] = jnp.where(flip, high[0], low[0])
        for side in range(2):
            at = 3 * side + c
            ref[comps, at : at + 1, :] = jnp.where(flip, high[1 + side], low[1 + side])


def spill_kernel(v_ref, force_ref, key_ref, low_ref, slot_ref, spill_ref, total_ref, col_ref, acc_ref):
    comps, nx, ny, nz = v_ref.shape
    fields, total = faces_of(key_ref, low_ref, slot_ref, force_ref, col_ref, acc_ref, nz)
    total_ref[...] = total
    for c in range(comps):
        for side, x in ((0, 0), (1, nx - 1)):
            face = fields[c][side * ny : (side + 1) * ny]
            spill_ref[side, c] = 0.25 * smooth(face, 0) + viscous * v_ref[c, x]


def forces(samples, acc, slot, drag, table, force_ref):
    relative = [
        samples[c] - jnp.take_along_axis(jnp.broadcast_to(table[c : c + 1], slot.shape), slot, axis=1)
        for c in range(3)
    ]
    square = relative[0] * relative[0] + relative[1] * relative[1] + relative[2] * relative[2]
    speed = drag * jnp.sqrt(square + softening)
    for c in range(3):
        force_ref[c] = speed * relative[c] + acc[c]


def load_kernel(held, count_y, v_any, old_any, cell_any, member_any, drag_any, inertia_any, mv_any, mass_any,
                v_ref, old_ref, drag_ref, inertia_ref, slot_ref, row_ref, depth_ref, key_ref, low_ref, xkey_ref,
                xface_ref, yface_ref, xlow_ref, own_ref, cell_ref, member_ref, mv_ref, mass_ref, sem):
    loads = [(cell_any, cell_ref), (member_any, member_ref), (mv_any, mv_ref), (mass_any, mass_ref),
             (drag_any, drag_ref), (inertia_any, inertia_ref), (v_any, v_ref), (old_any, old_ref)]
    copies = [pltpu.make_async_copy(a, b, sem.at[k]) for k, (a, b) in enumerate(loads)]
    for copy in copies:
        copy.start()
    comps, nx, ny, nz = v_ref.shape
    copies[0].wait()
    cell = cell_ref[...]
    row, depth = lax.div(cell, nz), lax.rem(cell, nz)
    row_ref[...] = row
    depth_ref[...] = depth
    x, y = lax.div(row, ny), lax.rem(row, ny)
    ring = 2 * (nx + ny)
    edge = jnp.where(x == 0, 2 * nx + y, jnp.where(x == nx - 1, 2 * nx + ny + y, -1))
    edge = jnp.where(y == 0, x, jnp.where(y == ny - 1, nx + x, edge))
    z = nz * ring // WIDE
    key_ref[...] = jnp.where(edge < 0, -1, lax.div(depth, z) * ring + edge)
    low_ref[...] = lax.rem(depth, z)
    part = lax.div(depth, nz // (LANES // FACE_ROWS)) * FACE_ROWS
    face = jnp.where(y == 0, x, jnp.where(y == ny - 1, nx + x, -1))
    yface_ref[...] = jnp.where(face < 0, -1, part + face)
    face = jnp.where(x == 0, y, jnp.where(x == nx - 1, ny + y, -1))
    xface_ref[...] = jnp.where(face < 0, -1, part + face)
    z = nz * 2 * ny // WIDE
    xkey_ref[...] = jnp.where(face < 0, -1, lax.div(depth, z) * (2 * ny) + face)
    xlow_ref[...] = lax.rem(depth, z)
    copies[1].wait()
    member = member_ref[...]
    owner = lax.div(lax.div(member, held), count_y)
    slot_ref[...] = (owner - lax.axis_index("gx") + 1) * held + lax.rem(member, held)
    for copy in copies[2:]:
        copy.wait()
    own_ref[...] = jnp.zeros_like(own_ref)
    own_ref[0:3, 0:held] = mv_ref[...]
    own_ref[3:4, 0:held] = mass_ref[...]


def sample_kernel(v_ref, old_ref, row_ref, depth_ref, inertia_ref, s_ref, acc_ref, table_ref, six_ref):
    comps, nx, ny, nz = v_ref.shape
    fields = [ref[k].reshape(nx * ny, nz) for ref in (v_ref, old_ref) for k in range(comps)]
    gather(fields, table_ref, row_ref, depth_ref, six_ref)
    for c in range(comps):
        s_ref[c] = six_ref[c]
        acc_ref[c] = inertia_ref[...] * (six_ref[c] - six_ref[comps + c])


def first_kernel(held, count_x, v_ref, s_ref, acc_ref, slot_ref, drag_ref, key_ref, low_ref, own_ref, even_ref,
                 odd_ref, force_ref, mtable_ref, spill_ref, ye_ref, yo_ref, total_ref, col_ref, field_ref):
    low, high = beside(even_ref[...], odd_ref[...], lax.axis_index("gx"), count_x)
    table = low + pltpu.roll(own_ref[...], held, axis=1) + pltpu.roll(high, 2 * held, axis=1)
    mtable_ref[...] = table
    forces([s_ref[c] for c in range(3)], [acc_ref[c] for c in range(3)], slot_ref[...], drag_ref[...], table,
           force_ref)
    edges(v_ref, force_ref, key_ref, low_ref, slot_ref, col_ref, field_ref, spill_ref, (ye_ref, yo_ref), total_ref)
    comps = v_ref.shape[0]
    for ref in (ye_ref, yo_ref):
        ref[comps, 8:16, :] = total_ref[...]


def pair_kernel(total_ref, came_ref, after_ref, out_ref):
    comps = came_ref.shape[0] - 1
    even = lax.axis_index("gy") % 2 == 0
    own, other = total_ref[...], came_ref[comps, 8:16, :]
    out_ref[0:8, :] = jnp.where(even, own, other)
    out_ref[8:16, :] = jnp.where(even, other, own)


def share_kernel(came_ref, after_ref, keep_ref, give_ref):
    even = lax.axis_index("gy") % 2 == 0
    first, second = came_ref[0:8, :], came_ref[8:16, :]
    keep_ref[...] = jnp.where(even, first, second)
    give_ref[...] = jnp.where(even, second, first)


def deposit(comps, force_ref, row_ref, depth_ref, col_ref, acc_ref, out_ref):
    rows, nz = out_ref.shape[1:]
    count = len(comps)
    for j in range(row_ref.shape[0] // 2):
        hot = hot_rows(wide_row(row_ref, j), rows)
        hit = hot_rows(wide_row(depth_ref, j), nz) > 0
        for k, c in enumerate(comps):
            for p, piece in enumerate(split(wide_row(force_ref.at[c], j))):
                wide = jnp.broadcast_to(piece, hit.shape)
                at = (p * count + k) * nz
                col_ref[at : at + nz, :] = jnp.where(hit, wide, jnp.zeros_like(wide))
        part = lax.dot_general(hot, col_ref[...], NT, preferred_element_type=f32)
        acc_ref[...] = part if j == 0 else acc_ref[...] + part
    for k in range(count):
        out_ref[k] = -(acc_ref[:, k * nz : (k + 1) * nz] + acc_ref[:, (count + k) * nz : (count + k + 1) * nz])


def deposit_kernel(comps, force_ref, row_ref, depth_ref, total_ref, out_ref, same_ref, col_ref, acc_ref):
    same_ref[...] = total_ref[...]
    deposit(comps, force_ref, row_ref, depth_ref, col_ref, acc_ref, out_ref)


def turn_kernel(count_y, spill_ref, odd_ref, even_ref, total_ref, after_ref, xe_ref, xo_ref):
    comps, ny, nz = spill_ref.shape[1:]
    low, high = beside(even_ref[comps], odd_ref[comps], lax.axis_index("gy"), count_y)
    even = lax.axis_index("gx") % 2 == 0
    ids = lax.broadcasted_iota(i32, (ny, nz), 0)
    for c in range(comps):
        sides = []
        for side in range(2):
            at = 3 * side + c
            face = spill_ref[side, c]
            face = face + jnp.where(ids == 0, low[at : at + 1], 0.0)
            face = face + jnp.where(ids == ny - 1, high[at : at + 1], 0.0)
            sides.append(face)
        xe_ref[c] = jnp.where(even, sides[1], sides[0])
        xo_ref[c] = jnp.where(even, sides[0], sides[1])
    for ref in (xe_ref, xo_ref):
        ref[comps, 0:8, :] = total_ref[...]
        ref[comps, 8:16, :] = jnp.zeros_like(total_ref)


def own_update(c, v_ref, load, l_ref, low, high):
    nx, ny, nz = v_ref.shape[1:]
    v = v_ref[c]
    w = smooth(smooth(smooth(load.reshape(nx, ny, nz), 2), 1), 0)
    beside_all = both(v, 0) + both(v, 1) + both(v, 2)
    l_ref[c] = v + viscous * (beside_all - 6.0 * v) + w
    add_y(c, low, high, l_ref)


def middle_kernel(count_y, v_ref, load_ref, odd_ref, even_ref, row_ref, depth_ref, after_ref, l_ref, s_ref,
                  table_ref):
    comps, nx, ny, nz = v_ref.shape
    low, high = beside(even_ref[...], odd_ref[...], lax.axis_index("gy"), count_y)
    for c in range(comps):
        own_update(c, v_ref, load_ref[c], l_ref, low, high)
    gather([l_ref[k].reshape(nx * ny, nz) for k in range(comps)], table_ref, row_ref, depth_ref, s_ref)


def sum_totals(held, count_x, total, low1, high1, kept, shared):
    own_x = lax.axis_index("gx")
    even = lax.axis_index("gy") % 2 == 0
    low2 = jnp.where(own_x > 1, jnp.where(even, kept, shared), 0.0)
    high2 = jnp.where(own_x < count_x - 2, jnp.where(even, shared, kept), 0.0)
    lane = lax.broadcasted_iota(i32, (8, LANES), 1)
    total = total + pltpu.roll(low1, LANES - held, axis=1) + pltpu.roll(high1, held, axis=1)
    total = total + jnp.where(lane < held, pltpu.roll(low2, LANES - 2 * held, axis=1), 0.0)
    return total + jnp.where(lane // held == 2, pltpu.roll(high2, 2 * held, axis=1), 0.0)


def second_kernel(held, count_x, l_ref, sp_ref, xo_ref, xe_ref, s_ref, inertia_ref, slot_ref, drag_ref, xkey_ref,
                  xlow_ref, yface_ref, low_ref, old_table_ref, old_total_ref, kept_ref, shared_ref,
                  v_ref, force_ref, mtable_ref, ye_ref, yo_ref, col_ref, acc_ref, face_ref, sample_ref):
    comps, nx, ny, nz = l_ref.shape
    low, high = beside(xe_ref[...], xo_ref[...], lax.axis_index("gx"), count_x)
    total = sum_totals(held, count_x, old_total_ref[...], low[comps, 0:8], high[comps, 0:8], kept_ref[...], shared_ref[...])
    old = old_table_ref[...]
    row = lax.broadcasted_iota(i32, (8, LANES), 0)
    lane = lax.broadcasted_iota(i32, (8, LANES), 1)
    table = jnp.where((row < 3) & (lane < 3 * held), old + old[3:4] * total, old)
    mtable_ref[...] = table
    z = nz * 2 * ny // WIDE
    for c in range(comps):
        turned = jnp.concatenate([low[c], high[c]], axis=0).T
        wide = jnp.concatenate([turned[h * z : (h + 1) * z] for h in range(nz // z)], axis=1)
        at = comps * z + c * z
        face_ref[c * z : (c + 1) * z, :], face_ref[at : at + z, :] = split(wide)
    for j in range(xkey_ref.shape[0] // 2):
        hot = hot_rows(wide_row(xkey_ref, j), WIDE)
        product = jnp.dot(face_ref[...], hot, preferred_element_type=f32)
        product = product[: comps * z] + product[comps * z :]
        for k, found in enumerate(pick(product, wide_row(xlow_ref, j), comps)):
            store_row(sample_ref, k, j, found)
    for c in range(comps):
        v_ref[c, 0] = l_ref[c, 0] + low[c]
        v_ref[c, 1 : nx - 1] = l_ref[c, 1 : nx - 1]
        v_ref[c, nx - 1] = l_ref[c, nx - 1] + high[c]
    samples = [sp_ref[c] + sample_ref[c] for c in range(comps)]
    acc = [inertia_ref[...] * (samples[c] - s_ref[c]) for c in range(comps)]
    forces(samples, acc, slot_ref[...], drag_ref[...], table, force_ref)
    fields, _ = faces_of(yface_ref, low_ref, None, force_ref, col_ref, acc_ref, nz)
    for c in range(comps):
        y_messages(v_ref, c, (fields[c][:nx], fields[c][nx:]), (ye_ref, yo_ref))


def finish_kernel(count_y, early, v_ref, load_ref, odd_ref, even_ref, force_ref, row_ref, depth_ref, after_ref,
                  out_hbm, face_ref, l_ref, rest_ref, col_ref, acc_ref, sem):
    comps, nx = v_ref.shape[:2]
    low, high = beside(even_ref[...], odd_ref[...], lax.axis_index("gy"), count_y)
    if early < comps:
        deposit(range(early, comps), force_ref, row_ref, depth_ref, col_ref, acc_ref, rest_ref)
    for c in range(comps):
        load = load_ref[c] if c < early else rest_ref[c - early]
        own_update(c, v_ref, load, l_ref, low, high)
        pltpu.make_async_copy(l_ref.at[c], out_hbm.at[c], sem.at[c]).start()
        face_ref[c, 0] = l_ref[c, 0]
        face_ref[c, 1] = l_ref[c, nx - 1]
    for c in range(comps):
        pltpu.make_async_copy(l_ref.at[c], out_hbm.at[c], sem.at[c]).wait()


def last_kernel(held, count_x, face_ref, xo_ref, xe_ref, mtable_ref, total_ref, old_hbm, m_hbm, v_hbm, new_ref, m_ref, sem):
    comps, nx = v_hbm.shape[:2]
    low, high = beside(xe_ref[...], xo_ref[...], lax.axis_index("gx"), count_x)
    copies = []
    for side, part in enumerate((low, high)):
        for c in range(comps):
            new_ref[side, c] = face_ref[c, side] + part[c]
        copies.append(pltpu.make_async_copy(new_ref.at[side], v_hbm.at[:, side * (nx - 1)], sem.at[side]))
        copies[-1].start()
    total = total_ref[...] + pltpu.roll(low[comps, 0:8], LANES - held, axis=1)
    total = total + pltpu.roll(high[comps, 0:8], held, axis=1)
    table = mtable_ref[...]
    table = table + table[3:4] * total
    m_ref[...] = pltpu.roll(table, LANES - held, axis=1)[0:3, :held]
    copies.append(pltpu.make_async_copy(m_ref, m_hbm, sem.at[2]))
    copies[-1].start()
    for copy in copies:
        copy.wait()


def near_pairs(axis, odd):
    count_x, count_y = lax.axis_size("gx"), lax.axis_size("gy")
    found = []
    for x in range(count_x):
        for y in range(count_y):
            at, count = (x, count_x) if axis == "gx" else (y, count_y)
            to = ((at + 1) ^ 1) - 1 if odd else at ^ 1
            if axis == "gy":
                target = (x, to % count)
            else:
                target = (to, y) if 0 <= to < count else (x, y ^ 1)
            found.append((x * count_y + y, target[0] * count_y + target[1]))
    return found


def cross_pairs():
    count_x, count_y = lax.axis_size("gx"), lax.axis_size("gy")
    found = []
    for x in range(count_x):
        for y in range(count_y):
            to = x - 2 if y % 2 == 0 else x + 2
            target = (to, y ^ 1) if 0 <= to < count_x else (x ^ 1, y)
            found.append((x * count_y + y, target[0] * count_y + target[1]))
    return found


def exchange(even_msg, odd_msg, axis):
    both_axes = ("gx", "gy")
    came_odd = lax.ppermute(odd_msg, both_axes, near_pairs(axis, True))
    came_even = lax.ppermute(even_msg, both_axes, near_pairs(axis, False))
    return came_even, came_odd


def per_device(velocity, velocity_old, station_cell, station_member, drag_coef, inertia_coef, member_velocity,
               member_inv_mass):
    count_x, count_y = lax.axis_size("gx"), lax.axis_size("gy")
    held = member_velocity.shape[1]
    grid = velocity.shape
    comps, nx, ny, nz = grid
    rows = nx * ny
    lines = (station_cell.shape[0] // LANES, LANES)
    ints = jax.ShapeDtypeStruct(lines, i32)
    one = real(*lines)
    three = real(3, *lines)
    tile = real(8, LANES)
    face = real(comps + 1, max(nx, ny), nz)
    spill = real(2, comps, ny, nz)
    product = 12 * nz * rows * lines[0] * LANES
    table = pltpu.VMEM((2, comps * nz, rows), bf16)

    (v, old, drag, inertia, slot, row, depth, key, low, xkey, xface, yface, xlow, own) = call(
        "load", functools.partial(load_kernel, held, count_y),
        (velocity, velocity_old, station_cell.reshape(lines), station_member.reshape(lines),
         drag_coef.reshape(lines), inertia_coef.reshape(lines), member_velocity, member_inv_mass.reshape(1, held)),
        [real(*grid)] * 2 + [one] * 2 + [ints] * 9 + [tile],
        [pltpu.VMEM(lines, i32), pltpu.VMEM(lines, i32), pltpu.VMEM((3, held), f32), pltpu.VMEM((1, held), f32),
         pltpu.SemaphoreType.DMA((8,))],
        in_hbm=range(8),
    )
    own_even, own_odd = exchange(own, own, "gx")
    s, acc = call(
        "samples", sample_kernel, (v, old, row, depth, inertia), [three, three],
        [pltpu.VMEM((2, 2 * comps * nz, rows), bf16), pltpu.VMEM((6,) + lines, f32)], flops=2 * product,
    )
    slots = -(-3 * held // 16) * 16
    work = [pltpu.VMEM((WIDE, WIDE), bf16), pltpu.VMEM((WIDE + slots, WIDE), f32)]
    edge_parts = [three, tile, spill, face, face, tile]
    force, mtable, spills, y_even, y_odd, total = call(
        "first_forces", functools.partial(first_kernel, held, count_x),
        (v, s, acc, slot, drag, key, low, own, own_even, own_odd), edge_parts, work, flops=product // 2,
    )

    def dep_scratch(count):
        return [pltpu.VMEM((2 * count * nz, WIDE), bf16), pltpu.VMEM((rows, 2 * count * nz), f32)]

    def spread(force, count, after):
        return call(
            "deposit", functools.partial(deposit_kernel, range(count)), (force, row, depth, after),
            [real(count, rows, nz), tile], dep_scratch(count), flops=product * count // comps,
        )

    def turn(spills, y_even, y_odd, total, after):
        return call(
            "turn", functools.partial(turn_kernel, count_y), (spills, y_odd, y_even, total, after), [face, face]
        )

    y_even, y_odd = exchange(y_even, y_odd, "gy")
    load, total = spread(force, comps, total)
    (sums,) = call("pair", pair_kernel, (total, y_even, load), [real(16, LANES)])
    sums = lax.ppermute(sums, ("gx", "gy"), cross_pairs())
    x_even, x_odd = turn(spills, y_even, y_odd, total, load)
    kept, given = call("share", share_kernel, (sums, x_even), [tile, tile])
    shared = lax.ppermute(given, ("gx", "gy"), near_pairs("gy", False))
    local, samples = call(
        "middle", functools.partial(middle_kernel, count_y), (v, load, y_odd, y_even, row, depth, kept),
        [real(*grid), three], [table], flops=product,
    )
    x_even, x_odd = exchange(x_even, x_odd, "gx")
    z = nz * 2 * ny // WIDE
    v, force, mtable, y_even, y_odd = call(
        "second_forces", functools.partial(second_kernel, held, count_x),
        (local, samples, x_odd, x_even, s, inertia, slot, drag, xkey, xlow, yface, low, mtable, total,
         kept, shared),
        [real(*grid), three, tile, face, face],
        [pltpu.VMEM((WIDE, WIDE), bf16), pltpu.VMEM((LANES, WIDE), f32),
         pltpu.VMEM((2 * comps * z, WIDE), bf16), pltpu.VMEM((3,) + lines, f32)],
        flops=product // 2,
    )
    y_even, y_odd = exchange(y_even, y_odd, "gy")
    spills, total = call(
        "spills", spill_kernel, (v, force, xface, low, slot), [spill, tile],
        [pltpu.VMEM((WIDE, WIDE), bf16), pltpu.VMEM((LANES + slots, WIDE), f32)], flops=product // 4,
    )
    load, total = spread(force, 2, total)
    x_even, x_odd = turn(spills, y_even, y_odd, total, load)
    late = max(comps - 2, 1)
    out, faces = call(
        "finish", functools.partial(finish_kernel, count_y, 2),
        (v, load, y_odd, y_even, force, row, depth, x_even),
        [real(*grid), real(comps, 2, ny, nz)],
        [pltpu.VMEM(grid, f32), pltpu.VMEM((late, rows, nz), f32)] + dep_scratch(late)
        + [pltpu.SemaphoreType.DMA((comps,))],
        out_hbm=(0,), flops=product // 3,
    )
    x_even, x_odd = exchange(x_even, x_odd, "gx")
    members, out = call(
        "last", functools.partial(last_kernel, held, count_x), (faces, x_odd, x_even, mtable, total, out),
        [real(3, held), real(*grid)],
        [pltpu.VMEM((2, comps, ny, nz), f32), pltpu.VMEM((3, held), f32), pltpu.SemaphoreType.DMA((3,))],
        in_hbm=(5,), out_hbm=(0, 1), aliases={5: 1},
    )
    return out, members


def solution(mesh):
    return jax.shard_map(
        per_device,
        mesh=mesh,
        in_specs=(
            P(None, "gx", "gy", None),
            P(None, "gx", "gy", None),
            P(("gx", "gy")),
            P(("gx", "gy"), None),
            P(("gx", "gy")),
            P(("gx", "gy")),
            P(None, ("gx", "gy")),
            P(("gx", "gy")),
        ),
        out_specs=(P(None, "gx", "gy", None), P(None, ("gx", "gy"))),
        check_vma=False,
    )
```

```python
import functools

import jax
import jax.numpy as jnp
from jax import lax
from jax.experimental import pallas as pl
from jax.experimental.pallas import tpu as pltpu
from jax.sharding import PartitionSpec as P

LANES = 128
WIDE = 256
FACE_ROWS = 32

viscous = 0.125
softening = 0.01

f32 = jnp.float32
i32 = jnp.int32
bf16 = jnp.bfloat16
HBM = pl.BlockSpec(memory_space=pltpu.HBM)
NT = (((1,), (1,)), ((), ()))


def call(name, body, ins, outs, scratch=(), in_hbm=(), out_hbm=(), flops=0, size=1 << 18, aliases=None):
    whole = pl.BlockSpec(memory_space=pltpu.VMEM)
    ins = [pltpu.with_memory_space_constraint(x, pltpu.HBM) if k in in_hbm else x for k, x in enumerate(ins)]
    outs = [pltpu.HBM(x.shape, x.dtype) if k in out_hbm else x for k, x in enumerate(outs)]
    return pl.pallas_call(
        body,
        name=name,
        out_shape=outs,
        in_specs=[HBM if k in in_hbm else whole for k in range(len(ins))],
        out_specs=[HBM if k in out_hbm else whole for k in range(len(outs))],
        scratch_shapes=list(scratch),
        input_output_aliases=aliases or {},
        compiler_params=pltpu.CompilerParams(vmem_limit_bytes=24 << 20),
        cost_estimate=pl.CostEstimate(flops=flops, bytes_accessed=size, transcendentals=0),
    )(*ins)


def real(*shape):
    return jax.ShapeDtypeStruct(shape, f32)


def split(x):
    top = x.astype(bf16)
    return top, (x - top.astype(f32)).astype(bf16)


def hot_rows(index, count):
    ids = lax.broadcasted_iota(i32, (count, index.shape[1]), 0).astype(f32).astype(bf16)
    wide = jnp.broadcast_to(index.astype(f32).astype(bf16), ids.shape)
    return jnp.where(ids == wide, jnp.ones_like(wide), jnp.zeros_like(wide))


def wide_row(ref, j):
    return jnp.concatenate([ref[2 * j : 2 * j + 1, :], ref[2 * j + 1 : 2 * j + 2, :]], axis=1)


def store_row(ref, k, j, row):
    ref[k, 2 * j : 2 * j + 1, :] = row[:, :LANES]
    ref[k, 2 * j + 1 : 2 * j + 2, :] = row[:, LANES:]


def pick(product, depth_row, count):
    z = product.shape[0] // count
    hit = lax.broadcasted_iota(i32, (z, depth_row.shape[1]), 0) == depth_row
    return [
        jnp.sum(jnp.where(hit, product[k * z : (k + 1) * z], 0.0), axis=0, keepdims=True) for k in range(count)
    ]


def gather(fields, table_ref, row_ref, depth_ref, out_ref):
    rows, z = fields[0].shape
    count = len(fields)
    for k, field in enumerate(fields):
        table_ref[0, k * z : (k + 1) * z, :], table_ref[1, k * z : (k + 1) * z, :] = split(field.T)
    for j in range(row_ref.shape[0] // 2):
        hot = hot_rows(wide_row(row_ref, j), rows)
        hit = lax.broadcasted_iota(i32, (z, WIDE), 0) == wide_row(depth_ref, j)
        for k in range(count):
            part = slice(k * z, (k + 1) * z)
            product = jnp.dot(table_ref[0, part], hot, preferred_element_type=f32)
            product = product + jnp.dot(table_ref[1, part], hot, preferred_element_type=f32)
            store_row(out_ref, k, j, jnp.sum(jnp.where(hit, product, 0.0), axis=0, keepdims=True))


def columns(ref, force_ref, depth_row, z, j, groups):
    hit = hot_rows(depth_row, z) > 0
    for c in range(3):
        for p, piece in enumerate(split(wide_row(force_ref.at[c], j))):
            wide = jnp.broadcast_to(piece, hit.shape)
            at = (p * groups + c) * z
            ref[at : at + z, :] = jnp.where(hit, wide, jnp.zeros_like(wide))


def moved(x, axis, by):
    n = x.shape[axis]
    if axis >= x.ndim - 2:
        ids = lax.broadcasted_iota(i32, x.shape, axis)
        return jnp.where(ids == (0 if by > 0 else n - 1), 0.0, pltpu.roll(x, by % n, axis=axis))
    zero = jnp.zeros_like(lax.slice_in_dim(x, 0, 1, axis=axis))
    if by > 0:
        return jnp.concatenate([zero, lax.slice_in_dim(x, 0, n - 1, axis=axis)], axis=axis)
    return jnp.concatenate([lax.slice_in_dim(x, 1, n, axis=axis), zero], axis=axis)


def both(x, axis):
    return moved(x, axis, 1) + moved(x, axis, -1)


def smooth(x, axis):
    return 0.5 * x + 0.25 * both(x, axis)


def beside(even_msg, odd_msg, own, count):
    even = own % 2 == 0
    low = jnp.where(own > 0, jnp.where(even, odd_msg, even_msg), 0.0)
    high = jnp.where(own < count - 1, jnp.where(even, even_msg, odd_msg), 0.0)
    return low, high


def add_y(c, face_low, face_high, ref):
    ny = ref.shape[2]
    ref[c, :, 0, :] += face_low[c]
    ref[c, :, ny - 1, :] += face_high[c]


def edges(v_ref, force_ref, key_ref, low_ref, slot_ref, col_ref, acc_ref, spill_ref, y_refs, total_ref):
    comps, nx, ny, nz = v_ref.shape
    ring = 2 * (nx + ny)
    parts = WIDE // ring
    z = nz // parts
    slots = acc_ref.shape[0] - WIDE
    free = 3 * z
    for p in range(2):
        col_ref[p * LANES + free : (p + 1) * LANES, :] = jnp.zeros((LANES - free, WIDE), bf16)
    for j in range(key_ref.shape[0] // 2):
        hot = jnp.concatenate([hot_rows(wide_row(key_ref, j), WIDE), hot_rows(wide_row(slot_ref, j), slots)], axis=0)
        columns(col_ref, force_ref, wide_row(low_ref, j), z, j, LANES // z)
        pieces = [split(wide_row(force_ref.at[c], j)) for c in range(3)]
        for p in range(2):
            rows = [piece[p].astype(f32) for piece in pieces] + [jnp.zeros((13, WIDE), f32)]
            col_ref[p * LANES + free : p * LANES + free + 16, :] = jnp.concatenate(rows, axis=0).astype(bf16)
        part = lax.dot_general(hot, col_ref[...], NT, preferred_element_type=f32)
        acc_ref[...] = part if j == 0 else acc_ref[...] + part
    found = acc_ref[:, :LANES] + acc_ref[:, LANES:]
    sums = jnp.concatenate([found[WIDE:], jnp.zeros((LANES - slots, LANES), f32)], axis=0)
    total_ref[...] = sums.T[free : free + 8]
    found = -found[:WIDE]
    lane = lax.broadcasted_iota(i32, (ring, LANES), 1) // z
    yid = lax.broadcasted_iota(i32, (ny, nz), 0)
    for c in range(comps):
        w = jnp.zeros((ring, nz), f32)
        for h in range(parts):
            block = found[h * ring : (h + 1) * ring]
            by = (h - c) * z % LANES
            block = pltpu.roll(block, by, axis=1) if by else block
            w = jnp.where(lane == h, block, w)
        w = smooth(w, 1)
        y_ends = (w[:nx], w[nx : 2 * nx])
        for side, x in ((0, 0), (1, nx - 1)):
            face = w[2 * nx + side * ny : 2 * nx + (side + 1) * ny]
            face = jnp.where(yid == 0, y_ends[0][x : x + 1], face)
            face = jnp.where(yid == ny - 1, y_ends[1][x : x + 1], face)
            spill_ref[side, c] = 0.25 * smooth(face, 0) + viscous * v_ref[c, x]
        y_messages(v_ref, c, y_ends, y_refs)


def faces_of(key_ref, low_ref, slot_ref, force_ref, col_ref, acc_ref, nz):
    parts = LANES // FACE_ROWS
    z = nz // parts
    free = 3 * z
    slots = acc_ref.shape[0] - LANES
    for p in range(2):
        col_ref[p * LANES + free : (p + 1) * LANES, :] = jnp.zeros((LANES - free, WIDE), bf16)
    for j in range(key_ref.shape[0] // 2):
        hot = hot_rows(wide_row(key_ref, j), LANES)
        columns(col_ref, force_ref, wide_row(low_ref, j), z, j, LANES // z)
        if slot_ref is not None:
            hot = jnp.concatenate([hot, hot_rows(wide_row(slot_ref, j), slots)], axis=0)
            pieces = [split(wide_row(force_ref.at[c], j)) for c in range(3)]
            for p in range(2):
                rows = [piece[p].astype(f32) for piece in pieces] + [jnp.zeros((13, WIDE), f32)]
                col_ref[p * LANES + free : p * LANES + free + 16, :] = jnp.concatenate(rows, axis=0).astype(bf16)
        part = lax.dot_general(hot, col_ref[...], NT, preferred_element_type=f32)
        acc_ref[...] = part if j == 0 else acc_ref[...] + part
    found = acc_ref[:, :LANES] + acc_ref[:, LANES:]
    total = None
    if slot_ref is not None:
        sums = jnp.concatenate([found[LANES:], jnp.zeros((LANES - slots, LANES), f32)], axis=0)
        total = sums.T[free : free + 8]
    lane = lax.broadcasted_iota(i32, (FACE_ROWS, LANES), 1) // z
    fields = []
    for c in range(3):
        w = jnp.zeros((FACE_ROWS, nz), f32)
        for h in range(parts):
            block = -found[h * FACE_ROWS : (h + 1) * FACE_ROWS]
            by = (h - c) * z % LANES
            block = pltpu.roll(block, by, axis=1) if by else block
            w = jnp.where(lane == h, block, w)
        fields.append(smooth(w, 1))
    return fields, total


def y_messages(v_ref, c, y_ends, y_refs):
    comps, nx, ny, nz = v_ref.shape
    even = lax.axis_index("gy") % 2 == 0
    low, high = [
        (smooth(0.25 * w_y, 0) + viscous * v_ref[c, :, y, :], 0.0625 * w_y[0:1], 0.0625 * w_y[nx - 1 : nx])
        for y, w_y in zip((0, ny - 1), y_ends)
    ]
    for ref, flip in zip(y_refs, (even, jnp.logical_not(even))):
        ref[c] = jnp.where(flip, high[0], low[0])
        for side in range(2):
            at = 3 * side + c
            ref[comps, at : at + 1, :] = jnp.where(flip, high[1 + side], low[1 + side])


def spill_kernel(v_ref, force_ref, key_ref, low_ref, slot_ref, spill_ref, total_ref, col_ref, acc_ref):
    comps, nx, ny, nz = v_ref.shape
    fields, total = faces_of(key_ref, low_ref, slot_ref, force_ref, col_ref, acc_ref, nz)
    total_ref[...] = total
    for c in range(comps):
        for side, x in ((0, 0), (1, nx - 1)):
            face = fields[c][side * ny : (side + 1) * ny]
            spill_ref[side, c] = 0.25 * smooth(face, 0) + viscous * v_ref[c, x]


def forces(samples, acc, slot, drag, table, force_ref):
    relative = [
        samples[c] - jnp.take_along_axis(jnp.broadcast_to(table[c : c + 1], slot.shape), slot, axis=1)
        for c in range(3)
    ]
    square = relative[0] * relative[0] + relative[1] * relative[1] + relative[2] * relative[2]
    speed = drag * jnp.sqrt(square + softening)
    for c in range(3):
        force_ref[c] = speed * relative[c] + acc[c]


def load_kernel(held, count_y, v_any, old_any, cell_any, member_any, drag_any, inertia_any, mv_any, mass_any,
                v_ref, old_ref, drag_ref, inertia_ref, slot_ref, row_ref, depth_ref, key_ref, low_ref, xkey_ref,
                xface_ref, yface_ref, xlow_ref, own_ref, cell_ref, member_ref, mv_ref, mass_ref, sem):
    loads = [(v_any, v_ref), (old_any, old_ref), (cell_any, cell_ref), (member_any, member_ref), (mv_any, mv_ref),
             (mass_any, mass_ref), (drag_any, drag_ref), (inertia_any, inertia_ref)]
    copies = [pltpu.make_async_copy(a, b, sem.at[k]) for k, (a, b) in enumerate(loads)]
    for copy in copies:
        copy.start()
    comps, nx, ny, nz = v_ref.shape
    copies[2].wait()
    cell = cell_ref[...]
    row, depth = lax.div(cell, nz), lax.rem(cell, nz)
    row_ref[...] = row
    depth_ref[...] = depth
    x, y = lax.div(row, ny), lax.rem(row, ny)
    ring = 2 * (nx + ny)
    edge = jnp.where(x == 0, 2 * nx + y, jnp.where(x == nx - 1, 2 * nx + ny + y, -1))
    edge = jnp.where(y == 0, x, jnp.where(y == ny - 1, nx + x, edge))
    z = nz * ring // WIDE
    key_ref[...] = jnp.where(edge < 0, -1, lax.div(depth, z) * ring + edge)
    low_ref[...] = lax.rem(depth, z)
    part = lax.div(depth, nz // (LANES // FACE_ROWS)) * FACE_ROWS
    face = jnp.where(y == 0, x, jnp.where(y == ny - 1, nx + x, -1))
    yface_ref[...] = jnp.where(face < 0, -1, part + face)
    face = jnp.where(x == 0, y, jnp.where(x == nx - 1, ny + y, -1))
    xface_ref[...] = jnp.where(face < 0, -1, part + face)
    z = nz * 2 * ny // WIDE
    xkey_ref[...] = jnp.where(face < 0, -1, lax.div(depth, z) * (2 * ny) + face)
    xlow_ref[...] = lax.rem(depth, z)
    copies[3].wait()
    member = member_ref[...]
    owner = lax.div(lax.div(member, held), count_y)
    slot_ref[...] = (owner - lax.axis_index("gx") + 1) * held + lax.rem(member, held)
    for copy in copies[4:] + copies[:2]:
        copy.wait()
    own_ref[...] = jnp.zeros_like(own_ref)
    own_ref[0:3, 0:held] = mv_ref[...]
    own_ref[3:4, 0:held] = mass_ref[...]


def sample_kernel(v_ref, old_ref, row_ref, depth_ref, inertia_ref, s_ref, acc_ref, table_ref, six_ref):
    comps, nx, ny, nz = v_ref.shape
    fields = [ref[k].reshape(nx * ny, nz) for ref in (v_ref, old_ref) for k in range(comps)]
    gather(fields, table_ref, row_ref, depth_ref, six_ref)
    for c in range(comps):
        s_ref[c] = six_ref[c]
        acc_ref[c] = inertia_ref[...] * (six_ref[c] - six_ref[comps + c])


def first_kernel(held, count_x, v_ref, s_ref, acc_ref, slot_ref, drag_ref, key_ref, low_ref, own_ref, even_ref,
                 odd_ref, force_ref, mtable_ref, spill_ref, ye_ref, yo_ref, total_ref, col_ref, field_ref):
    low, high = beside(even_ref[...], odd_ref[...], lax.axis_index("gx"), count_x)
    table = low + pltpu.roll(own_ref[...], held, axis=1) + pltpu.roll(high, 2 * held, axis=1)
    mtable_ref[...] = table
    forces([s_ref[c] for c in range(3)], [acc_ref[c] for c in range(3)], slot_ref[...], drag_ref[...], table,
           force_ref)
    edges(v_ref, force_ref, key_ref, low_ref, slot_ref, col_ref, field_ref, spill_ref, (ye_ref, yo_ref), total_ref)
    comps = v_ref.shape[0]
    for ref in (ye_ref, yo_ref):
        ref[comps, 8:16, :] = total_ref[...]


def pair_kernel(total_ref, came_ref, after_ref, out_ref):
    comps = came_ref.shape[0] - 1
    even = lax.axis_index("gy") % 2 == 0
    own, other = total_ref[...], came_ref[comps, 8:16, :]
    out_ref[0:8, :] = jnp.where(even, own, other)
    out_ref[8:16, :] = jnp.where(even, other, own)


def share_kernel(came_ref, after_ref, keep_ref, give_ref):
    even = lax.axis_index("gy") % 2 == 0
    first, second = came_ref[0:8, :], came_ref[8:16, :]
    keep_ref[...] = jnp.where(even, first, second)
    give_ref[...] = jnp.where(even, second, first)


def deposit(comps, force_ref, row_ref, depth_ref, col_ref, acc_ref, out_ref):
    rows, nz = out_ref.shape[1:]
    count = len(comps)
    for j in range(row_ref.shape[0] // 2):
        hot = hot_rows(wide_row(row_ref, j), rows)
        hit = hot_rows(wide_row(depth_ref, j), nz) > 0
        for k, c in enumerate(comps):
            for p, piece in enumerate(split(wide_row(force_ref.at[c], j))):
                wide = jnp.broadcast_to(piece, hit.shape)
                at = (p * count + k) * nz
                col_ref[at : at + nz, :] = jnp.where(hit, wide, jnp.zeros_like(wide))
        part = lax.dot_general(hot, col_ref[...], NT, preferred_element_type=f32)
        acc_ref[...] = part if j == 0 else acc_ref[...] + part
    for k in range(count):
        out_ref[k] = -(acc_ref[:, k * nz : (k + 1) * nz] + acc_ref[:, (count + k) * nz : (count + k + 1) * nz])


def deposit_kernel(comps, force_ref, row_ref, depth_ref, total_ref, out_ref, same_ref, col_ref, acc_ref):
    same_ref[...] = total_ref[...]
    deposit(comps, force_ref, row_ref, depth_ref, col_ref, acc_ref, out_ref)


def turn_kernel(count_y, spill_ref, odd_ref, even_ref, total_ref, after_ref, xe_ref, xo_ref):
    comps, ny, nz = spill_ref.shape[1:]
    low, high = beside(even_ref[comps], odd_ref[comps], lax.axis_index("gy"), count_y)
    even = lax.axis_index("gx") % 2 == 0
    ids = lax.broadcasted_iota(i32, (ny, nz), 0)
    for c in range(comps):
        sides = []
        for side in range(2):
            at = 3 * side + c
            face = spill_ref[side, c]
            face = face + jnp.where(ids == 0, low[at : at + 1], 0.0)
            face = face + jnp.where(ids == ny - 1, high[at : at + 1], 0.0)
            sides.append(face)
        xe_ref[c] = jnp.where(even, sides[1], sides[0])
        xo_ref[c] = jnp.where(even, sides[0], sides[1])
    for ref in (xe_ref, xo_ref):
        ref[comps, 0:8, :] = total_ref[...]
        ref[comps, 8:16, :] = jnp.zeros_like(total_ref)


def own_update(c, v_ref, load, l_ref, low, high):
    nx, ny, nz = v_ref.shape[1:]
    v = v_ref[c]
    w = smooth(smooth(smooth(load.reshape(nx, ny, nz), 2), 1), 0)
    beside_all = both(v, 0) + both(v, 1) + both(v, 2)
    l_ref[c] = v + viscous * (beside_all - 6.0 * v) + w
    add_y(c, low, high, l_ref)


def middle_kernel(count_y, v_ref, load_ref, odd_ref, even_ref, row_ref, depth_ref, after_ref, l_ref, s_ref,
                  table_ref):
    comps, nx, ny, nz = v_ref.shape
    low, high = beside(even_ref[...], odd_ref[...], lax.axis_index("gy"), count_y)
    for c in range(comps):
        own_update(c, v_ref, load_ref[c], l_ref, low, high)
    gather([l_ref[k].reshape(nx * ny, nz) for k in range(comps)], table_ref, row_ref, depth_ref, s_ref)


def sum_totals(held, count_x, total, low1, high1, kept, shared):
    own_x = lax.axis_index("gx")
    even = lax.axis_index("gy") % 2 == 0
    low2 = jnp.where(own_x > 1, jnp.where(even, kept, shared), 0.0)
    high2 = jnp.where(own_x < count_x - 2, jnp.where(even, shared, kept), 0.0)
    lane = lax.broadcasted_iota(i32, (8, LANES), 1)
    total = total + pltpu.roll(low1, LANES - held, axis=1) + pltpu.roll(high1, held, axis=1)
    total = total + jnp.where(lane < held, pltpu.roll(low2, LANES - 2 * held, axis=1), 0.0)
    return total + jnp.where(lane // held == 2, pltpu.roll(high2, 2 * held, axis=1), 0.0)


def second_kernel(held, count_x, l_ref, sp_ref, xo_ref, xe_ref, s_ref, inertia_ref, slot_ref, drag_ref, xkey_ref,
                  xlow_ref, yface_ref, low_ref, old_table_ref, old_total_ref, kept_ref, shared_ref,
                  v_ref, force_ref, mtable_ref, ye_ref, yo_ref, col_ref, acc_ref, face_ref, sample_ref):
    comps, nx, ny, nz = l_ref.shape
    low, high = beside(xe_ref[...], xo_ref[...], lax.axis_index("gx"), count_x)
    total = sum_totals(held, count_x, old_total_ref[...], low[comps, 0:8], high[comps, 0:8], kept_ref[...], shared_ref[...])
    old = old_table_ref[...]
    row = lax.broadcasted_iota(i32, (8, LANES), 0)
    lane = lax.broadcasted_iota(i32, (8, LANES), 1)
    table = jnp.where((row < 3) & (lane < 3 * held), old + old[3:4] * total, old)
    mtable_ref[...] = table
    z = nz * 2 * ny // WIDE
    for c in range(comps):
        turned = jnp.concatenate([low[c], high[c]], axis=0).T
        wide = jnp.concatenate([turned[h * z : (h + 1) * z] for h in range(nz // z)], axis=1)
        at = comps * z + c * z
        face_ref[c * z : (c + 1) * z, :], face_ref[at : at + z, :] = split(wide)
    for j in range(xkey_ref.shape[0] // 2):
        hot = hot_rows(wide_row(xkey_ref, j), WIDE)
        product = jnp.dot(face_ref[...], hot, preferred_element_type=f32)
        product = product[: comps * z] + product[comps * z :]
        for k, found in enumerate(pick(product, wide_row(xlow_ref, j), comps)):
            store_row(sample_ref, k, j, found)
    for c in range(comps):
        v_ref[c, 0] = l_ref[c, 0] + low[c]
        v_ref[c, 1 : nx - 1] = l_ref[c, 1 : nx - 1]
        v_ref[c, nx - 1] = l_ref[c, nx - 1] + high[c]
    samples = [sp_ref[c] + sample_ref[c] for c in range(comps)]
    acc = [inertia_ref[...] * (samples[c] - s_ref[c]) for c in range(comps)]
    forces(samples, acc, slot_ref[...], drag_ref[...], table, force_ref)
    fields, _ = faces_of(yface_ref, low_ref, None, force_ref, col_ref, acc_ref, nz)
    for c in range(comps):
        y_messages(v_ref, c, (fields[c][:nx], fields[c][nx:]), (ye_ref, yo_ref))


def finish_kernel(count_y, early, v_ref, load_ref, odd_ref, even_ref, force_ref, row_ref, depth_ref, after_ref,
                  out_hbm, face_ref, l_ref, rest_ref, col_ref, acc_ref, sem):
    comps, nx = v_ref.shape[:2]
    low, high = beside(even_ref[...], odd_ref[...], lax.axis_index("gy"), count_y)
    if early < comps:
        deposit(range(early, comps), force_ref, row_ref, depth_ref, col_ref, acc_ref, rest_ref)
    for c in range(comps):
        load = load_ref[c] if c < early else rest_ref[c - early]
        own_update(c, v_ref, load, l_ref, low, high)
        pltpu.make_async_copy(l_ref.at[c], out_hbm.at[c], sem.at[c]).start()
        face_ref[c, 0] = l_ref[c, 0]
        face_ref[c, 1] = l_ref[c, nx - 1]
    for c in range(comps):
        pltpu.make_async_copy(l_ref.at[c], out_hbm.at[c], sem.at[c]).wait()


def last_kernel(held, count_x, face_ref, xo_ref, xe_ref, mtable_ref, total_ref, old_hbm, m_hbm, v_hbm, new_ref, m_ref, sem):
    comps, nx = v_hbm.shape[:2]
    low, high = beside(xe_ref[...], xo_ref[...], lax.axis_index("gx"), count_x)
    copies = []
    for side, part in enumerate((low, high)):
        for c in range(comps):
            new_ref[side, c] = face_ref[c, side] + part[c]
        copies.append(pltpu.make_async_copy(new_ref.at[side], v_hbm.at[:, side * (nx - 1)], sem.at[side]))
        copies[-1].start()
    total = total_ref[...] + pltpu.roll(low[comps, 0:8], LANES - held, axis=1)
    total = total + pltpu.roll(high[comps, 0:8], held, axis=1)
    table = mtable_ref[...]
    table = table + table[3:4] * total
    m_ref[...] = pltpu.roll(table, LANES - held, axis=1)[0:3, :held]
    copies.append(pltpu.make_async_copy(m_ref, m_hbm, sem.at[2]))
    copies[-1].start()
    for copy in copies:
        copy.wait()


def near_pairs(axis, odd):
    count_x, count_y = lax.axis_size("gx"), lax.axis_size("gy")
    found = []
    for x in range(count_x):
        for y in range(count_y):
            at, count = (x, count_x) if axis == "gx" else (y, count_y)
            to = ((at + 1) ^ 1) - 1 if odd else at ^ 1
            if axis == "gy":
                target = (x, to % count)
            else:
                target = (to, y) if 0 <= to < count else (x, y ^ 1)
            found.append((x * count_y + y, target[0] * count_y + target[1]))
    return found


def cross_pairs():
    count_x, count_y = lax.axis_size("gx"), lax.axis_size("gy")
    found = []
    for x in range(count_x):
        for y in range(count_y):
            to = x - 2 if y % 2 == 0 else x + 2
            target = (to, y ^ 1) if 0 <= to < count_x else (x ^ 1, y)
            found.append((x * count_y + y, target[0] * count_y + target[1]))
    return found


def exchange(even_msg, odd_msg, axis):
    both_axes = ("gx", "gy")
    came_odd = lax.ppermute(odd_msg, both_axes, near_pairs(axis, True))
    came_even = lax.ppermute(even_msg, both_axes, near_pairs(axis, False))
    return came_even, came_odd


def per_device(velocity, velocity_old, station_cell, station_member, drag_coef, inertia_coef, member_velocity,
               member_inv_mass):
    count_x, count_y = lax.axis_size("gx"), lax.axis_size("gy")
    held = member_velocity.shape[1]
    grid = velocity.shape
    comps, nx, ny, nz = grid
    rows = nx * ny
    lines = (station_cell.shape[0] // LANES, LANES)
    ints = jax.ShapeDtypeStruct(lines, i32)
    one = real(*lines)
    three = real(3, *lines)
    tile = real(8, LANES)
    face = real(comps + 1, max(nx, ny), nz)
    spill = real(2, comps, ny, nz)
    product = 12 * nz * rows * lines[0] * LANES
    table = pltpu.VMEM((2, comps * nz, rows), bf16)

    (v, old, drag, inertia, slot, row, depth, key, low, xkey, xface, yface, xlow, own) = call(
        "load", functools.partial(load_kernel, held, count_y),
        (velocity, velocity_old, station_cell.reshape(lines), station_member.reshape(lines),
         drag_coef.reshape(lines), inertia_coef.reshape(lines), member_velocity, member_inv_mass.reshape(1, held)),
        [real(*grid)] * 2 + [one] * 2 + [ints] * 9 + [tile],
        [pltpu.VMEM(lines, i32), pltpu.VMEM(lines, i32), pltpu.VMEM((3, held), f32), pltpu.VMEM((1, held), f32),
         pltpu.SemaphoreType.DMA((8,))],
        in_hbm=range(8),
    )
    own_even, own_odd = exchange(own, own, "gx")
    s, acc = call(
        "samples", sample_kernel, (v, old, row, depth, inertia), [three, three],
        [pltpu.VMEM((2, 2 * comps * nz, rows), bf16), pltpu.VMEM((6,) + lines, f32)], flops=2 * product,
    )
    slots = -(-3 * held // 16) * 16
    work = [pltpu.VMEM((WIDE, WIDE), bf16), pltpu.VMEM((WIDE + slots, WIDE), f32)]
    edge_parts = [three, tile, spill, face, face, tile]
    force, mtable, spills, y_even, y_odd, total = call(
        "first_forces", functools.partial(first_kernel, held, count_x),
        (v, s, acc, slot, drag, key, low, own, own_even, own_odd), edge_parts, work, flops=product // 2,
    )

    def dep_scratch(count):
        return [pltpu.VMEM((2 * count * nz, WIDE), bf16), pltpu.VMEM((rows, 2 * count * nz), f32)]

    def spread(force, count, after):
        return call(
            "deposit", functools.partial(deposit_kernel, range(count)), (force, row, depth, after),
            [real(count, rows, nz), tile], dep_scratch(count), flops=product * count // comps,
        )

    def turn(spills, y_even, y_odd, total, after):
        return call(
            "turn", functools.partial(turn_kernel, count_y), (spills, y_odd, y_even, total, after), [face, face]
        )

    y_even, y_odd = exchange(y_even, y_odd, "gy")
    load, total = spread(force, comps, total)
    (sums,) = call("pair", pair_kernel, (total, y_even, load), [real(16, LANES)])
    sums = lax.ppermute(sums, ("gx", "gy"), cross_pairs())
    x_even, x_odd = turn(spills, y_even, y_odd, total, load)
    kept, given = call("share", share_kernel, (sums, x_even), [tile, tile])
    shared = lax.ppermute(given, ("gx", "gy"), near_pairs("gy", False))
    local, samples = call(
        "middle", functools.partial(middle_kernel, count_y), (v, load, y_odd, y_even, row, depth, kept),
        [real(*grid), three], [table], flops=product,
    )
    x_even, x_odd = exchange(x_even, x_odd, "gx")
    z = nz * 2 * ny // WIDE
    v, force, mtable, y_even, y_odd = call(
        "second_forces", functools.partial(second_kernel, held, count_x),
        (local, samples, x_odd, x_even, s, inertia, slot, drag, xkey, xlow, yface, low, mtable, total,
         kept, shared),
        [real(*grid), three, tile, face, face],
        [pltpu.VMEM((WIDE, WIDE), bf16), pltpu.VMEM((LANES, WIDE), f32),
         pltpu.VMEM((2 * comps * z, WIDE), bf16), pltpu.VMEM((3,) + lines, f32)],
        flops=product // 2,
    )
    y_even, y_odd = exchange(y_even, y_odd, "gy")
    spills, total = call(
        "spills", spill_kernel, (v, force, xface, low, slot), [spill, tile],
        [pltpu.VMEM((WIDE, WIDE), bf16), pltpu.VMEM((LANES + slots, WIDE), f32)], flops=product // 4,
    )
    load, total = spread(force, 2, total)
    x_even, x_odd = turn(spills, y_even, y_odd, total, load)
    late = max(comps - 2, 1)
    out, faces = call(
        "finish", functools.partial(finish_kernel, count_y, 2),
        (v, load, y_odd, y_even, force, row, depth, x_even),
        [real(*grid), real(comps, 2, ny, nz)],
        [pltpu.VMEM(grid, f32), pltpu.VMEM((late, rows, nz), f32)] + dep_scratch(late)
        + [pltpu.SemaphoreType.DMA((comps,))],
        out_hbm=(0,), flops=product // 3,
    )
    x_even, x_odd = exchange(x_even, x_odd, "gx")
    members, out = call(
        "last", functools.partial(last_kernel, held, count_x), (faces, x_odd, x_even, mtable, total, out),
        [real(3, held), real(*grid)],
        [pltpu.VMEM((2, comps, ny, nz), f32), pltpu.VMEM((3, held), f32), pltpu.SemaphoreType.DMA((3,))],
        in_hbm=(5,), out_hbm=(0, 1), aliases={5: 1},
    )
    return out, members


def solution(mesh):
    return jax.shard_map(
        per_device,
        mesh=mesh,
        in_specs=(
            P(None, "gx", "gy", None),
            P(None, "gx", "gy", None),
            P(("gx", "gy")),
            P(("gx", "gy"), None),
            P(("gx", "gy")),
            P(("gx", "gy")),
            P(None, ("gx", "gy")),
            P(("gx", "gy")),
        ),
        out_specs=(P(None, "gx", "gy", None), P(None, ("gx", "gy"))),
        check_vma=False,
    )
```

```python
import functools

import jax
import jax.numpy as jnp
from jax import lax
from jax.experimental import pallas as pl
from jax.experimental.pallas import tpu as pltpu
from jax.sharding import PartitionSpec as P

LANES = 128
WIDE = 256
FACE_ROWS = 32

viscous = 0.125
softening = 0.01

f32 = jnp.float32
i32 = jnp.int32
bf16 = jnp.bfloat16
HBM = pl.BlockSpec(memory_space=pltpu.HBM)
NT = (((1,), (1,)), ((), ()))


def call(name, body, ins, outs, scratch=(), in_hbm=(), out_hbm=(), flops=0, size=1 << 18, aliases=None):
    whole = pl.BlockSpec(memory_space=pltpu.VMEM)
    ins = [pltpu.with_memory_space_constraint(x, pltpu.HBM) if k in in_hbm else x for k, x in enumerate(ins)]
    outs = [pltpu.HBM(x.shape, x.dtype) if k in out_hbm else x for k, x in enumerate(outs)]
    return pl.pallas_call(
        body,
        name=name,
        out_shape=outs,
        in_specs=[HBM if k in in_hbm else whole for k in range(len(ins))],
        out_specs=[HBM if k in out_hbm else whole for k in range(len(outs))],
        scratch_shapes=list(scratch),
        input_output_aliases=aliases or {},
        compiler_params=pltpu.CompilerParams(vmem_limit_bytes=24 << 20),
        cost_estimate=pl.CostEstimate(flops=flops, bytes_accessed=size, transcendentals=0),
    )(*ins)


def real(*shape):
    return jax.ShapeDtypeStruct(shape, f32)


def split(x):
    top = x.astype(bf16)
    return top, (x - top.astype(f32)).astype(bf16)


def hot_rows(index, count):
    ids = lax.broadcasted_iota(i32, (count, index.shape[1]), 0).astype(f32).astype(bf16)
    wide = jnp.broadcast_to(index.astype(f32).astype(bf16), ids.shape)
    return jnp.where(ids == wide, jnp.ones_like(wide), jnp.zeros_like(wide))


def wide_row(ref, j):
    return jnp.concatenate([ref[2 * j : 2 * j + 1, :], ref[2 * j + 1 : 2 * j + 2, :]], axis=1)


def store_row(ref, k, j, row):
    ref[k, 2 * j : 2 * j + 1, :] = row[:, :LANES]
    ref[k, 2 * j + 1 : 2 * j + 2, :] = row[:, LANES:]


def pick(product, depth_row, count):
    z = product.shape[0] // count
    hit = lax.broadcasted_iota(i32, (z, depth_row.shape[1]), 0) == depth_row
    return [
        jnp.sum(jnp.where(hit, product[k * z : (k + 1) * z], 0.0), axis=0, keepdims=True) for k in range(count)
    ]


def gather(fields, table_ref, row_ref, depth_ref, out_ref):
    rows, z = fields[0].shape
    count = len(fields)
    for k, field in enumerate(fields):
        table_ref[k, :z, :], table_ref[k, z:, :] = split(field.T)
    for j in range(row_ref.shape[0] // 2):
        hot = hot_rows(wide_row(row_ref, j), rows)
        hit = lax.broadcasted_iota(i32, (z, WIDE), 0) == wide_row(depth_ref, j)
        for k in range(count):
            product = jnp.dot(table_ref[k], hot, preferred_element_type=f32)
            product = product[:z] + product[z:]
            store_row(out_ref, k, j, jnp.sum(jnp.where(hit, product, 0.0), axis=0, keepdims=True))


def columns(ref, force_ref, depth_row, z, j, groups):
    hit = hot_rows(depth_row, z) > 0
    for c in range(3):
        for p, piece in enumerate(split(wide_row(force_ref.at[c], j))):
            wide = jnp.broadcast_to(piece, hit.shape)
            at = (p * groups + c) * z
            ref[at : at + z, :] = jnp.where(hit, wide, jnp.zeros_like(wide))


def moved(x, axis, by):
    n = x.shape[axis]
    if axis >= x.ndim - 2:
        ids = lax.broadcasted_iota(i32, x.shape, axis)
        return jnp.where(ids == (0 if by > 0 else n - 1), 0.0, pltpu.roll(x, by % n, axis=axis))
    zero = jnp.zeros_like(lax.slice_in_dim(x, 0, 1, axis=axis))
    if by > 0:
        return jnp.concatenate([zero, lax.slice_in_dim(x, 0, n - 1, axis=axis)], axis=axis)
    return jnp.concatenate([lax.slice_in_dim(x, 1, n, axis=axis), zero], axis=axis)


def both(x, axis):
    return moved(x, axis, 1) + moved(x, axis, -1)


def smooth(x, axis):
    return 0.5 * x + 0.25 * both(x, axis)


def beside(even_msg, odd_msg, own, count):
    even = own % 2 == 0
    low = jnp.where(own > 0, jnp.where(even, odd_msg, even_msg), 0.0)
    high = jnp.where(own < count - 1, jnp.where(even, even_msg, odd_msg), 0.0)
    return low, high


def add_y(c, face_low, face_high, ref):
    ny = ref.shape[2]
    ref[c, :, 0, :] += face_low[c]
    ref[c, :, ny - 1, :] += face_high[c]


def edges(v_ref, force_ref, key_ref, low_ref, slot_ref, col_ref, acc_ref, spill_ref, y_refs, total_ref):
    comps, nx, ny, nz = v_ref.shape
    ring = 2 * (nx + ny)
    parts = WIDE // ring
    z = nz // parts
    slots = acc_ref.shape[0] - WIDE
    free = 3 * z
    for p in range(2):
        col_ref[p * LANES + free : (p + 1) * LANES, :] = jnp.zeros((LANES - free, WIDE), bf16)
    for j in range(key_ref.shape[0] // 2):
        hot = jnp.concatenate([hot_rows(wide_row(key_ref, j), WIDE), hot_rows(wide_row(slot_ref, j), slots)], axis=0)
        columns(col_ref, force_ref, wide_row(low_ref, j), z, j, LANES // z)
        pieces = [split(wide_row(force_ref.at[c], j)) for c in range(3)]
        for p in range(2):
            rows = [piece[p].astype(f32) for piece in pieces] + [jnp.zeros((13, WIDE), f32)]
            col_ref[p * LANES + free : p * LANES + free + 16, :] = jnp.concatenate(rows, axis=0).astype(bf16)
        part = lax.dot_general(hot, col_ref[...], NT, preferred_element_type=f32)
        acc_ref[...] = part if j == 0 else acc_ref[...] + part
    found = acc_ref[:, :LANES] + acc_ref[:, LANES:]
    sums = jnp.concatenate([found[WIDE:], jnp.zeros((LANES - slots, LANES), f32)], axis=0)
    total_ref[...] = sums.T[free : free + 8]
    found = -found[:WIDE]
    lane = lax.broadcasted_iota(i32, (ring, LANES), 1) // z
    yid = lax.broadcasted_iota(i32, (ny, nz), 0)
    for c in range(comps):
        w = jnp.zeros((ring, nz), f32)
        for h in range(parts):
            block = found[h * ring : (h + 1) * ring]
            by = (h - c) * z % LANES
            block = pltpu.roll(block, by, axis=1) if by else block
            w = jnp.where(lane == h, block, w)
        w = smooth(w, 1)
        y_ends = (w[:nx], w[nx : 2 * nx])
        for side, x in ((0, 0), (1, nx - 1)):
            face = w[2 * nx + side * ny : 2 * nx + (side + 1) * ny]
            face = jnp.where(yid == 0, y_ends[0][x : x + 1], face)
            face = jnp.where(yid == ny - 1, y_ends[1][x : x + 1], face)
            spill_ref[side, c] = 0.25 * smooth(face, 0) + viscous * v_ref[c, x]
        y_messages(v_ref, c, y_ends, y_refs)


def faces_of(key_ref, low_ref, slot_ref, force_ref, col_ref, acc_ref, nz):
    parts = LANES // FACE_ROWS
    z = nz // parts
    free = 3 * z
    slots = acc_ref.shape[0] - LANES
    for p in range(2):
        col_ref[p * LANES + free : (p + 1) * LANES, :] = jnp.zeros((LANES - free, WIDE), bf16)
    for j in range(key_ref.shape[0] // 2):
        hot = hot_rows(wide_row(key_ref, j), LANES)
        columns(col_ref, force_ref, wide_row(low_ref, j), z, j, LANES // z)
        if slot_ref is not None:
            hot = jnp.concatenate([hot, hot_rows(wide_row(slot_ref, j), slots)], axis=0)
            pieces = [split(wide_row(force_ref.at[c], j)) for c in range(3)]
            for p in range(2):
                rows = [piece[p].astype(f32) for piece in pieces] + [jnp.zeros((13, WIDE), f32)]
                col_ref[p * LANES + free : p * LANES + free + 16, :] = jnp.concatenate(rows, axis=0).astype(bf16)
        part = lax.dot_general(hot, col_ref[...], NT, preferred_element_type=f32)
        acc_ref[...] = part if j == 0 else acc_ref[...] + part
    found = acc_ref[:, :LANES] + acc_ref[:, LANES:]
    total = None
    if slot_ref is not None:
        sums = jnp.concatenate([found[LANES:], jnp.zeros((LANES - slots, LANES), f32)], axis=0)
        total = sums.T[free : free + 8]
    lane = lax.broadcasted_iota(i32, (FACE_ROWS, LANES), 1) // z
    fields = []
    for c in range(3):
        w = jnp.zeros((FACE_ROWS, nz), f32)
        for h in range(parts):
            block = -found[h * FACE_ROWS : (h + 1) * FACE_ROWS]
            by = (h - c) * z % LANES
            block = pltpu.roll(block, by, axis=1) if by else block
            w = jnp.where(lane == h, block, w)
        fields.append(smooth(w, 1))
    return fields, total


def y_messages(v_ref, c, y_ends, y_refs):
    comps, nx, ny, nz = v_ref.shape
    even = lax.axis_index("gy") % 2 == 0
    low, high = [
        (smooth(0.25 * w_y, 0) + viscous * v_ref[c, :, y, :], 0.0625 * w_y[0:1], 0.0625 * w_y[nx - 1 : nx])
        for y, w_y in zip((0, ny - 1), y_ends)
    ]
    for ref, flip in zip(y_refs, (even, jnp.logical_not(even))):
        ref[c] = jnp.where(flip, high[0], low[0])
        for side in range(2):
            at = 3 * side + c
            ref[comps, at : at + 1, :] = jnp.where(flip, high[1 + side], low[1 + side])


def spill_kernel(v_ref, force_ref, key_ref, low_ref, slot_ref, spill_ref, total_ref, col_ref, acc_ref):
    comps, nx, ny, nz = v_ref.shape
    fields, total = faces_of(key_ref, low_ref, slot_ref, force_ref, col_ref, acc_ref, nz)
    total_ref[...] = total
    for c in range(comps):
        for side, x in ((0, 0), (1, nx - 1)):
            face = fields[c][side * ny : (side + 1) * ny]
            spill_ref[side, c] = 0.25 * smooth(face, 0) + viscous * v_ref[c, x]


def forces(samples, acc, slot, drag, table, force_ref):
    relative = [
        samples[c] - jnp.take_along_axis(jnp.broadcast_to(table[c : c + 1], slot.shape), slot, axis=1)
        for c in range(3)
    ]
    square = relative[0] * relative[0] + relative[1] * relative[1] + relative[2] * relative[2]
    speed = drag * jnp.sqrt(square + softening)
    for c in range(3):
        force_ref[c] = speed * relative[c] + acc[c]


def load_kernel(held, count_y, v_any, old_any, cell_any, member_any, drag_any, inertia_any, mv_any, mass_any,
                v_ref, old_ref, drag_ref, inertia_ref, slot_ref, row_ref, depth_ref, key_ref, low_ref, xkey_ref,
                xface_ref, yface_ref, xlow_ref, own_ref, cell_ref, member_ref, mv_ref, mass_ref, sem):
    loads = [(v_any, v_ref), (old_any, old_ref), (cell_any, cell_ref), (member_any, member_ref), (mv_any, mv_ref),
             (mass_any, mass_ref), (drag_any, drag_ref), (inertia_any, inertia_ref)]
    copies = [pltpu.make_async_copy(a, b, sem.at[k]) for k, (a, b) in enumerate(loads)]
    for copy in copies:
        copy.start()
    comps, nx, ny, nz = v_ref.shape
    copies[2].wait()
    cell = cell_ref[...]
    row, depth = lax.div(cell, nz), lax.rem(cell, nz)
    row_ref[...] = row
    depth_ref[...] = depth
    x, y = lax.div(row, ny), lax.rem(row, ny)
    ring = 2 * (nx + ny)
    edge = jnp.where(x == 0, 2 * nx + y, jnp.where(x == nx - 1, 2 * nx + ny + y, -1))
    edge = jnp.where(y == 0, x, jnp.where(y == ny - 1, nx + x, edge))
    z = nz * ring // WIDE
    key_ref[...] = jnp.where(edge < 0, -1, lax.div(depth, z) * ring + edge)
    low_ref[...] = lax.rem(depth, z)
    part = lax.div(depth, nz // (LANES // FACE_ROWS)) * FACE_ROWS
    face = jnp.where(y == 0, x, jnp.where(y == ny - 1, nx + x, -1))
    yface_ref[...] = jnp.where(face < 0, -1, part + face)
    face = jnp.where(x == 0, y, jnp.where(x == nx - 1, ny + y, -1))
    xface_ref[...] = jnp.where(face < 0, -1, part + face)
    z = nz * 2 * ny // WIDE
    xkey_ref[...] = jnp.where(face < 0, -1, lax.div(depth, z) * (2 * ny) + face)
    xlow_ref[...] = lax.rem(depth, z)
    copies[3].wait()
    member = member_ref[...]
    owner = lax.div(lax.div(member, held), count_y)
    slot_ref[...] = (owner - lax.axis_index("gx") + 1) * held + lax.rem(member, held)
    for copy in copies[4:] + copies[:2]:
        copy.wait()
    own_ref[...] = jnp.zeros_like(own_ref)
    own_ref[0:3, 0:held] = mv_ref[...]
    own_ref[3:4, 0:held] = mass_ref[...]


def sample_kernel(v_ref, old_ref, row_ref, depth_ref, inertia_ref, s_ref, acc_ref, table_ref, six_ref):
    comps, nx, ny, nz = v_ref.shape
    fields = [ref[k].reshape(nx * ny, nz) for ref in (v_ref, old_ref) for k in range(comps)]
    gather(fields, table_ref, row_ref, depth_ref, six_ref)
    for c in range(comps):
        s_ref[c] = six_ref[c]
        acc_ref[c] = inertia_ref[...] * (six_ref[c] - six_ref[comps + c])


def first_kernel(held, count_x, v_ref, s_ref, acc_ref, slot_ref, drag_ref, key_ref, low_ref, own_ref, even_ref,
                 odd_ref, force_ref, mtable_ref, spill_ref, ye_ref, yo_ref, total_ref, col_ref, field_ref):
    low, high = beside(even_ref[...], odd_ref[...], lax.axis_index("gx"), count_x)
    table = low + pltpu.roll(own_ref[...], held, axis=1) + pltpu.roll(high, 2 * held, axis=1)
    mtable_ref[...] = table
    forces([s_ref[c] for c in range(3)], [acc_ref[c] for c in range(3)], slot_ref[...], drag_ref[...], table,
           force_ref)
    edges(v_ref, force_ref, key_ref, low_ref, slot_ref, col_ref, field_ref, spill_ref, (ye_ref, yo_ref), total_ref)
    comps = v_ref.shape[0]
    for ref in (ye_ref, yo_ref):
        ref[comps, 8:16, :] = total_ref[...]


def pair_kernel(total_ref, came_ref, after_ref, out_ref):
    comps = came_ref.shape[0] - 1
    even = lax.axis_index("gy") % 2 == 0
    own, other = total_ref[...], came_ref[comps, 8:16, :]
    out_ref[0:8, :] = jnp.where(even, own, other)
    out_ref[8:16, :] = jnp.where(even, other, own)


def share_kernel(came_ref, after_ref, keep_ref, give_ref):
    even = lax.axis_index("gy") % 2 == 0
    first, second = came_ref[0:8, :], came_ref[8:16, :]
    keep_ref[...] = jnp.where(even, first, second)
    give_ref[...] = jnp.where(even, second, first)


def deposit(comps, force_ref, row_ref, depth_ref, col_ref, acc_ref, out_ref):
    rows, nz = out_ref.shape[1:]
    count = len(comps)
    for j in range(row_ref.shape[0] // 2):
        hot = hot_rows(wide_row(row_ref, j), rows)
        hit = hot_rows(wide_row(depth_ref, j), nz) > 0
        for k, c in enumerate(comps):
            for p, piece in enumerate(split(wide_row(force_ref.at[c], j))):
                wide = jnp.broadcast_to(piece, hit.shape)
                at = (p * count + k) * nz
                col_ref[at : at + nz, :] = jnp.where(hit, wide, jnp.zeros_like(wide))
        part = lax.dot_general(hot, col_ref[...], NT, preferred_element_type=f32)
        acc_ref[...] = part if j == 0 else acc_ref[...] + part
    for k in range(count):
        out_ref[k] = -(acc_ref[:, k * nz : (k + 1) * nz] + acc_ref[:, (count + k) * nz : (count + k + 1) * nz])


def deposit_kernel(comps, force_ref, row_ref, depth_ref, total_ref, out_ref, same_ref, col_ref, acc_ref):
    same_ref[...] = total_ref[...]
    deposit(comps, force_ref, row_ref, depth_ref, col_ref, acc_ref, out_ref)


def turn_kernel(count_y, spill_ref, odd_ref, even_ref, total_ref, after_ref, xe_ref, xo_ref):
    comps, ny, nz = spill_ref.shape[1:]
    low, high = beside(even_ref[comps], odd_ref[comps], lax.axis_index("gy"), count_y)
    even = lax.axis_index("gx") % 2 == 0
    ids = lax.broadcasted_iota(i32, (ny, nz), 0)
    for c in range(comps):
        sides = []
        for side in range(2):
            at = 3 * side + c
            face = spill_ref[side, c]
            face = face + jnp.where(ids == 0, low[at : at + 1], 0.0)
            face = face + jnp.where(ids == ny - 1, high[at : at + 1], 0.0)
            sides.append(face)
        xe_ref[c] = jnp.where(even, sides[1], sides[0])
        xo_ref[c] = jnp.where(even, sides[0], sides[1])
    for ref in (xe_ref, xo_ref):
        ref[comps, 0:8, :] = total_ref[...]
        ref[comps, 8:16, :] = jnp.zeros_like(total_ref)


def own_update(c, v_ref, load, l_ref, low, high):
    nx, ny, nz = v_ref.shape[1:]
    v = v_ref[c]
    w = smooth(smooth(smooth(load.reshape(nx, ny, nz), 2), 1), 0)
    beside_all = both(v, 0) + both(v, 1) + both(v, 2)
    l_ref[c] = v + viscous * (beside_all - 6.0 * v) + w
    add_y(c, low, high, l_ref)


def middle_kernel(count_y, v_ref, load_ref, odd_ref, even_ref, row_ref, depth_ref, after_ref, l_ref, s_ref,
                  table_ref):
    comps, nx, ny, nz = v_ref.shape
    low, high = beside(even_ref[...], odd_ref[...], lax.axis_index("gy"), count_y)
    for c in range(comps):
        own_update(c, v_ref, load_ref[c], l_ref, low, high)
    gather([l_ref[k].reshape(nx * ny, nz) for k in range(comps)], table_ref, row_ref, depth_ref, s_ref)


def sum_totals(held, count_x, total, low1, high1, kept, shared):
    own_x = lax.axis_index("gx")
    even = lax.axis_index("gy") % 2 == 0
    low2 = jnp.where(own_x > 1, jnp.where(even, kept, shared), 0.0)
    high2 = jnp.where(own_x < count_x - 2, jnp.where(even, shared, kept), 0.0)
    lane = lax.broadcasted_iota(i32, (8, LANES), 1)
    total = total + pltpu.roll(low1, LANES - held, axis=1) + pltpu.roll(high1, held, axis=1)
    total = total + jnp.where(lane < held, pltpu.roll(low2, LANES - 2 * held, axis=1), 0.0)
    return total + jnp.where(lane // held == 2, pltpu.roll(high2, 2 * held, axis=1), 0.0)


def second_kernel(held, count_x, l_ref, sp_ref, xo_ref, xe_ref, s_ref, inertia_ref, slot_ref, drag_ref, xkey_ref,
                  xlow_ref, yface_ref, low_ref, old_table_ref, old_total_ref, kept_ref, shared_ref,
                  v_ref, force_ref, mtable_ref, ye_ref, yo_ref, col_ref, acc_ref, face_ref, sample_ref):
    comps, nx, ny, nz = l_ref.shape
    low, high = beside(xe_ref[...], xo_ref[...], lax.axis_index("gx"), count_x)
    total = sum_totals(held, count_x, old_total_ref[...], low[comps, 0:8], high[comps, 0:8], kept_ref[...], shared_ref[...])
    old = old_table_ref[...]
    row = lax.broadcasted_iota(i32, (8, LANES), 0)
    lane = lax.broadcasted_iota(i32, (8, LANES), 1)
    table = jnp.where((row < 3) & (lane < 3 * held), old + old[3:4] * total, old)
    mtable_ref[...] = table
    z = nz * 2 * ny // WIDE
    for c in range(comps):
        turned = jnp.concatenate([low[c], high[c]], axis=0).T
        wide = jnp.concatenate([turned[h * z : (h + 1) * z] for h in range(nz // z)], axis=1)
        at = comps * z + c * z
        face_ref[c * z : (c + 1) * z, :], face_ref[at : at + z, :] = split(wide)
    for j in range(xkey_ref.shape[0] // 2):
        hot = hot_rows(wide_row(xkey_ref, j), WIDE)
        product = jnp.dot(face_ref[...], hot, preferred_element_type=f32)
        product = product[: comps * z] + product[comps * z :]
        for k, found in enumerate(pick(product, wide_row(xlow_ref, j), comps)):
            store_row(sample_ref, k, j, found)
    for c in range(comps):
        v_ref[c, 0] = l_ref[c, 0] + low[c]
        v_ref[c, 1 : nx - 1] = l_ref[c, 1 : nx - 1]
        v_ref[c, nx - 1] = l_ref[c, nx - 1] + high[c]
    samples = [sp_ref[c] + sample_ref[c] for c in range(comps)]
    acc = [inertia_ref[...] * (samples[c] - s_ref[c]) for c in range(comps)]
    forces(samples, acc, slot_ref[...], drag_ref[...], table, force_ref)
    fields, _ = faces_of(yface_ref, low_ref, None, force_ref, col_ref, acc_ref, nz)
    for c in range(comps):
        y_messages(v_ref, c, (fields[c][:nx], fields[c][nx:]), (ye_ref, yo_ref))


def finish_kernel(count_y, early, v_ref, load_ref, odd_ref, even_ref, force_ref, row_ref, depth_ref, after_ref,
                  out_hbm, face_ref, l_ref, rest_ref, col_ref, acc_ref, sem):
    comps, nx = v_ref.shape[:2]
    low, high = beside(even_ref[...], odd_ref[...], lax.axis_index("gy"), count_y)
    if early < comps:
        deposit(range(early, comps), force_ref, row_ref, depth_ref, col_ref, acc_ref, rest_ref)
    for c in range(comps):
        load = load_ref[c] if c < early else rest_ref[c - early]
        own_update(c, v_ref, load, l_ref, low, high)
        pltpu.make_async_copy(l_ref.at[c], out_hbm.at[c], sem.at[c]).start()
        face_ref[c, 0] = l_ref[c, 0]
        face_ref[c, 1] = l_ref[c, nx - 1]
    for c in range(comps):
        pltpu.make_async_copy(l_ref.at[c], out_hbm.at[c], sem.at[c]).wait()


def last_kernel(held, count_x, face_ref, xo_ref, xe_ref, mtable_ref, total_ref, old_hbm, m_hbm, v_hbm, new_ref, m_ref, sem):
    comps, nx = v_hbm.shape[:2]
    low, high = beside(xe_ref[...], xo_ref[...], lax.axis_index("gx"), count_x)
    copies = []
    for side, part in enumerate((low, high)):
        for c in range(comps):
            new_ref[side, c] = face_ref[c, side] + part[c]
        copies.append(pltpu.make_async_copy(new_ref.at[side], v_hbm.at[:, side * (nx - 1)], sem.at[side]))
        copies[-1].start()
    total = total_ref[...] + pltpu.roll(low[comps, 0:8], LANES - held, axis=1)
    total = total + pltpu.roll(high[comps, 0:8], held, axis=1)
    table = mtable_ref[...]
    table = table + table[3:4] * total
    m_ref[...] = pltpu.roll(table, LANES - held, axis=1)[0:3, :held]
    copies.append(pltpu.make_async_copy(m_ref, m_hbm, sem.at[2]))
    copies[-1].start()
    for copy in copies:
        copy.wait()


def near_pairs(axis, odd):
    count_x, count_y = lax.axis_size("gx"), lax.axis_size("gy")
    found = []
    for x in range(count_x):
        for y in range(count_y):
            at, count = (x, count_x) if axis == "gx" else (y, count_y)
            to = ((at + 1) ^ 1) - 1 if odd else at ^ 1
            if axis == "gy":
                target = (x, to % count)
            else:
                target = (to, y) if 0 <= to < count else (x, y ^ 1)
            found.append((x * count_y + y, target[0] * count_y + target[1]))
    return found


def cross_pairs():
    count_x, count_y = lax.axis_size("gx"), lax.axis_size("gy")
    found = []
    for x in range(count_x):
        for y in range(count_y):
            to = x - 2 if y % 2 == 0 else x + 2
            target = (to, y ^ 1) if 0 <= to < count_x else (x ^ 1, y)
            found.append((x * count_y + y, target[0] * count_y + target[1]))
    return found


def exchange(even_msg, odd_msg, axis):
    both_axes = ("gx", "gy")
    came_odd = lax.ppermute(odd_msg, both_axes, near_pairs(axis, True))
    came_even = lax.ppermute(even_msg, both_axes, near_pairs(axis, False))
    return came_even, came_odd


def per_device(velocity, velocity_old, station_cell, station_member, drag_coef, inertia_coef, member_velocity,
               member_inv_mass):
    count_x, count_y = lax.axis_size("gx"), lax.axis_size("gy")
    held = member_velocity.shape[1]
    grid = velocity.shape
    comps, nx, ny, nz = grid
    rows = nx * ny
    lines = (station_cell.shape[0] // LANES, LANES)
    ints = jax.ShapeDtypeStruct(lines, i32)
    one = real(*lines)
    three = real(3, *lines)
    tile = real(8, LANES)
    face = real(comps + 1, max(nx, ny), nz)
    spill = real(2, comps, ny, nz)
    product = 12 * nz * rows * lines[0] * LANES
    table = pltpu.VMEM((comps, 2 * nz, rows), bf16)

    (v, old, drag, inertia, slot, row, depth, key, low, xkey, xface, yface, xlow, own) = call(
        "load", functools.partial(load_kernel, held, count_y),
        (velocity, velocity_old, station_cell.reshape(lines), station_member.reshape(lines),
         drag_coef.reshape(lines), inertia_coef.reshape(lines), member_velocity, member_inv_mass.reshape(1, held)),
        [real(*grid)] * 2 + [one] * 2 + [ints] * 9 + [tile],
        [pltpu.VMEM(lines, i32), pltpu.VMEM(lines, i32), pltpu.VMEM((3, held), f32), pltpu.VMEM((1, held), f32),
         pltpu.SemaphoreType.DMA((8,))],
        in_hbm=range(8),
    )
    own_even, own_odd = exchange(own, own, "gx")
    s, acc = call(
        "samples", sample_kernel, (v, old, row, depth, inertia), [three, three],
        [pltpu.VMEM((2 * comps, 2 * nz, rows), bf16), pltpu.VMEM((6,) + lines, f32)], flops=2 * product,
    )
    slots = -(-3 * held // 16) * 16
    work = [pltpu.VMEM((WIDE, WIDE), bf16), pltpu.VMEM((WIDE + slots, WIDE), f32)]
    edge_parts = [three, tile, spill, face, face, tile]
    force, mtable, spills, y_even, y_odd, total = call(
        "first_forces", functools.partial(first_kernel, held, count_x),
        (v, s, acc, slot, drag, key, low, own, own_even, own_odd), edge_parts, work, flops=product // 2,
    )

    def dep_scratch(count):
        return [pltpu.VMEM((2 * count * nz, WIDE), bf16), pltpu.VMEM((rows, 2 * count * nz), f32)]

    def spread(force, count, after):
        return call(
            "deposit", functools.partial(deposit_kernel, range(count)), (force, row, depth, after),
            [real(count, rows, nz), tile], dep_scratch(count), flops=product * count // comps,
        )

    def turn(spills, y_even, y_odd, total, after):
        return call(
            "turn", functools.partial(turn_kernel, count_y), (spills, y_odd, y_even, total, after), [face, face]
        )

    y_even, y_odd = exchange(y_even, y_odd, "gy")
    load, total = spread(force, comps, total)
    (sums,) = call("pair", pair_kernel, (total, y_even, load), [real(16, LANES)])
    sums = lax.ppermute(sums, ("gx", "gy"), cross_pairs())
    x_even, x_odd = turn(spills, y_even, y_odd, total, load)
    kept, given = call("share", share_kernel, (sums, x_even), [tile, tile])
    shared = lax.ppermute(given, ("gx", "gy"), near_pairs("gy", False))
    local, samples = call(
        "middle", functools.partial(middle_kernel, count_y), (v, load, y_odd, y_even, row, depth, kept),
        [real(*grid), three], [table], flops=product,
    )
    x_even, x_odd = exchange(x_even, x_odd, "gx")
    z = nz * 2 * ny // WIDE
    v, force, mtable, y_even, y_odd = call(
        "second_forces", functools.partial(second_kernel, held, count_x),
        (local, samples, x_odd, x_even, s, inertia, slot, drag, xkey, xlow, yface, low, mtable, total,
         kept, shared),
        [real(*grid), three, tile, face, face],
        [pltpu.VMEM((WIDE, WIDE), bf16), pltpu.VMEM((LANES, WIDE), f32),
         pltpu.VMEM((2 * comps * z, WIDE), bf16), pltpu.VMEM((3,) + lines, f32)],
        flops=product // 2,
    )
    y_even, y_odd = exchange(y_even, y_odd, "gy")
    spills, total = call(
        "spills", spill_kernel, (v, force, xface, low, slot), [spill, tile],
        [pltpu.VMEM((WIDE, WIDE), bf16), pltpu.VMEM((LANES + slots, WIDE), f32)], flops=product // 4,
    )
    load, total = spread(force, 2, total)
    x_even, x_odd = turn(spills, y_even, y_odd, total, load)
    late = max(comps - 2, 1)
    out, faces = call(
        "finish", functools.partial(finish_kernel, count_y, 2),
        (v, load, y_odd, y_even, force, row, depth, x_even),
        [real(*grid), real(comps, 2, ny, nz)],
        [pltpu.VMEM(grid, f32), pltpu.VMEM((late, rows, nz), f32)] + dep_scratch(late)
        + [pltpu.SemaphoreType.DMA((comps,))],
        out_hbm=(0,), flops=product // 3,
    )
    x_even, x_odd = exchange(x_even, x_odd, "gx")
    members, out = call(
        "last", functools.partial(last_kernel, held, count_x), (faces, x_odd, x_even, mtable, total, out),
        [real(3, held), real(*grid)],
        [pltpu.VMEM((2, comps, ny, nz), f32), pltpu.VMEM((3, held), f32), pltpu.SemaphoreType.DMA((3,))],
        in_hbm=(5,), out_hbm=(0, 1), aliases={5: 1},
    )
    return out, members


def solution(mesh):
    return jax.shard_map(
        per_device,
        mesh=mesh,
        in_specs=(
            P(None, "gx", "gy", None),
            P(None, "gx", "gy", None),
            P(("gx", "gy")),
            P(("gx", "gy"), None),
            P(("gx", "gy")),
            P(("gx", "gy")),
            P(None, ("gx", "gy")),
            P(("gx", "gy")),
        ),
        out_specs=(P(None, "gx", "gy", None), P(None, ("gx", "gy"))),
        check_vma=False,
    )
```
